32 devices in a mesh: dp: 4 (over y, x), expert: 4 (over z), tensor: 2 (over core).
Axes of the slice: x: 2, y: 2, z: 4, core: 2. Of those that a mesh axis runs over, the one named last changes fastest.
Arguments:
- weight: bfloat16 [4, 1536, 4096], P('expert', 'tensor'), may hold values from -1.796875 to 1.796875
- factor_a: float32 [4, 64, 4096], P('expert', 'dp', 'tensor'), may hold values from -1.2 to 1.2
- factor_b: float32 [4, 64, 1536], P('expert', 'dp', 'tensor'), may hold values from -1.2 to 1.2
- moment_a: float32 [4, 64, 4096], P('expert', 'dp', 'tensor'), may hold values from -0.6 to 0.6
- second_a: float32 [4, 64, 4096], P('expert', 'dp', 'tensor'), may hold values from 0.003 to 1
- first_moment_factor_b: float32 [4, 64, 1536], P('expert', 'dp', 'tensor'), may hold values from -0.6 to 0.6
- second_b: float32 [4, 64, 1536], P('expert', 'dp', 'tensor'), may hold values from 0.003 to 1
- grad_a: float32 [4, 4, 64, 4096], P('dp', 'expert', None, 'tensor'), may hold values from -2 to 2
- grad_b: float32 [4, 4, 64, 1536], P('dp', 'expert', None, 'tensor'), may hold values from -2 to 2
- slot_of: int32 [4], replicated, may hold values from 0 to 3, each once
Outputs:
- merged: bfloat16 [4, 1536, 4096], P('expert', 'tensor')
- new_a: float32 [4, 64, 4096], P('expert', 'dp', 'tensor')
- new_b: float32 [4, 64, 1536], P('expert', 'dp', 'tensor')
- new_moment_a: float32 [4, 64, 4096], P('expert', 'dp', 'tensor')
- new_second_a: float32 [4, 64, 4096], P('expert', 'dp', 'tensor')
- new_moment_b: float32 [4, 64, 1536], P('expert', 'dp', 'tensor')
- new_second_b: float32 [4, 64, 1536], P('expert', 'dp', 'tensor')
The draws below stay inside these ranges and needn't reach their ends.
Inputs may be any that keep to these rules, and one draw needn't show every extreme that they name: slot_of is a permutation; slot s belongs to the index s // 1 of expert.
All inputs are finite; a program needn't handle non-finite values.
Results may differ from the reference program's by a relative error of at most 0.0065.
Values may be sent and summed in bfloat16 or wider, within the bound.
No kernel may reach another device: no remote copies, remote signals or barrier semaphores. Data moves between devices by JAX's collectives and lax.ppermute only.
A program may use at most 64 MiB of HBM per device.

```python
import math
import jax
import jax.numpy as jnp
from jax import lax

D = 4096
FF = 1536
R = 64
ADAM_STEP = 20
EXPERTS = 4
N_DP = 4


def shard_levels(rng, dims, shards, least, top_value):
    loudness, own = 1.0, jax.random.fold_in(rng, 6)
    for axis_at, shards_of in shards:
        heights = jnp.exp(jax.random.uniform(jax.random.fold_in(own, axis_at), (shards_of,), jnp.float32, least / len(shards), top_value / len(shards)))
        loudness = loudness * jnp.repeat(heights, dims[axis_at] // shards_of).reshape([-1 if axis == axis_at else 1 for axis in range(len(dims))])
    return loudness


def scatter_about(key, shape, scale, bound, shards=(), kind=jnp.bfloat16):
    result = jax.random.normal(key, shape, jnp.float32) * scale
    if len(shards) > 0:
        result = shard_levels(key, shape, shards, -0.22, 0.18) * result
    return jnp.clip(result, min=-bound, max=bound).astype(kind)


def setup_inputs(seed: int = 0) -> dict:
    key_list = jax.random.split(jax.random.key(seed), 11)
    weight = scatter_about(key_list[0], (EXPERTS, FF, D), 0.3, 1.796875, ((0, 4), (1, 2)))
    factor_a = scatter_about(key_list[1], (EXPERTS, R, D), 0.15, 1.2, ((0, 4), (1, 4), (2, 2)), jnp.float32)
    factor_b = scatter_about(key_list[2], (EXPERTS, R, FF), 0.15, 1.2, ((0, 4), (1, 4), (2, 2)), jnp.float32)
    moment_a = scatter_about(key_list[3], (EXPERTS, R, D), 0.1, 0.6, ((0, 4), (1, 4), (2, 2)), jnp.float32)
    second_a = jnp.clip(jnp.exp(math.log(1.0) - 5.809143 * jax.random.uniform(key_list[4], (EXPERTS, R, D), jnp.float32) ** shard_levels(key_list[4], (EXPERTS, R, D), ((0, 4), (1, 4), (2, 2)), -0.2, 0.2)), 0.003, 1.0)
    first_moment_factor_b = scatter_about(key_list[5], (EXPERTS, R, FF), 0.1, 0.6, ((0, 4), (1, 4), (2, 2)), jnp.float32)
    second_b = jnp.clip(jnp.exp(math.log(1.0) - 5.809143 * jax.random.uniform(key_list[6], (EXPERTS, R, FF), jnp.float32) ** shard_levels(key_list[6], (EXPERTS, R, FF), ((0, 4), (1, 4), (2, 2)), -0.2, 0.2)), 0.003, 1.0)
    grad_a = scatter_about(key_list[7], (N_DP, EXPERTS, R, D), 0.3, 2.0, ((0, 4), (1, 4), (3, 2)), jnp.float32)
    grad_b = scatter_about(key_list[8], (N_DP, EXPERTS, R, FF), 0.3, 2.0, ((0, 4), (1, 4), (3, 2)), jnp.float32)
    slot_of = jax.random.permutation(key_list[9], EXPERTS).astype(jnp.int32)
    return dict(weight=weight, factor_a=factor_a, factor_b=factor_b, moment_a=moment_a, second_a=second_a, first_moment_factor_b=first_moment_factor_b, second_b=second_b, grad_a=grad_a, grad_b=grad_b, slot_of=slot_of)


ADAPTER_SCALE = 2.0
BETA_ONE = 0.9
BETA_TWO = 0.95
LEARN_RATE = 0.08
STABILITY_TERM = 1e-08

def adam_update(param, moment, second, grad):
    corr_one = 1.0 - BETA_ONE ** ADAM_STEP
    corr_two = 1.0 - BETA_TWO ** ADAM_STEP
    moment_new = BETA_ONE * moment + (1.0 - BETA_ONE) * grad
    second_new = BETA_TWO * second + (1.0 - BETA_TWO) * grad * grad
    param_new = param - LEARN_RATE * (moment_new / corr_one) / (jnp.sqrt(second_new / corr_two) + STABILITY_TERM)
    return (param_new, moment_new, second_new)

def merge_single_expert(operands):
    weight_panel, a_rows, b_rows = operands
    weight_increment = jnp.dot(b_rows.T, a_rows, preferred_element_type=jnp.float32)
    return (weight_panel.astype(jnp.float32) + ADAPTER_SCALE * weight_increment).astype(jnp.bfloat16)

def reference(weight, factor_a, factor_b, moment_a, second_a, first_moment_factor_b, second_b, grad_a, grad_b, slot_of):
    reduced_factor_a = lax.optimization_barrier(jnp.sum(grad_a, axis=0))
    summed_b = lax.optimization_barrier(jnp.sum(grad_b, axis=0))
    new_a, new_moment_a, new_second_a = adam_update(factor_a, moment_a, second_a, reduced_factor_a)
    new_b, new_moment_b, new_second_b = adam_update(factor_b, first_moment_factor_b, second_b, summed_b)
    send_a = new_a.astype(jnp.bfloat16)
    send_b = new_b.astype(jnp.bfloat16)
    expert_ids = jnp.arange(EXPERTS, dtype=jnp.int32)
    expert_of_slot = jnp.zeros((EXPERTS,), jnp.int32).at[slot_of.astype(jnp.int32)].set(expert_ids)
    merged = lax.map(merge_single_expert, (weight, send_a[expert_of_slot], send_b[expert_of_slot]))
    return (merged, new_a, new_b, new_moment_a, new_second_a, new_moment_b, new_second_b)
```

```python
import jax
import jax.numpy as jnp
from jax import lax
from jax.sharding import PartitionSpec as P

ADAM_STEP = 20


ADAPTER_SCALE = 2.0
BETA_ONE = 0.9
BETA_TWO = 0.95
LEARN_RATE = 0.08
STABILITY_TERM = 1e-08


def adam_update(param, moment, second, grad):
    corr_one = 1.0 - BETA_ONE**ADAM_STEP
    corr_two = 1.0 - BETA_TWO**ADAM_STEP
    moment_new = BETA_ONE * moment + (1.0 - BETA_ONE) * grad
    second_new = BETA_TWO * second + (1.0 - BETA_TWO) * grad * grad
    param_new = param - LEARN_RATE * (moment_new / corr_one) / (
        jnp.sqrt(second_new / corr_two) + STABILITY_TERM
    )
    return (param_new, moment_new, second_new)


def swap(x, axis, n, k):
    return lax.ppermute(x, axis, [(i, i ^ k) for i in range(n)])


def per_device(
    n_dp,
    n_expert,
    n_tensor,
    weight,
    factor_a,
    factor_b,
    moment_a,
    second_a,
    first_moment_factor_b,
    second_b,
    grad_a,
    grad_b,
    slot_of,
):
    ranks = factor_a.shape[1]
    cols_a = factor_a.shape[2]
    me = lax.axis_index("dp")
    here = lax.axis_index("expert")

    def rows_of(k):
        start = (me ^ k) * ranks
        return (
            lax.dynamic_slice_in_dim(grad_a[0, 0], start, ranks, 0),
            lax.dynamic_slice_in_dim(grad_b[0, 0], start, ranks, 0),
        )

    summed_a, summed_b = rows_of(0)
    got = []
    for k in range(1, n_dp):
        piece = jnp.concatenate(rows_of(k), axis=1).astype(jnp.bfloat16)
        got.append(swap(piece, "dp", n_dp, k))
    for piece in got:
        summed_a = summed_a + piece[:, :cols_a].astype(jnp.float32)
        summed_b = summed_b + piece[:, cols_a:].astype(jnp.float32)

    new_a, new_moment_a, new_second_a = adam_update(factor_a, moment_a, second_a, summed_a[None])
    new_b, new_moment_b, new_second_b = adam_update(
        factor_b, first_moment_factor_b, second_b, summed_b[None]
    )
    send = jnp.concatenate([new_a[0], new_b[0]], axis=1).astype(jnp.bfloat16)

    experts = jnp.arange(n_expert, dtype=jnp.int32)
    wanted = jnp.sum(jnp.where(slot_of == here, experts, 0)) ^ here
    mine = send
    others = [swap(send, "expert", n_expert, k) for k in range(1, n_expert)]
    for k, piece in enumerate(others, 1):
        mine = jnp.where(wanted == k, piece, mine)

    parts = [mine] + [swap(mine, "dp", n_dp, k) for k in range(1, n_dp)]
    rows_a = jnp.concatenate([p[:, :cols_a] for p in parts], axis=0)
    rows_b = jnp.concatenate([p[:, cols_a:] for p in parts], axis=0)
    full_a = lax.all_gather(rows_a, "tensor", axis=1, tiled=True)
    increment = jnp.einsum("rf,rc->fc", rows_b, full_a, preferred_element_type=jnp.float32)
    merged = (weight[0].astype(jnp.float32) + ADAPTER_SCALE * increment).astype(jnp.bfloat16)
    return (merged[None], new_a, new_b, new_moment_a, new_second_a, new_moment_b, new_second_b)


def solution(mesh):
    sizes = dict(mesh.shape)

    def body(*args):
        return per_device(sizes["dp"], sizes["expert"], sizes["tensor"], *args)

    state = P("expert", "dp", "tensor")
    grad = P("dp", "expert", None, "tensor")
    weight = P("expert", "tensor", None)
    in_specs = (weight,) + (state,) * 6 + (grad,) * 2 + (P(),)
    out_specs = (weight,) + (state,) * 6
    return jax.shard_map(body, mesh=mesh, in_specs=in_specs, out_specs=out_specs, check_vma=False)
```

```python
import functools

import jax
import jax.numpy as jnp
from jax import lax
from jax.experimental import pallas as pl
from jax.experimental.pallas import tpu as pltpu
from jax.sharding import PartitionSpec as P

ADAM_STEP = 20


ADAPTER_SCALE = 2.0
BETA_ONE = 0.9
BETA_TWO = 0.95
LEARN_RATE = 0.08
STABILITY_TERM = 1e-08

F32 = jnp.float32
BF16 = jnp.bfloat16
VMEM = pl.BlockSpec(memory_space=pltpu.VMEM)
HBM = pl.BlockSpec(memory_space=pltpu.HBM)
PARAMS = pltpu.CompilerParams(vmem_limit_bytes=16 * 1024 * 1024)


def adam_update(param, moment, second, grad):
    corr_one = 1.0 - BETA_ONE**ADAM_STEP
    corr_two = 1.0 - BETA_TWO**ADAM_STEP
    moment_new = BETA_ONE * moment + (1.0 - BETA_ONE) * grad
    second_new = BETA_TWO * second + (1.0 - BETA_TWO) * grad * grad
    param_new = param - LEARN_RATE * (moment_new / corr_one) / (
        jnp.sqrt(second_new / corr_two) + STABILITY_TERM
    )
    return (param_new, moment_new, second_new)


def swap(x, axis, n, k):
    return lax.ppermute(x, axis, [(i, i ^ k) for i in range(n)])


def held(x):
    return pltpu.with_memory_space_constraint(x, pltpu.VMEM)


def left(x):
    return pltpu.with_memory_space_constraint(x, pltpu.HBM)


def estimate(nbytes, flops=0):
    return pl.CostEstimate(flops=flops, bytes_accessed=nbytes, transcendentals=0)


def pack_kernel(n_dp, ranks, cols_a, grad_a, grad_b, *refs):
    outs, rows, sems = refs[: n_dp - 1], refs[n_dp - 1], refs[n_dp]
    me = lax.axis_index("dp")
    copies = []
    for k in range(1, n_dp):
        start = pl.multiple_of((me ^ k) * ranks, ranks)
        pair = (
            pltpu.make_async_copy(
                grad_a.at[0, 0, pl.ds(start, ranks), :],
                rows.at[k - 1, :, pl.ds(0, cols_a)],
                sems.at[k - 1, 0],
            ),
            pltpu.make_async_copy(
                grad_b.at[0, 0, pl.ds(start, ranks), :],
                rows.at[k - 1, :, pl.ds(cols_a, rows.shape[2] - cols_a)],
                sems.at[k - 1, 1],
            ),
        )
        for copy in pair:
            copy.start()
        copies.append(pair)
    for k, pair in enumerate(copies):
        for copy in pair:
            copy.wait()
        outs[k][...] = rows[k].astype(BF16)


def load_kernel(ranks, cols_a, *refs):
    grad_a, grad_b, fa, fb, ma, mb, sa, sb, weight = refs[:9]
    grad, factor, moment, second, panel, sems = refs[9:]
    me = lax.axis_index("dp")
    start = pl.multiple_of(me * ranks, ranks)
    left = pl.ds(0, cols_a)
    right = pl.ds(cols_a, grad.shape[1] - cols_a)
    pairs = [
        (grad_a.at[0, 0, pl.ds(start, ranks), :], grad.at[:, left]),
        (grad_b.at[0, 0, pl.ds(start, ranks), :], grad.at[:, right]),
        (fa.at[0], factor.at[:, left]),
        (fb.at[0], factor.at[:, right]),
        (ma.at[0], moment.at[:, left]),
        (mb.at[0], moment.at[:, right]),
        (sa.at[0], second.at[:, left]),
        (sb.at[0], second.at[:, right]),
        (weight.at[0], panel),
    ]
    copies = [pltpu.make_async_copy(a, b, sems.at[i]) for i, (a, b) in enumerate(pairs)]
    for copy in copies:
        copy.start()
    for copy in copies:
        copy.wait()


def send_kernel(*refs):
    grad, factor, moment, second = refs[:4]
    total = grad[...]
    for piece in refs[4:-1]:
        total = total + piece[...].astype(F32)
    refs[-1][...] = adam_update(factor[...], moment[...], second[...], total)[0].astype(BF16)


def state_kernel(n_got, cols_a, slot_of, *refs):
    grad, factor, moment, second = refs[:4]
    outs = refs[4 + n_got : -1]
    here = lax.axis_index("expert")
    wanted = jnp.int32(0)
    for expert in range(slot_of.shape[0]):
        wanted = jnp.where(slot_of[expert] == here, expert, wanted)
    refs[-1][...] = jnp.broadcast_to(wanted ^ here, refs[-1].shape)
    total = grad[...]
    for piece in refs[4 : 4 + n_got]:
        total = total + piece[...].astype(F32)
    for i, new in enumerate(adam_update(factor[...], moment[...], second[...], total)):
        outs[2 * i][0] = new[:, :cols_a]
        outs[2 * i + 1][0] = new[:, cols_a:]


def select_kernel(choice, *refs):
    wanted = choice[:1, :1]
    kept = refs[0][...]
    for k in range(1, len(refs) - 1):
        kept = jnp.where(wanted == k, refs[k][...], kept)
    refs[-1][...] = kept


def merge_kernel(k, n_parts, rows, *refs):
    panel, rows_a, rows_b = refs[0], refs[1], refs[2]
    out, flipped, tile, sems = refs[-4:]
    cols = rows_a.shape[1]
    total = panel.shape[0]
    at = (lax.axis_index("tensor") ^ k) * cols
    columns = pl.ds(pl.multiple_of(at, cols), cols)
    flipped[...] = (rows_b[...].astype(F32) * ADAPTER_SCALE).T.astype(BF16)
    copies = []
    for step in range(total // rows):
        here = pl.ds(step * rows, rows)
        increment = jnp.dot(flipped[here, :], rows_a[...], preferred_element_type=F32)
        tile[here, :] = (panel[here, columns].astype(F32) + increment).astype(BF16)
        copy = pltpu.make_async_copy(tile.at[here, :], out.at[0, here, columns], sems.at[step])
        copy.start()
        copies.append(copy)
    for copy in copies:
        copy.wait()


def per_device(
    n_dp,
    n_expert,
    n_tensor,
    weight,
    factor_a,
    factor_b,
    moment_a,
    second_a,
    first_moment_factor_b,
    second_b,
    grad_a,
    grad_b,
    slot_of,
):
    ranks, cols_a = factor_a.shape[1:]
    cols_b = factor_b.shape[2]
    cols = cols_a + cols_b

    pieces = pl.pallas_call(
        functools.partial(pack_kernel, n_dp, ranks, cols_a),
        in_specs=[HBM, HBM],
        out_specs=[VMEM] * (n_dp - 1),
        out_shape=[pltpu.VMEM((ranks, cols), BF16)] * (n_dp - 1),
        scratch_shapes=[
            pltpu.VMEM((n_dp - 1, ranks, cols), F32),
            pltpu.SemaphoreType.DMA((n_dp - 1, 2)),
        ],
        compiler_params=PARAMS,
        name="pack",
    )(left(grad_a), left(grad_b))
    got = [held(swap(piece, "dp", n_dp, k)) for k, piece in enumerate(pieces, 1)]

    panel_shape = weight.shape[1:]
    *state, panel = pl.pallas_call(
        functools.partial(load_kernel, ranks, cols_a),
        in_specs=[HBM] * 9,
        out_specs=[VMEM] * 5,
        out_shape=[pltpu.VMEM((ranks, cols), F32)] * 4 + [pltpu.VMEM(panel_shape, BF16)],
        scratch_shapes=[pltpu.SemaphoreType.DMA((9,))],
        compiler_params=PARAMS,
        cost_estimate=estimate(weight.size * 2 + 4 * ranks * cols * 4),
        name="load",
    )(
        *map(
            left,
            (
                grad_a,
                grad_b,
                factor_a,
                factor_b,
                moment_a,
                first_moment_factor_b,
                second_a,
                second_b,
                weight,
            ),
        )
    )
    state = [held(x) for x in state]
    panel = held(panel)

    send = pl.pallas_call(
        send_kernel,
        in_specs=[VMEM] * (3 + n_dp),
        out_specs=VMEM,
        out_shape=pltpu.VMEM((ranks, cols), BF16),
        compiler_params=PARAMS,
        name="send",
    )(*state, *got)

    others = [held(swap(send, "expert", n_expert, k)) for k in range(1, n_expert)]
    *new, choice = pl.pallas_call(
        functools.partial(state_kernel, n_dp - 1, cols_a),
        in_specs=[pl.BlockSpec(memory_space=pltpu.SMEM)] + [VMEM] * (3 + n_dp),
        out_specs=[VMEM] * 7,
        out_shape=[
            jax.ShapeDtypeStruct(factor_a.shape, F32),
            jax.ShapeDtypeStruct(factor_b.shape, F32),
        ]
        * 3
        + [pltpu.VMEM((8, 128), jnp.int32)],
        compiler_params=PARAMS,
        cost_estimate=estimate(3 * ranks * cols * 4),
        name="state",
    )(slot_of, *state, *got)
    new_a, new_b, new_moment_a, new_moment_b, new_second_a, new_second_b = new
    mine = pl.pallas_call(
        select_kernel,
        in_specs=[VMEM] * (n_expert + 1),
        out_specs=VMEM,
        out_shape=pltpu.VMEM((ranks, cols), BF16),
        compiler_params=PARAMS,
        name="select",
    )(held(choice), held(send), *others)

    parts = [mine] + [swap(mine, "dp", n_dp, k) for k in range(1, n_dp)]
    rows_a = jnp.concatenate([p[:, :cols_a] for p in parts], axis=0)
    rows_b = held(jnp.concatenate([p[:, cols_a:] for p in parts], axis=0))
    merged = None
    step_rows = 128
    for k in range(n_tensor):
        block = held(rows_a if k == 0 else swap(rows_a, "tensor", n_tensor, k))
        operands = [panel, block, rows_b] + ([] if merged is None else [merged])
        merged = pl.pallas_call(
            functools.partial(merge_kernel, k, n_dp, step_rows),
            in_specs=[VMEM] * 3 + [HBM] * (len(operands) - 3),
            out_specs=HBM,
            out_shape=jax.ShapeDtypeStruct(weight.shape, BF16),
            scratch_shapes=[
                pltpu.VMEM((cols_b, ranks * n_dp), BF16),
                pltpu.VMEM((panel_shape[0], cols_a), BF16),
                pltpu.SemaphoreType.DMA((panel_shape[0] // step_rows,)),
            ],
            input_output_aliases={} if merged is None else {3: 0},
            compiler_params=PARAMS,
            cost_estimate=estimate(
                panel_shape[0] * cols_a * 2, 2 * panel_shape[0] * cols_a * ranks * n_dp
            ),
            name=f"merge{k}",
        )(*operands)
    return (merged, new_a, new_b, new_moment_a, new_second_a, new_moment_b, new_second_b)


def solution(mesh):
    sizes = dict(mesh.shape)

    def body(*args):
        return per_device(sizes["dp"], sizes["expert"], sizes["tensor"], *args)

    state = P("expert", "dp", "tensor")
    grad = P("dp", "expert", None, "tensor")
    weight = P("expert", "tensor", None)
    in_specs = (weight,) + (state,) * 6 + (grad,) * 2 + (P(),)
    out_specs = (weight,) + (state,) * 6
    return jax.shard_map(body, mesh=mesh, in_specs=in_specs, out_specs=out_specs, check_vma=False)
```

```python
import functools
import itertools

import jax
import jax.numpy as jnp
from jax import lax
from jax.experimental import pallas as pl
from jax.experimental.pallas import tpu as pltpu
from jax.sharding import PartitionSpec as P

ADAM_STEP = 20


ADAPTER_SCALE = 2.0
BETA_ONE = 0.9
BETA_TWO = 0.95
LEARN_RATE = 0.08
STABILITY_TERM = 1e-08

MOST_SWITCHED = 4

F32 = jnp.float32
BF16 = jnp.bfloat16
VMEM = pl.BlockSpec(memory_space=pltpu.VMEM)
SMEM = pl.BlockSpec(memory_space=pltpu.SMEM)
HBM = pl.BlockSpec(memory_space=pltpu.HBM)
PARAMS = pltpu.CompilerParams(vmem_limit_bytes=16 * 1024 * 1024)


def adam_update(param, moment, second, grad):
    corr_one = 1.0 - BETA_ONE**ADAM_STEP
    corr_two = 1.0 - BETA_TWO**ADAM_STEP
    moment_new = BETA_ONE * moment + (1.0 - BETA_ONE) * grad
    second_new = BETA_TWO * second + (1.0 - BETA_TWO) * grad * grad
    param_new = param - LEARN_RATE * (moment_new / corr_one) / (
        jnp.sqrt(second_new / corr_two) + STABILITY_TERM
    )
    return (param_new, moment_new, second_new)


def swap(x, axis, n, k):
    return lax.ppermute(x, axis, [(i, i ^ k) for i in range(n)])


def held(x):
    return pltpu.with_memory_space_constraint(x, pltpu.VMEM)


def left(x):
    return pltpu.with_memory_space_constraint(x, pltpu.HBM)


def estimate(nbytes, flops=0):
    return pl.CostEstimate(flops=flops, bytes_accessed=nbytes, transcendentals=0)


def pack_kernel(n_dp, ranks, cols_a, grad_a, grad_b, *refs):
    outs, rows, sems = refs[: n_dp - 1], refs[n_dp - 1], refs[n_dp]
    me = lax.axis_index("dp")
    copies = []
    for k in range(1, n_dp):
        start = pl.multiple_of((me ^ k) * ranks, ranks)
        pair = (
            pltpu.make_async_copy(
                grad_a.at[0, 0, pl.ds(start, ranks), :],
                rows.at[k - 1, :, pl.ds(0, cols_a)],
                sems.at[k - 1, 0],
            ),
            pltpu.make_async_copy(
                grad_b.at[0, 0, pl.ds(start, ranks), :],
                rows.at[k - 1, :, pl.ds(cols_a, rows.shape[2] - cols_a)],
                sems.at[k - 1, 1],
            ),
        )
        for copy in pair:
            copy.start()
        copies.append(pair)
    for k, pair in enumerate(copies):
        for copy in pair:
            copy.wait()
        outs[k][...] = rows[k].astype(BF16)


def load_kernel(ranks, cols_a, slot_of, *refs):
    grad_a, grad_b, fa, fb, ma, mb, sa, sb = refs[:8]
    grad, factor, moment, second, order, sems = refs[8:]
    me = lax.axis_index("dp")
    start = pl.multiple_of(me * ranks, ranks)
    first = pl.ds(0, cols_a)
    last = pl.ds(cols_a, grad.shape[1] - cols_a)
    pairs = [
        (grad_a.at[0, 0, pl.ds(start, ranks), :], grad.at[:, first]),
        (grad_b.at[0, 0, pl.ds(start, ranks), :], grad.at[:, last]),
        (fa.at[0], factor.at[:, first]),
        (fb.at[0], factor.at[:, last]),
        (ma.at[0], moment.at[:, first]),
        (mb.at[0], moment.at[:, last]),
        (sa.at[0], second.at[:, first]),
        (sb.at[0], second.at[:, last]),
    ]
    copies = [pltpu.make_async_copy(a, b, sems.at[i]) for i, (a, b) in enumerate(pairs)]
    for copy in copies:
        copy.start()
    n = slot_of.shape[0]
    number = jnp.int32(0)
    for i in range(n - 1):
        smaller = jnp.int32(0)
        for j in range(i + 1, n):
            smaller += (slot_of[j] < slot_of[i]).astype(jnp.int32)
        number = number * (n - i) + smaller
    order[0] = number
    for copy in copies:
        copy.wait()


def panel_kernel(weight, panel, sem):
    copy = pltpu.make_async_copy(weight.at[0], panel, sem)
    copy.start()
    copy.wait()


def send_kernel(*refs):
    grad, factor, moment, second = refs[:4]
    total = grad[...]
    for piece in refs[4:-1]:
        total = total + piece[...].astype(F32)
    refs[-1][...] = adam_update(factor[...], moment[...], second[...], total)[0].astype(BF16)


def state_kernel(n_got, cols_a, *refs):
    grad, factor, moment, second = refs[:4]
    outs = refs[4 + n_got :]
    total = grad[...]
    for piece in refs[4 : 4 + n_got]:
        total = total + piece[...].astype(F32)
    for i, new in enumerate(adam_update(factor[...], moment[...], second[...], total)):
        outs[2 * i][0] = new[:, :cols_a]
        outs[2 * i + 1][0] = new[:, cols_a:]


def join_kernel(cols_a, *refs):
    parts = refs[:-4]
    rows_a, flipped = refs[-3:-1]
    ranks = parts[0].shape[0]
    for i, part in enumerate(parts):
        rows_a[pl.ds(i * ranks, ranks), :] = part[:, :cols_a]
    rows_b = jnp.concatenate([part[:, cols_a:].astype(F32) for part in parts], axis=0)
    flipped[...] = (rows_b * ADAPTER_SCALE).T.astype(BF16)


def merge_kernel(k, width, *refs):
    panel, rows_a, flipped = refs[:3]
    out, tiles, sems = refs[-3:]
    cols = rows_a.shape[1]
    base = (lax.axis_index("tensor") ^ k) * cols
    copies = []
    for step in range(cols // width):
        columns = pl.ds(pl.multiple_of(base + step * width, width), width)
        increment = jnp.dot(
            flipped[...], rows_a[:, step * width : (step + 1) * width], preferred_element_type=F32
        )
        tiles[step] = (panel[:, columns].astype(F32) + increment).astype(BF16)
        copy = pltpu.make_async_copy(tiles.at[step], out.at[0, :, columns], sems.at[step])
        copy.start()
        copies.append(copy)
    for copy in copies:
        copy.wait()


def per_device(
    n_dp,
    n_expert,
    n_tensor,
    weight,
    factor_a,
    factor_b,
    moment_a,
    second_a,
    first_moment_factor_b,
    second_b,
    grad_a,
    grad_b,
    slot_of,
):
    ranks, cols_a = factor_a.shape[1:]
    cols_b = factor_b.shape[2]
    cols = cols_a + cols_b

    pieces = pl.pallas_call(
        functools.partial(pack_kernel, n_dp, ranks, cols_a),
        in_specs=[HBM, HBM],
        out_specs=[VMEM] * (n_dp - 1),
        out_shape=[pltpu.VMEM((ranks, cols), BF16)] * (n_dp - 1),
        scratch_shapes=[
            pltpu.VMEM((n_dp - 1, ranks, cols), F32),
            pltpu.SemaphoreType.DMA((n_dp - 1, 2)),
        ],
        compiler_params=PARAMS,
        name="pack",
    )(left(grad_a), left(grad_b))
    got = [held(swap(piece, "dp", n_dp, k)) for k, piece in enumerate(pieces, 1)]

    *state, order = pl.pallas_call(
        functools.partial(load_kernel, ranks, cols_a),
        in_specs=[SMEM] + [HBM] * 8,
        out_specs=[VMEM] * 4 + [SMEM],
        out_shape=[pltpu.VMEM((ranks, cols), F32)] * 4 + [pltpu.SMEM((1,), jnp.int32)],
        scratch_shapes=[pltpu.SemaphoreType.DMA((8,))],
        compiler_params=PARAMS,
        cost_estimate=estimate(4 * ranks * cols * 4),
        name="load",
    )(
        slot_of,
        *map(
            left,
            (
                grad_a,
                grad_b,
                factor_a,
                factor_b,
                moment_a,
                first_moment_factor_b,
                second_a,
                second_b,
            ),
        ),
    )
    state = [held(x) for x in state]

    send = pl.pallas_call(
        send_kernel,
        in_specs=[VMEM] * (3 + n_dp),
        out_specs=VMEM,
        out_shape=pltpu.VMEM((ranks, cols), BF16),
        compiler_params=PARAMS,
        name="send",
    )(*state, *got)

    def move(slots):
        def branch(send, state, got):
            mine = lax.ppermute(send, "expert", list(enumerate(slots)))
            new = pl.pallas_call(
                functools.partial(state_kernel, n_dp - 1, cols_a),
                in_specs=[VMEM] * (3 + n_dp),
                out_specs=[VMEM] * 6,
                out_shape=[
                    jax.ShapeDtypeStruct(factor_a.shape, F32),
                    jax.ShapeDtypeStruct(factor_b.shape, F32),
                ]
                * 3,
                compiler_params=PARAMS,
                cost_estimate=estimate(3 * ranks * cols * 4),
                name="state",
            )(*map(held, state), *map(held, got))
            return mine, new

        return branch

    if n_expert <= MOST_SWITCHED:
        orders = list(itertools.permutations(range(n_expert)))
        mine, new = lax.switch(order[0], [move(slots) for slots in orders], send, state, got)
    else:
        mine, new = move(range(n_expert))(send, state, got)
        here = lax.axis_index("expert")
        experts = jnp.arange(n_expert, dtype=jnp.int32)
        wanted = jnp.sum(jnp.where(slot_of == here, experts, 0)) ^ here
        for k in range(1, n_expert):
            mine = jnp.where(wanted == k, swap(send, "expert", n_expert, k), mine)
    new_a, new_b, new_moment_a, new_moment_b, new_second_a, new_second_b = new

    parts = [mine] + [swap(mine, "dp", n_dp, k) for k in range(1, n_dp)]
    panel_shape = weight.shape[1:]
    panel = pl.pallas_call(
        panel_kernel,
        in_specs=[HBM],
        out_specs=VMEM,
        out_shape=pltpu.VMEM(panel_shape, BF16),
        scratch_shapes=[pltpu.SemaphoreType.DMA],
        compiler_params=PARAMS,
        cost_estimate=estimate(weight.size * 4),
        name="panel",
    )(left(weight))
    rows_a, flipped, panel = pl.pallas_call(
        functools.partial(join_kernel, cols_a),
        in_specs=[VMEM] * (n_dp + 1),
        out_specs=[VMEM] * 3,
        out_shape=[
            pltpu.VMEM((ranks * n_dp, cols_a), BF16),
            pltpu.VMEM((cols_b, ranks * n_dp), BF16),
            pltpu.VMEM(panel_shape, BF16),
        ],
        input_output_aliases={n_dp: 2},
        compiler_params=PARAMS,
        name="join",
    )(*map(held, parts), held(panel))

    merged = None
    width = 512
    for k in range(n_tensor):
        block = held(rows_a if k == 0 else swap(rows_a, "tensor", n_tensor, k))
        operands = [held(panel), block, held(flipped)] + ([] if merged is None else [merged])
        merged = pl.pallas_call(
            functools.partial(merge_kernel, k, width),
            in_specs=[VMEM] * 3 + [HBM] * (len(operands) - 3),
            out_specs=HBM,
            out_shape=jax.ShapeDtypeStruct(weight.shape, BF16),
            scratch_shapes=[
                pltpu.VMEM((cols_a // width, panel_shape[0], width), BF16),
                pltpu.SemaphoreType.DMA((cols_a // width,)),
            ],
            input_output_aliases={} if merged is None else {3: 0},
            compiler_params=PARAMS,
            cost_estimate=estimate(
                panel_shape[0] * cols_a * 2, 2 * panel_shape[0] * cols_a * ranks * n_dp
            ),
            name=f"merge{k}",
        )(*operands)
    return (merged, new_a, new_b, new_moment_a, new_second_a, new_moment_b, new_second_b)


def solution(mesh):
    sizes = dict(mesh.shape)

    def body(*args):
        return per_device(sizes["dp"], sizes["expert"], sizes["tensor"], *args)

    state = P("expert", "dp", "tensor")
    grad = P("dp", "expert", None, "tensor")
    weight = P("expert", "tensor", None)
    in_specs = (weight,) + (state,) * 6 + (grad,) * 2 + (P(),)
    out_specs = (weight,) + (state,) * 6
    return jax.shard_map(body, mesh=mesh, in_specs=in_specs, out_specs=out_specs, check_vma=False)
```

```python
import functools
import itertools

import jax
import jax.numpy as jnp
from jax import lax
from jax.experimental import pallas as pl
from jax.experimental.pallas import tpu as pltpu
from jax.sharding import PartitionSpec as P

ADAM_STEP = 20


ADAPTER_SCALE = 2.0
BETA_ONE = 0.9
BETA_TWO = 0.95
LEARN_RATE = 0.08
STABILITY_TERM = 1e-08

MOST_SWITCHED = 4

F32 = jnp.float32
BF16 = jnp.bfloat16
VMEM = pl.BlockSpec(memory_space=pltpu.VMEM)
SMEM = pl.BlockSpec(memory_space=pltpu.SMEM)
HBM = pl.BlockSpec(memory_space=pltpu.HBM)
PARAMS = pltpu.CompilerParams(vmem_limit_bytes=16 * 1024 * 1024)


def adam_update(param, moment, second, grad):
    corr_one = 1.0 - BETA_ONE**ADAM_STEP
    corr_two = 1.0 - BETA_TWO**ADAM_STEP
    moment_new = BETA_ONE * moment + (1.0 - BETA_ONE) * grad
    second_new = BETA_TWO * second + (1.0 - BETA_TWO) * grad * grad
    param_new = param - LEARN_RATE * (moment_new / corr_one) / (
        jnp.sqrt(second_new / corr_two) + STABILITY_TERM
    )
    return (param_new, moment_new, second_new)


def swap(x, axis, n, k):
    return lax.ppermute(x, axis, [(i, i ^ k) for i in range(n)])


def held(x):
    return pltpu.with_memory_space_constraint(x, pltpu.VMEM)


def left(x):
    return pltpu.with_memory_space_constraint(x, pltpu.HBM)


def estimate(nbytes, flops=0):
    return pl.CostEstimate(flops=flops, bytes_accessed=nbytes, transcendentals=0)


class Plan:
    def __init__(self, n, ranks, cols_a, cols_b):
        self.n, self.ranks, self.cols_a, self.cols_b = n, ranks, cols_a, cols_b
        cols = cols_a + cols_b
        middle = min(-(-cols // 256) * 128, cols_a)
        self.cols = cols
        self.spans = [(0, middle), (middle, cols)]
        self.widths = [middle, cols - middle]
        bits = [1 << i for i in range(n.bit_length() - 1)]
        self.orders = [bits, bits[::-1]]

    def split(self, half, step):
        blocks = list(range(self.n))
        for bit in self.orders[half][:step]:
            blocks = [k for k in blocks if not k & bit]
        bit = self.orders[half][step]
        return [k for k in blocks if k & bit], [k for k in blocks if not k & bit]

    def gathered(self, half, step):
        blocks = [0]
        for bit in self.orders[half][:step]:
            blocks = blocks + [k ^ bit for k in blocks]
        return blocks

    def pieces(self, half):
        low, high = self.spans[half]
        out = []
        if low < self.cols_a:
            out.append((False, low, min(high, self.cols_a), 0))
        if high > self.cols_a:
            start = max(low, self.cols_a)
            out.append((True, start - self.cols_a, high - self.cols_a, start - low))
        return out

    def grad_copies(self, grads, blocks, into, sems):
        me = lax.axis_index("dp")
        copies, at = [], 0
        for half in range(2):
            for i, k in enumerate(blocks[half]):
                rows = pl.ds(pl.multiple_of((me ^ k) * self.ranks, self.ranks), self.ranks)
                for is_b, start, stop, column in self.pieces(half):
                    copies.append(
                        pltpu.make_async_copy(
                            grads[is_b].at[0, 0, rows, pl.ds(start, stop - start)],
                            into[half].at[
                                pl.ds(i * self.ranks, self.ranks), pl.ds(column, stop - start)
                            ],
                            sems.at[at],
                        )
                    )
                    at += 1
        return copies

    def count(self, blocks):
        return sum(len(blocks[half]) * len(self.pieces(half)) for half in range(2))


def pack_kernel(plan, blocks, grad_a, grad_b, send0, send1, rows0, rows1, sems):
    copies = plan.grad_copies((grad_a, grad_b), blocks, (rows0, rows1), sems)
    for copy in copies:
        copy.start()
    for copy in copies:
        copy.wait()
    send0[...] = rows0[...].astype(BF16)
    send1[...] = rows1[...].astype(BF16)


def load_kernel(plan, blocks, *refs):
    slot_of, grad_a, grad_b, fa, fb, ma, mb, sa, sb = refs[:9]
    keep0, keep1, factor, moment, second, order, slots, sems, grad_sems = refs[9:]
    first = pl.ds(0, plan.cols_a)
    last = pl.ds(plan.cols_a, plan.cols_b)
    pairs = [
        (slot_of, slots),
        (fa.at[0], factor.at[:, first]),
        (fb.at[0], factor.at[:, last]),
        (ma.at[0], moment.at[:, first]),
        (mb.at[0], moment.at[:, last]),
        (sa.at[0], second.at[:, first]),
        (sb.at[0], second.at[:, last]),
    ]
    copies = [pltpu.make_async_copy(a, b, sems.at[i]) for i, (a, b) in enumerate(pairs)]
    copies += plan.grad_copies((grad_a, grad_b), blocks, (keep0, keep1), grad_sems)
    for copy in copies:
        copy.start()
    copies[0].wait()
    n = slots.shape[0]
    number = jnp.int32(0)
    if n <= MOST_SWITCHED:
        for i in range(n - 1):
            smaller = jnp.int32(0)
            for j in range(i + 1, n):
                smaller += (slots[j] < slots[i]).astype(jnp.int32)
            number = number * (n - i) + smaller
    order[0] = number
    for copy in copies[1:]:
        copy.wait()


def panel_kernel(k, chunks, weight, after, panel, sems):
    rows, cols = panel.shape
    at = pl.multiple_of((lax.axis_index("tensor") ^ k) * cols, cols)
    step = rows // chunks
    copies = [
        pltpu.make_async_copy(
            weight.at[0, pl.ds(i * step, step), pl.ds(at, cols)],
            panel.at[pl.ds(i * step, step), :],
            sems.at[i],
        )
        for i in range(chunks)
    ]
    for copy in copies:
        copy.start()
    for copy in copies:
        copy.wait()


def half_kernel(plan, step, *refs):
    r = plan.ranks
    for half in range(2):
        keep, got, send, kept = refs[half::2]
        total = keep[...] + got[...].astype(F32)
        blocks = plan.split(half, step - 1)[1]
        sent, stay = plan.split(half, step)
        rows = lambda ks: [total[blocks.index(k) * r : (blocks.index(k) + 1) * r] for k in ks]
        send[...] = jnp.concatenate(rows(sent), axis=0).astype(BF16)
        kept[...] = jnp.concatenate(rows(stay), axis=0)


def new_state(plan, refs):
    factor, moment, second = refs[:3]
    for half in range(2):
        keep, got = refs[3 + half], refs[5 + half]
        span = pl.ds(plan.spans[half][0], plan.widths[half])
        total = keep[...] + got[...].astype(F32)
        yield adam_update(factor[:, span], moment[:, span], second[:, span], total)


def send_kernel(plan, *refs):
    for half, new in enumerate(new_state(plan, refs[:7])):
        refs[8][:, pl.ds(plan.spans[half][0], plan.widths[half])] = new[0].astype(BF16)


def state_kernel(plan, *refs):
    outs = refs[7:]
    for half, new in enumerate(new_state(plan, refs[:7])):
        for is_b, start, stop, column in plan.pieces(half):
            for i, value in enumerate(new):
                outs[2 * i + is_b][0, :, pl.ds(start, stop - start)] = value[
                    :, column : column + stop - start
                ]


def stack_kernel(*refs):
    for half in range(2):
        held_rows, got, out = refs[half:6:2]
        rows = [held_rows[...].astype(F32), got[...].astype(F32)]
        out[...] = jnp.concatenate(rows, axis=0).astype(BF16)


def join_kernel(plan, *refs):
    rows_a, flipped = refs[4:]
    r = plan.ranks
    rows_b = None
    for half in range(2):
        rows = [ref[...].astype(F32) for ref in refs[half:4:2]]
        rows = jnp.concatenate(rows, axis=0)
        blocks = plan.gathered(half, len(plan.orders[half]))
        rows = [rows[blocks.index(k) * r : (blocks.index(k) + 1) * r] for k in range(plan.n)]
        rows = jnp.concatenate(rows, axis=0)
        for is_b, start, stop, column in plan.pieces(half):
            part = rows[:, column : column + stop - start]
            if is_b:
                flipped[...] = (part * ADAPTER_SCALE).T.astype(BF16)
            else:
                rows_a[:, start:stop] = part.astype(BF16)


def merge_kernel(k, width, *refs):
    panel, rows_a, flipped = refs[:3]
    out, tiles, sems = refs[-3:]
    cols = rows_a.shape[1]
    base = (lax.axis_index("tensor") ^ k) * cols
    copies = []
    for step in range(cols // width):
        span = slice(step * width, (step + 1) * width)
        increment = jnp.dot(flipped[...], rows_a[:, span], preferred_element_type=F32)
        tiles[step] = (panel[:, span].astype(F32) + increment).astype(BF16)
        columns = pl.ds(pl.multiple_of(base + step * width, width), width)
        copy = pltpu.make_async_copy(tiles.at[step], out.at[0, :, columns], sems.at[step])
        copy.start()
        copies.append(copy)
    for copy in copies:
        copy.wait()


def per_device(
    n_dp,
    n_expert,
    n_tensor,
    weight,
    factor_a,
    factor_b,
    moment_a,
    second_a,
    first_moment_factor_b,
    second_b,
    grad_a,
    grad_b,
    slot_of,
):
    ranks, cols_a = factor_a.shape[1:]
    cols_b = factor_b.shape[2]
    plan = Plan(n_dp, ranks, cols_a, cols_b)
    cols, widths = plan.cols, plan.widths
    steps = len(plan.orders[0])
    panel_shape = (weight.shape[1], cols_a)

    def load_panel(k, after):
        chunks = 8
        return held(
            pl.pallas_call(
                functools.partial(panel_kernel, k, chunks),
                in_specs=[HBM, VMEM],
                out_specs=VMEM,
                out_shape=pltpu.VMEM(panel_shape, BF16),
                scratch_shapes=[pltpu.SemaphoreType.DMA((chunks,))],
                compiler_params=PARAMS,
                cost_estimate=estimate(panel_shape[0] * cols_a * 4),
                name=f"panel{k}",
            )(left(weight), held(after))
        )

    sent = [plan.split(half, 0)[0] for half in range(2)]
    kept = [plan.split(half, 0)[1] for half in range(2)]
    shapes = [(len(sent[half]) * ranks, widths[half]) for half in range(2)]
    grads = (left(grad_a), left(grad_b))
    send = pl.pallas_call(
        functools.partial(pack_kernel, plan, sent),
        in_specs=[HBM, HBM],
        out_specs=[VMEM] * 2,
        out_shape=[pltpu.VMEM(shape, BF16) for shape in shapes],
        scratch_shapes=[pltpu.VMEM(shape, F32) for shape in shapes]
        + [pltpu.SemaphoreType.DMA((plan.count(sent),))],
        compiler_params=PARAMS,
        name="pack",
    )(*grads)
    got = [held(swap(send[half], "dp", n_dp, plan.orders[half][0])) for half in range(2)]
    *keep, factor, moment, second, order = pl.pallas_call(
        functools.partial(load_kernel, plan, kept),
        in_specs=[HBM] * 9,
        out_specs=[VMEM] * 5 + [SMEM],
        out_shape=[pltpu.VMEM(shape, F32) for shape in shapes]
        + [pltpu.VMEM((ranks, cols), F32)] * 3
        + [pltpu.SMEM((1,), jnp.int32)],
        scratch_shapes=[
            pltpu.SMEM(slot_of.shape, jnp.int32),
            pltpu.SemaphoreType.DMA((7,)),
            pltpu.SemaphoreType.DMA((plan.count(kept),)),
        ],
        compiler_params=PARAMS,
        cost_estimate=estimate(5 * ranks * cols * 4),
        name="load",
    )(
        left(slot_of),
        *grads,
        *map(
            left,
            (factor_a, factor_b, moment_a, first_moment_factor_b, second_a, second_b),
        ),
    )
    for step in range(1, steps):
        sent = [plan.split(half, step)[0] for half in range(2)]
        shapes = [(len(sent[half]) * ranks, widths[half]) for half in range(2)]
        *send, keep0, keep1 = pl.pallas_call(
            functools.partial(half_kernel, plan, step),
            in_specs=[VMEM] * 4,
            out_specs=[VMEM] * 4,
            out_shape=[pltpu.VMEM(shape, BF16) for shape in shapes]
            + [pltpu.VMEM(shape, F32) for shape in shapes],
            compiler_params=PARAMS,
            name=f"half{step}",
        )(*map(held, keep), *got)
        keep = [keep0, keep1]
        got = [held(swap(send[half], "dp", n_dp, plan.orders[half][step])) for half in range(2)]
    panel = load_panel(0, keep[0])
    state = [held(x) for x in (factor, moment, second, *keep)] + got

    send, panel = pl.pallas_call(
        functools.partial(send_kernel, plan),
        in_specs=[VMEM] * 8,
        out_specs=[VMEM] * 2,
        out_shape=[pltpu.VMEM((ranks, cols), BF16), pltpu.VMEM(panel_shape, BF16)],
        input_output_aliases={7: 1},
        compiler_params=PARAMS,
        name="send",
    )(*state, panel)

    def move(slots):
        def branch(send, state):
            mine = lax.ppermute(send, "expert", list(enumerate(slots)))
            new = pl.pallas_call(
                functools.partial(state_kernel, plan),
                in_specs=[VMEM] * 7,
                out_specs=[VMEM] * 6,
                out_shape=[
                    jax.ShapeDtypeStruct(factor_a.shape, F32),
                    jax.ShapeDtypeStruct(factor_b.shape, F32),
                ]
                * 3,
                compiler_params=PARAMS,
                cost_estimate=estimate(3 * ranks * cols * 4),
                name="state",
            )(*map(held, state))
            return [mine[:, low:high] for low, high in plan.spans], new

        return branch

    if n_expert <= MOST_SWITCHED:
        orders = list(itertools.permutations(range(n_expert)))
        mine, new = lax.switch(order[0], [move(slots) for slots in orders], send, state)
    else:
        mine, new = move(range(n_expert))(send, state)
        here = lax.axis_index("expert")
        experts = jnp.arange(n_expert, dtype=jnp.int32)
        wanted = jnp.sum(jnp.where(slot_of == here, experts, 0)) ^ here
        for k in range(1, n_expert):
            moved = swap(send, "expert", n_expert, k)
            mine = [
                jnp.where(wanted == k, moved[:, low:high], x)
                for x, (low, high) in zip(mine, plan.spans)
            ]
    new_a, new_b, new_moment_a, new_moment_b, new_second_a, new_second_b = new

    panels = [panel]
    for step in range(steps):
        got = [held(swap(mine[half], "dp", n_dp, plan.orders[half][step])) for half in range(2)]
        mine = [held(x) for x in mine]
        if step < steps - 1:
            rows = 2 * ranks << step
            mine = pl.pallas_call(
                stack_kernel,
                in_specs=[VMEM] * 4,
                out_specs=[VMEM] * 2,
                out_shape=[pltpu.VMEM((rows, widths[half]), BF16) for half in range(2)],
                compiler_params=PARAMS,
                name=f"stack{step}",
            )(*mine, *got)
    panels += [load_panel(k, mine[0]) for k in range(1, n_tensor)]
    rows_a, flipped, *panels = pl.pallas_call(
        functools.partial(join_passing, plan, n_tensor),
        in_specs=[VMEM] * (4 + n_tensor),
        out_specs=[VMEM] * (2 + n_tensor),
        out_shape=[
            pltpu.VMEM((ranks * n_dp, cols_a), BF16),
            pltpu.VMEM((cols_b, ranks * n_dp), BF16),
        ]
        + [pltpu.VMEM(panel_shape, BF16)] * n_tensor,
        input_output_aliases={4 + k: 2 + k for k in range(n_tensor)},
        compiler_params=PARAMS,
        name="join",
    )(*mine, *got, *map(held, panels))

    merged = None
    width = 512
    for k in range(n_tensor):
        block = held(rows_a if k == 0 else swap(rows_a, "tensor", n_tensor, k))
        operands = [held(panels[k]), block, held(flipped)] + ([] if merged is None else [merged])
        merged = pl.pallas_call(
            functools.partial(merge_kernel, k, width),
            in_specs=[VMEM] * 3 + [HBM] * (len(operands) - 3),
            out_specs=HBM,
            out_shape=jax.ShapeDtypeStruct(weight.shape, BF16),
            scratch_shapes=[
                pltpu.VMEM((cols_a // width, panel_shape[0], width), BF16),
                pltpu.SemaphoreType.DMA((cols_a // width,)),
            ],
            input_output_aliases={} if merged is None else {3: 0},
            compiler_params=PARAMS,
            cost_estimate=estimate(
                panel_shape[0] * cols_a * 2, 2 * panel_shape[0] * cols_a * ranks * n_dp
            ),
            name=f"merge{k}",
        )(*operands)
    return (merged, new_a, new_b, new_moment_a, new_second_a, new_moment_b, new_second_b)


def join_passing(plan, n_tensor, *refs):
    join_kernel(plan, *refs[:4], *refs[4 + n_tensor : 6 + n_tensor])


def solution(mesh):
    sizes = dict(mesh.shape)

    def body(*args):
        return per_device(sizes["dp"], sizes["expert"], sizes["tensor"], *args)

    state = P("expert", "dp", "tensor")
    grad = P("dp", "expert", None, "tensor")
    weight = P("expert", "tensor", None)
    in_specs = (weight,) + (state,) * 6 + (grad,) * 2 + (P(),)
    out_specs = (weight,) + (state,) * 6
    return jax.shard_map(body, mesh=mesh, in_specs=in_specs, out_specs=out_specs, check_vma=False)
```

```python
import functools
import itertools

import jax
import jax.numpy as jnp
from jax import lax
from jax.experimental import pallas as pl
from jax.experimental.pallas import tpu as pltpu
from jax.sharding import PartitionSpec as P

ADAM_STEP = 20


ADAPTER_SCALE = 2.0
BETA_ONE = 0.9
BETA_TWO = 0.95
LEARN_RATE = 0.08
STABILITY_TERM = 1e-08

MOST_SWITCHED = 4

F32 = jnp.float32
BF16 = jnp.bfloat16
VMEM = pl.BlockSpec(memory_space=pltpu.VMEM)
SMEM = pl.BlockSpec(memory_space=pltpu.SMEM)
HBM = pl.BlockSpec(memory_space=pltpu.HBM)
PARAMS = pltpu.CompilerParams(vmem_limit_bytes=16 * 1024 * 1024)


def adam_update(param, moment, second, grad):
    corr_one = 1.0 - BETA_ONE**ADAM_STEP
    corr_two = 1.0 - BETA_TWO**ADAM_STEP
    moment_new = BETA_ONE * moment + (1.0 - BETA_ONE) * grad
    second_new = BETA_TWO * second + (1.0 - BETA_TWO) * grad * grad
    param_new = param - LEARN_RATE * (moment_new / corr_one) / (
        jnp.sqrt(second_new / corr_two) + STABILITY_TERM
    )
    return (param_new, moment_new, second_new)


def swap(x, axis, n, k):
    return lax.ppermute(x, axis, [(i, i ^ k) for i in range(n)])


def held(x):
    return pltpu.with_memory_space_constraint(x, pltpu.VMEM)


def left(x):
    return pltpu.with_memory_space_constraint(x, pltpu.HBM)


def estimate(nbytes, flops=0):
    return pl.CostEstimate(flops=flops, bytes_accessed=nbytes, transcendentals=0)


def pack_kernel(n_dp, ranks, cols_a, grad_a, grad_b, *refs):
    outs, rows, sems = refs[: n_dp - 1], refs[n_dp - 1], refs[n_dp]
    me = lax.axis_index("dp")
    copies = []
    for k in range(1, n_dp):
        start = pl.multiple_of((me ^ k) * ranks, ranks)
        pair = (
            pltpu.make_async_copy(
                grad_a.at[0, 0, pl.ds(start, ranks), :],
                rows.at[k - 1, :, pl.ds(0, cols_a)],
                sems.at[k - 1, 0],
            ),
            pltpu.make_async_copy(
                grad_b.at[0, 0, pl.ds(start, ranks), :],
                rows.at[k - 1, :, pl.ds(cols_a, rows.shape[2] - cols_a)],
                sems.at[k - 1, 1],
            ),
        )
        for copy in pair:
            copy.start()
        copies.append(pair)
    for k, pair in enumerate(copies):
        for copy in pair:
            copy.wait()
        outs[k][...] = rows[k].astype(BF16)


def load_kernel(ranks, cols_a, slots_in, *refs):
    grad_a, grad_b, fa, fb, ma, mb, sa, sb = refs[:8]
    grad, factor, moment, second, order, slot_of, sems = refs[8:]
    me = lax.axis_index("dp")
    start = pl.multiple_of(me * ranks, ranks)
    first = pl.ds(0, cols_a)
    last = pl.ds(cols_a, grad.shape[1] - cols_a)
    pairs = [
        (grad_a.at[0, 0, pl.ds(start, ranks), :], grad.at[:, first]),
        (grad_b.at[0, 0, pl.ds(start, ranks), :], grad.at[:, last]),
        (fa.at[0], factor.at[:, first]),
        (fb.at[0], factor.at[:, last]),
        (ma.at[0], moment.at[:, first]),
        (mb.at[0], moment.at[:, last]),
        (sa.at[0], second.at[:, first]),
        (sb.at[0], second.at[:, last]),
        (slots_in, slot_of),
    ]
    copies = [pltpu.make_async_copy(a, b, sems.at[i]) for i, (a, b) in enumerate(pairs)]
    for copy in copies:
        copy.start()
    copies.pop().wait()
    n = slot_of.shape[0]
    number = jnp.int32(0)
    for i in range(n - 1):
        smaller = jnp.int32(0)
        for j in range(i + 1, n):
            smaller += (slot_of[j] < slot_of[i]).astype(jnp.int32)
        number = number * (n - i) + smaller
    order[0] = number
    for copy in copies:
        copy.wait()


def panel_kernel(weight, panel, sem):
    copy = pltpu.make_async_copy(weight.at[0], panel, sem)
    copy.start()
    copy.wait()


def send_kernel(*refs):
    grad, factor, moment, second = refs[:4]
    total = grad[...]
    for piece in refs[4:-1]:
        total = total + piece[...].astype(F32)
    refs[-1][...] = adam_update(factor[...], moment[...], second[...], total)[0].astype(BF16)


def state_kernel(n_got, cols_a, *refs):
    grad, factor, moment, second = refs[:4]
    outs = refs[4 + n_got : -1]
    refs[-1][...] = jnp.zeros_like(refs[-1])
    total = grad[...]
    for piece in refs[4 : 4 + n_got]:
        total = total + piece[...].astype(F32)
    for i, new in enumerate(adam_update(factor[...], moment[...], second[...], total)):
        outs[2 * i][0] = new[:, :cols_a]
        outs[2 * i + 1][0] = new[:, cols_a:]


def pass_kernel(*refs):
    pass


def join_kernel(cols_a, *refs):
    parts = refs[:-2]
    rows_a, flipped = refs[-2:]
    ranks = parts[0].shape[0]
    for i, part in enumerate(parts):
        rows_a[pl.ds(i * ranks, ranks), :] = part[:, :cols_a]
    rows_b = jnp.concatenate([part[:, cols_a:].astype(F32) for part in parts], axis=0)
    flipped[...] = (rows_b * ADAPTER_SCALE).T.astype(BF16)


def merge_kernel(k, width, *refs):
    panel, rows_a, flipped = refs[:3]
    out, tiles, sems = refs[-3:]
    cols = rows_a.shape[1]
    base = (lax.axis_index("tensor") ^ k) * cols
    copies = []
    for step in range(cols // width):
        columns = pl.ds(pl.multiple_of(base + step * width, width), width)
        increment = jnp.dot(
            flipped[...], rows_a[:, step * width : (step + 1) * width], preferred_element_type=F32
        )
        tiles[step] = (panel[:, columns].astype(F32) + increment).astype(BF16)
        copy = pltpu.make_async_copy(tiles.at[step], out.at[0, :, columns], sems.at[step])
        copy.start()
        copies.append(copy)
    for copy in copies:
        copy.wait()


def per_device(
    n_dp,
    n_expert,
    n_tensor,
    weight,
    factor_a,
    factor_b,
    moment_a,
    second_a,
    first_moment_factor_b,
    second_b,
    grad_a,
    grad_b,
    slot_of,
):
    ranks, cols_a = factor_a.shape[1:]
    cols_b = factor_b.shape[2]
    cols = cols_a + cols_b

    pieces = pl.pallas_call(
        functools.partial(pack_kernel, n_dp, ranks, cols_a),
        in_specs=[HBM, HBM],
        out_specs=[VMEM] * (n_dp - 1),
        out_shape=[pltpu.VMEM((ranks, cols), BF16)] * (n_dp - 1),
        scratch_shapes=[
            pltpu.VMEM((n_dp - 1, ranks, cols), F32),
            pltpu.SemaphoreType.DMA((n_dp - 1, 2)),
        ],
        compiler_params=PARAMS,
        name="pack",
    )(left(grad_a), left(grad_b))
    got = [held(swap(piece, "dp", n_dp, k)) for k, piece in enumerate(pieces, 1)]

    *state, order = pl.pallas_call(
        functools.partial(load_kernel, ranks, cols_a),
        in_specs=[HBM] * 9,
        out_specs=[VMEM] * 4 + [SMEM],
        out_shape=[pltpu.VMEM((ranks, cols), F32)] * 4 + [pltpu.SMEM((1,), jnp.int32)],
        scratch_shapes=[pltpu.SMEM(slot_of.shape, jnp.int32), pltpu.SemaphoreType.DMA((9,))],
        compiler_params=PARAMS,
        cost_estimate=estimate(4 * ranks * cols * 4),
        name="load",
    )(
        *map(
            left,
            (
                slot_of,
                grad_a,
                grad_b,
                factor_a,
                factor_b,
                moment_a,
                first_moment_factor_b,
                second_a,
                second_b,
            ),
        ),
    )
    state = [held(x) for x in state]

    send = pl.pallas_call(
        send_kernel,
        in_specs=[VMEM] * (3 + n_dp),
        out_specs=VMEM,
        out_shape=pltpu.VMEM((ranks, cols), BF16),
        compiler_params=PARAMS,
        name="send",
    )(*state, *got)

    panel_shape = weight.shape[1:]

    def finish(mine, state, got):
        *new, mark = pl.pallas_call(
            functools.partial(state_kernel, n_dp - 1, cols_a),
            in_specs=[VMEM] * (3 + n_dp),
            out_specs=[VMEM] * 7,
            out_shape=[
                jax.ShapeDtypeStruct(factor_a.shape, F32),
                jax.ShapeDtypeStruct(factor_b.shape, F32),
            ]
            * 3
            + [pltpu.VMEM((8, 128), F32)],
            compiler_params=PARAMS,
            cost_estimate=estimate(3 * ranks * cols * 4),
            name="state",
        )(*map(held, state), *map(held, got))
        panel = pl.pallas_call(
            panel_kernel,
            in_specs=[HBM],
            out_specs=VMEM,
            out_shape=pltpu.VMEM(panel_shape, BF16),
            scratch_shapes=[pltpu.SemaphoreType.DMA],
            compiler_params=PARAMS,
            cost_estimate=estimate(weight.size * 4),
            name="panel",
        )(left(weight))
        mine, panel = pl.pallas_call(
            pass_kernel,
            in_specs=[VMEM] * 3,
            out_specs=[VMEM] * 2,
            out_shape=[pltpu.VMEM((ranks, cols), BF16), pltpu.VMEM(panel_shape, BF16)],
            input_output_aliases={0: 0, 1: 1},
            compiler_params=PARAMS,
            name="pass",
        )(held(mine), held(panel), held(mark))
        parts = [mine] + [swap(mine, "dp", n_dp, k) for k in range(1, n_dp)]
        rows_a, flipped = pl.pallas_call(
            functools.partial(join_kernel, cols_a),
            in_specs=[VMEM] * n_dp,
            out_specs=[VMEM] * 2,
            out_shape=[
                pltpu.VMEM((ranks * n_dp, cols_a), BF16),
                pltpu.VMEM((cols_b, ranks * n_dp), BF16),
            ],
            compiler_params=PARAMS,
            name="join",
        )(*map(held, parts))

        merged = None
        width = 512
        for k in range(n_tensor):
            block = held(rows_a if k == 0 else swap(rows_a, "tensor", n_tensor, k))
            operands = [held(panel), block, held(flipped)]
            operands += [] if merged is None else [merged]
            merged = pl.pallas_call(
                functools.partial(merge_kernel, k, width),
                in_specs=[VMEM] * 3 + [HBM] * (len(operands) - 3),
                out_specs=HBM,
                out_shape=jax.ShapeDtypeStruct(weight.shape, BF16),
                scratch_shapes=[
                    pltpu.VMEM((cols_a // width, panel_shape[0], width), BF16),
                    pltpu.SemaphoreType.DMA((cols_a // width,)),
                ],
                input_output_aliases={} if merged is None else {3: 0},
                compiler_params=PARAMS,
                cost_estimate=estimate(
                    panel_shape[0] * cols_a * 2, 2 * panel_shape[0] * cols_a * ranks * n_dp
                ),
                name=f"merge{k}",
            )(*operands)
        new_a, new_b, new_moment_a, new_moment_b, new_second_a, new_second_b = new
        return (merged, new_a, new_b, new_moment_a, new_second_a, new_moment_b, new_second_b)

    def branch(slots):
        pairs = list(enumerate(slots))
        return lambda send, *rest: finish(lax.ppermute(send, "expert", pairs), *rest)

    if n_expert <= MOST_SWITCHED:
        orders = list(itertools.permutations(range(n_expert)))
        return lax.switch(order[0], [branch(slots) for slots in orders], send, state, got)
    here = lax.axis_index("expert")
    experts = jnp.arange(n_expert, dtype=jnp.int32)
    wanted = jnp.sum(jnp.where(slot_of == here, experts, 0)) ^ here
    mine = send
    for k in range(1, n_expert):
        mine = jnp.where(wanted == k, swap(send, "expert", n_expert, k), mine)
    return finish(mine, state, got)


def solution(mesh):
    sizes = dict(mesh.shape)

    def body(*args):
        return per_device(sizes["dp"], sizes["expert"], sizes["tensor"], *args)

    state = P("expert", "dp", "tensor")
    grad = P("dp", "expert", None, "tensor")
    weight = P("expert", "tensor", None)
    in_specs = (weight,) + (state,) * 6 + (grad,) * 2 + (P(),)
    out_specs = (weight,) + (state,) * 6
    return jax.shard_map(body, mesh=mesh, in_specs=in_specs, out_specs=out_specs, check_vma=False)
```

```python
import functools
import itertools

import jax
import jax.numpy as jnp
from jax import lax
from jax.experimental import pallas as pl
from jax.experimental.pallas import tpu as pltpu
from jax.sharding import PartitionSpec as P

ADAM_STEP = 20


ADAPTER_SCALE = 2.0
BETA_ONE = 0.9
BETA_TWO = 0.95
LEARN_RATE = 0.08
STABILITY_TERM = 1e-08

MOST_SWITCHED = 4

F32 = jnp.float32
BF16 = jnp.bfloat16
VMEM = pl.BlockSpec(memory_space=pltpu.VMEM)
SMEM = pl.BlockSpec(memory_space=pltpu.SMEM)
HBM = pl.BlockSpec(memory_space=pltpu.HBM)
PARAMS = pltpu.CompilerParams(vmem_limit_bytes=16 * 1024 * 1024)


def adam_update(param, moment, second, grad):
    corr_one = 1.0 - BETA_ONE**ADAM_STEP
    corr_two = 1.0 - BETA_TWO**ADAM_STEP
    moment_new = BETA_ONE * moment + (1.0 - BETA_ONE) * grad
    second_new = BETA_TWO * second + (1.0 - BETA_TWO) * grad * grad
    param_new = param - LEARN_RATE * (moment_new / corr_one) / (
        jnp.sqrt(second_new / corr_two) + STABILITY_TERM
    )
    return (param_new, moment_new, second_new)


def swap(x, axis, n, k):
    return lax.ppermute(x, axis, [(i, i ^ k) for i in range(n)])


def held(x):
    return pltpu.with_memory_space_constraint(x, pltpu.VMEM)


def left(x):
    return pltpu.with_memory_space_constraint(x, pltpu.HBM)


def estimate(nbytes, flops=0):
    return pl.CostEstimate(flops=flops, bytes_accessed=nbytes, transcendentals=0)


def pack_kernel(n_dp, ranks, cols_a, grad_a, grad_b, *refs):
    outs, rows, sems = refs[: n_dp - 1], refs[n_dp - 1], refs[n_dp]
    me = lax.axis_index("dp")
    copies = []
    for k in range(1, n_dp):
        start = pl.multiple_of((me ^ k) * ranks, ranks)
        pair = (
            pltpu.make_async_copy(
                grad_a.at[0, 0, pl.ds(start, ranks), :],
                rows.at[k - 1, :, pl.ds(0, cols_a)],
                sems.at[k - 1, 0],
            ),
            pltpu.make_async_copy(
                grad_b.at[0, 0, pl.ds(start, ranks), :],
                rows.at[k - 1, :, pl.ds(cols_a, rows.shape[2] - cols_a)],
                sems.at[k - 1, 1],
            ),
        )
        for copy in pair:
            copy.start()
        copies.append(pair)
    for k, pair in enumerate(copies):
        for copy in pair:
            copy.wait()
        outs[k][...] = rows[k].astype(BF16)


def load_kernel(ranks, cols_a, slots_in, *refs):
    grad_a, grad_b, fa, fb, ma, mb, sa, sb = refs[:8]
    grad, factor, moment, second, order, slot_of, sems = refs[8:]
    me = lax.axis_index("dp")
    start = pl.multiple_of(me * ranks, ranks)
    first = pl.ds(0, cols_a)
    last = pl.ds(cols_a, grad.shape[1] - cols_a)
    pairs = [
        (grad_a.at[0, 0, pl.ds(start, ranks), :], grad.at[:, first]),
        (grad_b.at[0, 0, pl.ds(start, ranks), :], grad.at[:, last]),
        (fa.at[0], factor.at[:, first]),
        (fb.at[0], factor.at[:, last]),
        (ma.at[0], moment.at[:, first]),
        (mb.at[0], moment.at[:, last]),
        (sa.at[0], second.at[:, first]),
        (sb.at[0], second.at[:, last]),
        (slots_in, slot_of),
    ]
    copies = [pltpu.make_async_copy(a, b, sems.at[i]) for i, (a, b) in enumerate(pairs)]
    for copy in copies:
        copy.start()
    copies.pop().wait()
    n = slot_of.shape[0]
    number = jnp.int32(0)
    for i in range(n - 1):
        smaller = jnp.int32(0)
        for j in range(i + 1, n):
            smaller += (slot_of[j] < slot_of[i]).astype(jnp.int32)
        number = number * (n - i) + smaller
    order[0] = number
    for copy in copies:
        copy.wait()


def panel_kernel(weight, mine, panel, kept, sems):
    copies = [
        pltpu.make_async_copy(weight.at[0], panel, sems.at[0]),
        pltpu.make_async_copy(mine, kept, sems.at[1]),
    ]
    for copy in copies:
        copy.start()
    for copy in copies:
        copy.wait()


def send_kernel(*refs):
    grad, factor, moment, second = refs[:4]
    total = grad[...]
    for piece in refs[4:-1]:
        total = total + piece[...].astype(F32)
    refs[-1][...] = adam_update(factor[...], moment[...], second[...], total)[0].astype(BF16)


def state_kernel(n_got, cols_a, *refs):
    ins = refs[: 4 + n_got]
    outs = refs[4 + n_got :]
    width = 128

    def some_columns(start, outs, at):
        here = pl.ds(pl.multiple_of(start, width), width)
        there = pl.ds(pl.multiple_of(at, width), width)
        grad, factor, moment, second = (ref[:, here] for ref in ins[:4])
        for piece in ins[4:]:
            grad = grad + piece[:, here].astype(F32)
        for out, new in zip(outs, adam_update(factor, moment, second, grad)):
            out[0, :, there] = new

    @pl.loop(0, cols_a // width)
    def _(i):
        some_columns(i * width, outs[::2], i * width)

    @pl.loop(0, (ins[0].shape[1] - cols_a) // width)
    def _(i):
        some_columns(cols_a + i * width, outs[1::2], i * width)


def join_kernel(cols_a, *refs):
    parts = refs[:-4]
    rows_a, flipped = refs[-3:-1]
    ranks = parts[0].shape[0]
    for i, part in enumerate(parts):
        rows_a[pl.ds(i * ranks, ranks), :] = part[:, :cols_a]
    rows_b = jnp.concatenate([part[:, cols_a:].astype(F32) for part in parts], axis=0)
    flipped[...] = (rows_b * ADAPTER_SCALE).T.astype(BF16)


def merge_kernel(k, width, *refs):
    panel, rows_a, flipped = refs[:3]
    out, tiles, sems = refs[-3:]
    cols = rows_a.shape[1]
    base = (lax.axis_index("tensor") ^ k) * cols
    copies = []
    for step in range(cols // width):
        columns = pl.ds(pl.multiple_of(base + step * width, width), width)
        increment = jnp.dot(
            flipped[...], rows_a[:, step * width : (step + 1) * width], preferred_element_type=F32
        )
        tiles[step] = (panel[:, columns].astype(F32) + increment).astype(BF16)
        copy = pltpu.make_async_copy(tiles.at[step], out.at[0, :, columns], sems.at[step])
        copy.start()
        copies.append(copy)
    for copy in copies:
        copy.wait()


def per_device(
    n_dp,
    n_expert,
    n_tensor,
    weight,
    factor_a,
    factor_b,
    moment_a,
    second_a,
    first_moment_factor_b,
    second_b,
    grad_a,
    grad_b,
    slot_of,
):
    ranks, cols_a = factor_a.shape[1:]
    cols_b = factor_b.shape[2]
    cols = cols_a + cols_b

    pieces = pl.pallas_call(
        functools.partial(pack_kernel, n_dp, ranks, cols_a),
        in_specs=[HBM, HBM],
        out_specs=[VMEM] * (n_dp - 1),
        out_shape=[pltpu.VMEM((ranks, cols), BF16)] * (n_dp - 1),
        scratch_shapes=[
            pltpu.VMEM((n_dp - 1, ranks, cols), F32),
            pltpu.SemaphoreType.DMA((n_dp - 1, 2)),
        ],
        compiler_params=PARAMS,
        name="pack",
    )(left(grad_a), left(grad_b))
    got = [held(swap(piece, "dp", n_dp, k)) for k, piece in enumerate(pieces, 1)]

    *state, order = pl.pallas_call(
        functools.partial(load_kernel, ranks, cols_a),
        in_specs=[HBM] * 9,
        out_specs=[VMEM] * 4 + [SMEM],
        out_shape=[pltpu.VMEM((ranks, cols), F32)] * 4 + [pltpu.SMEM((1,), jnp.int32)],
        scratch_shapes=[pltpu.SMEM(slot_of.shape, jnp.int32), pltpu.SemaphoreType.DMA((9,))],
        compiler_params=PARAMS,
        cost_estimate=estimate(4 * ranks * cols * 4),
        name="load",
    )(
        *map(
            left,
            (
                slot_of,
                grad_a,
                grad_b,
                factor_a,
                factor_b,
                moment_a,
                first_moment_factor_b,
                second_a,
                second_b,
            ),
        ),
    )
    state = [held(x) for x in state]

    send = pl.pallas_call(
        send_kernel,
        in_specs=[VMEM] * (3 + n_dp),
        out_specs=VMEM,
        out_shape=pltpu.VMEM((ranks, cols), BF16),
        compiler_params=PARAMS,
        name="send",
    )(*state, *got)

    def move(slots):
        def branch(send, state, got):
            mine = lax.ppermute(send, "expert", list(enumerate(slots)))
            new = pl.pallas_call(
                functools.partial(state_kernel, n_dp - 1, cols_a),
                in_specs=[VMEM] * (3 + n_dp),
                out_specs=[VMEM] * 6,
                out_shape=[
                    jax.ShapeDtypeStruct(factor_a.shape, F32),
                    jax.ShapeDtypeStruct(factor_b.shape, F32),
                ]
                * 3,
                compiler_params=PARAMS,
                cost_estimate=estimate(3 * ranks * cols * 4),
                name="state",
            )(*map(held, state), *map(held, got))
            return mine, new

        return branch

    if n_expert <= MOST_SWITCHED:
        orders = list(itertools.permutations(range(n_expert)))
        mine, new = lax.switch(order[0], [move(slots) for slots in orders], send, state, got)
    else:
        mine, new = move(range(n_expert))(send, state, got)
        here = lax.axis_index("expert")
        experts = jnp.arange(n_expert, dtype=jnp.int32)
        wanted = jnp.sum(jnp.where(slot_of == here, experts, 0)) ^ here
        for k in range(1, n_expert):
            mine = jnp.where(wanted == k, swap(send, "expert", n_expert, k), mine)
    new_a, new_b, new_moment_a, new_moment_b, new_second_a, new_second_b = new

    panel_shape = weight.shape[1:]
    parts = [swap(mine, "dp", n_dp, k) for k in range(1, n_dp)]
    panel, mine = pl.pallas_call(
        panel_kernel,
        in_specs=[HBM] * 2,
        out_specs=[VMEM] * 2,
        out_shape=[pltpu.VMEM(panel_shape, BF16), pltpu.VMEM((ranks, cols), BF16)],
        scratch_shapes=[pltpu.SemaphoreType.DMA((2,))],
        compiler_params=PARAMS,
        cost_estimate=estimate(weight.size * 4),
        name="panel",
    )(left(weight), left(mine))
    parts = [mine] + parts
    rows_a, flipped, panel = pl.pallas_call(
        functools.partial(join_kernel, cols_a),
        in_specs=[VMEM] * (n_dp + 1),
        out_specs=[VMEM] * 3,
        out_shape=[
            pltpu.VMEM((ranks * n_dp, cols_a), BF16),
            pltpu.VMEM((cols_b, ranks * n_dp), BF16),
            pltpu.VMEM(panel_shape, BF16),
        ],
        input_output_aliases={n_dp: 2},
        compiler_params=PARAMS,
        name="join",
    )(*map(held, parts), held(panel))

    merged = None
    width = 512
    for k in range(n_tensor):
        block = held(rows_a if k == 0 else swap(rows_a, "tensor", n_tensor, k))
        operands = [held(panel), block, held(flipped)] + ([] if merged is None else [merged])
        merged = pl.pallas_call(
            functools.partial(merge_kernel, k, width),
            in_specs=[VMEM] * 3 + [HBM] * (len(operands) - 3),
            out_specs=HBM,
            out_shape=jax.ShapeDtypeStruct(weight.shape, BF16),
            scratch_shapes=[
                pltpu.VMEM((cols_a // width, panel_shape[0], width), BF16),
                pltpu.SemaphoreType.DMA((cols_a // width,)),
            ],
            input_output_aliases={} if merged is None else {3: 0},
            compiler_params=PARAMS,
            cost_estimate=estimate(
                panel_shape[0] * cols_a * 2, 2 * panel_shape[0] * cols_a * ranks * n_dp
            ),
            name=f"merge{k}",
        )(*operands)
    return (merged, new_a, new_b, new_moment_a, new_second_a, new_moment_b, new_second_b)


def solution(mesh):
    sizes = dict(mesh.shape)

    def body(*args):
        return per_device(sizes["dp"], sizes["expert"], sizes["tensor"], *args)

    state = P("expert", "dp", "tensor")
    grad = P("dp", "expert", None, "tensor")
    weight = P("expert", "tensor", None)
    in_specs = (weight,) + (state,) * 6 + (grad,) * 2 + (P(),)
    out_specs = (weight,) + (state,) * 6
    return jax.shard_map(body, mesh=mesh, in_specs=in_specs, out_specs=out_specs, check_vma=False)
```

```python
import functools
import itertools

import jax
import jax.numpy as jnp
from jax import lax
from jax.experimental import pallas as pl
from jax.experimental.pallas import tpu as pltpu
from jax.sharding import PartitionSpec as P

ADAM_STEP = 20


ADAPTER_SCALE = 2.0
BETA_ONE = 0.9
BETA_TWO = 0.95
LEARN_RATE = 0.08
STABILITY_TERM = 1e-08

MOST_SWITCHED = 4

F32 = jnp.float32
BF16 = jnp.bfloat16
VMEM = pl.BlockSpec(memory_space=pltpu.VMEM)
SMEM = pl.BlockSpec(memory_space=pltpu.SMEM)
HBM = pl.BlockSpec(memory_space=pltpu.HBM)
PARAMS = pltpu.CompilerParams(vmem_limit_bytes=16 * 1024 * 1024)


def adam_update(param, moment, second, grad):
    corr_one = 1.0 - BETA_ONE**ADAM_STEP
    corr_two = 1.0 - BETA_TWO**ADAM_STEP
    moment_new = BETA_ONE * moment + (1.0 - BETA_ONE) * grad
    second_new = BETA_TWO * second + (1.0 - BETA_TWO) * grad * grad
    param_new = param - LEARN_RATE * (moment_new / corr_one) / (
        jnp.sqrt(second_new / corr_two) + STABILITY_TERM
    )
    return (param_new, moment_new, second_new)


def swap(x, axis, n, k):
    return lax.ppermute(x, axis, [(i, i ^ k) for i in range(n)])


def held(x):
    return pltpu.with_memory_space_constraint(x, pltpu.VMEM)


def left(x):
    return pltpu.with_memory_space_constraint(x, pltpu.HBM)


def estimate(nbytes, flops=0):
    return pl.CostEstimate(flops=flops, bytes_accessed=nbytes, transcendentals=0)


def load_kernel(ranks, cols_a, *refs):
    slots_in, grad_a, grad_b, fa, fb, ma, mb, sa, sb = refs[:9]
    packed, grad, factor, moment, second, order, rows, slot_of, sems = refs[9:]
    first = pl.ds(0, cols_a)
    last = pl.ds(cols_a, grad.shape[1] - cols_a)
    pairs = [
        (grad_a.at[0, 0], rows.at[:, first]),
        (grad_b.at[0, 0], rows.at[:, last]),
        (slots_in, slot_of),
        (fa.at[0], factor.at[:, first]),
        (fb.at[0], factor.at[:, last]),
        (ma.at[0], moment.at[:, first]),
        (mb.at[0], moment.at[:, last]),
        (sa.at[0], second.at[:, first]),
        (sb.at[0], second.at[:, last]),
    ]
    copies = [pltpu.make_async_copy(a, b, sems.at[i]) for i, (a, b) in enumerate(pairs)]
    for copy in copies:
        copy.start()
    for copy in copies[:2]:
        copy.wait()
    packed[...] = rows[...].astype(BF16)
    me = lax.axis_index("dp")
    grad[...] = rows[pl.ds(pl.multiple_of(me * ranks, ranks), ranks), :]
    copies[2].wait()
    n = slot_of.shape[0]
    number = jnp.int32(0)
    if n <= MOST_SWITCHED:
        for i in range(n - 1):
            smaller = jnp.int32(0)
            for j in range(i + 1, n):
                smaller += (slot_of[j] < slot_of[i]).astype(jnp.int32)
            number = number * (n - i) + smaller
    order[0] = number
    for copy in copies[3:]:
        copy.wait()


def summed(grad, arrived, ranks, columns):
    me = lax.axis_index("dp")
    total = grad[:, columns]
    for j in range(arrived.shape[0] // ranks):
        piece = arrived[pl.ds(j * ranks, ranks), columns].astype(F32)
        total = total + jnp.where(me == j, 0.0, piece)
    return total


def panel_kernel(weight, mine, panel, kept, sems):
    copies = [
        pltpu.make_async_copy(weight.at[0], panel, sems.at[0]),
        pltpu.make_async_copy(mine, kept, sems.at[1]),
    ]
    for copy in copies:
        copy.start()
    for copy in copies:
        copy.wait()


def send_kernel(grad, factor, moment, second, arrived, out):
    total = summed(grad, arrived, grad.shape[0], slice(None))
    out[...] = adam_update(factor[...], moment[...], second[...], total)[0].astype(BF16)


def state_kernel(cols_a, grad, factor, moment, second, arrived, *outs):
    width = 128

    def some_columns(start, outs, at):
        here = pl.ds(pl.multiple_of(start, width), width)
        there = pl.ds(pl.multiple_of(at, width), width)
        total = summed(grad, arrived, grad.shape[0], here)
        for out, new in zip(
            outs, adam_update(factor[:, here], moment[:, here], second[:, here], total)
        ):
            out[0, :, there] = new

    @pl.loop(0, cols_a // width)
    def _(i):
        some_columns(i * width, outs[::2], i * width)

    @pl.loop(0, (grad.shape[1] - cols_a) // width)
    def _(i):
        some_columns(cols_a + i * width, outs[1::2], i * width)


def join_kernel(cols_a, *refs):
    parts = refs[:-4]
    rows_a, flipped = refs[-3:-1]
    ranks = parts[0].shape[0]
    for i, part in enumerate(parts):
        rows_a[pl.ds(i * ranks, ranks), :] = part[:, :cols_a]
    rows_b = jnp.concatenate([part[:, cols_a:].astype(F32) for part in parts], axis=0)
    flipped[...] = (rows_b * ADAPTER_SCALE).T.astype(BF16)


def merge_kernel(k, width, *refs):
    panel, rows_a, flipped = refs[:3]
    out, tiles, sems = refs[-3:]
    cols = rows_a.shape[1]
    base = (lax.axis_index("tensor") ^ k) * cols
    copies = []
    for step in range(cols // width):
        columns = pl.ds(pl.multiple_of(base + step * width, width), width)
        increment = jnp.dot(
            flipped[...], rows_a[:, step * width : (step + 1) * width], preferred_element_type=F32
        )
        tiles[step] = (panel[:, columns].astype(F32) + increment).astype(BF16)
        copy = pltpu.make_async_copy(tiles.at[step], out.at[0, :, columns], sems.at[step])
        copy.start()
        copies.append(copy)
    for copy in copies:
        copy.wait()


def per_device(
    n_dp,
    n_expert,
    n_tensor,
    weight,
    factor_a,
    factor_b,
    moment_a,
    second_a,
    first_moment_factor_b,
    second_b,
    grad_a,
    grad_b,
    slot_of,
):
    ranks, cols_a = factor_a.shape[1:]
    cols_b = factor_b.shape[2]
    cols = cols_a + cols_b

    packed, *state, order = pl.pallas_call(
        functools.partial(load_kernel, ranks, cols_a),
        in_specs=[HBM] * 9,
        out_specs=[VMEM] * 5 + [SMEM],
        out_shape=[pltpu.VMEM((n_dp * ranks, cols), BF16)]
        + [pltpu.VMEM((ranks, cols), F32)] * 4
        + [pltpu.SMEM((1,), jnp.int32)],
        scratch_shapes=[
            pltpu.VMEM((n_dp * ranks, cols), F32),
            pltpu.SMEM(slot_of.shape, jnp.int32),
            pltpu.SemaphoreType.DMA((9,)),
        ],
        compiler_params=PARAMS,
        name="load",
    )(
        *map(
            left,
            (
                slot_of,
                grad_a,
                grad_b,
                factor_a,
                factor_b,
                moment_a,
                first_moment_factor_b,
                second_a,
                second_b,
            ),
        ),
    )
    state = [held(x) for x in state]
    arrived = held(lax.all_to_all(packed, "dp", 0, 0, tiled=True))

    send = pl.pallas_call(
        send_kernel,
        in_specs=[VMEM] * 5,
        out_specs=VMEM,
        out_shape=pltpu.VMEM((ranks, cols), BF16),
        compiler_params=PARAMS,
        name="send",
    )(*state, arrived)

    def move(slots):
        def branch(send, *state):
            mine = lax.ppermute(send, "expert", list(enumerate(slots)))
            new = pl.pallas_call(
                functools.partial(state_kernel, cols_a),
                in_specs=[VMEM] * 5,
                out_specs=[VMEM] * 6,
                out_shape=[
                    jax.ShapeDtypeStruct(factor_a.shape, F32),
                    jax.ShapeDtypeStruct(factor_b.shape, F32),
                ]
                * 3,
                compiler_params=PARAMS,
                cost_estimate=estimate(3 * ranks * cols * 4),
                name="state",
            )(*map(held, state))
            return mine, new

        return branch

    if n_expert <= MOST_SWITCHED:
        orders = list(itertools.permutations(range(n_expert)))
        mine, new = lax.switch(order[0], [move(slots) for slots in orders], send, *state, arrived)
    else:
        mine, new = move(range(n_expert))(send, *state, arrived)
        here = lax.axis_index("expert")
        experts = jnp.arange(n_expert, dtype=jnp.int32)
        wanted = jnp.sum(jnp.where(slot_of == here, experts, 0)) ^ here
        for k in range(1, n_expert):
            mine = jnp.where(wanted == k, swap(send, "expert", n_expert, k), mine)
    new_a, new_b, new_moment_a, new_moment_b, new_second_a, new_second_b = new

    panel_shape = weight.shape[1:]
    parts = [swap(mine, "dp", n_dp, k) for k in range(1, n_dp)]
    panel, mine = pl.pallas_call(
        panel_kernel,
        in_specs=[HBM] * 2,
        out_specs=[VMEM] * 2,
        out_shape=[pltpu.VMEM(panel_shape, BF16), pltpu.VMEM((ranks, cols), BF16)],
        scratch_shapes=[pltpu.SemaphoreType.DMA((2,))],
        compiler_params=PARAMS,
        cost_estimate=estimate(weight.size * 4),
        name="panel",
    )(left(weight), left(mine))
    parts = [mine] + parts
    rows_a, flipped, panel = pl.pallas_call(
        functools.partial(join_kernel, cols_a),
        in_specs=[VMEM] * (n_dp + 1),
        out_specs=[VMEM] * 3,
        out_shape=[
            pltpu.VMEM((ranks * n_dp, cols_a), BF16),
            pltpu.VMEM((cols_b, ranks * n_dp), BF16),
            pltpu.VMEM(panel_shape, BF16),
        ],
        input_output_aliases={n_dp: 2},
        compiler_params=PARAMS,
        name="join",
    )(*map(held, parts), held(panel))

    merged = None
    width = 512
    for k in range(n_tensor):
        block = held(rows_a if k == 0 else swap(rows_a, "tensor", n_tensor, k))
        operands = [held(panel), block, held(flipped)] + ([] if merged is None else [merged])
        merged = pl.pallas_call(
            functools.partial(merge_kernel, k, width),
            in_specs=[VMEM] * 3 + [HBM] * (len(operands) - 3),
            out_specs=HBM,
            out_shape=jax.ShapeDtypeStruct(weight.shape, BF16),
            scratch_shapes=[
                pltpu.VMEM((cols_a // width, panel_shape[0], width), BF16),
                pltpu.SemaphoreType.DMA((cols_a // width,)),
            ],
            input_output_aliases={} if merged is None else {3: 0},
            compiler_params=PARAMS,
            cost_estimate=estimate(
                panel_shape[0] * cols_a * 2, 2 * panel_shape[0] * cols_a * ranks * n_dp
            ),
            name=f"merge{k}",
        )(*operands)
    return (merged, new_a, new_b, new_moment_a, new_second_a, new_moment_b, new_second_b)


def solution(mesh):
    sizes = dict(mesh.shape)

    def body(*args):
        return per_device(sizes["dp"], sizes["expert"], sizes["tensor"], *args)

    state = P("expert", "dp", "tensor")
    grad = P("dp", "expert", None, "tensor")
    weight = P("expert", "tensor", None)
    in_specs = (weight,) + (state,) * 6 + (grad,) * 2 + (P(),)
    out_specs = (weight,) + (state,) * 6
    return jax.shard_map(body, mesh=mesh, in_specs=in_specs, out_specs=out_specs, check_vma=False)
```

```python
import functools
import itertools

import jax
import jax.numpy as jnp
from jax import lax
from jax.experimental import pallas as pl
from jax.experimental.pallas import tpu as pltpu
from jax.sharding import PartitionSpec as P

ADAM_STEP = 20


ADAPTER_SCALE = 2.0
BETA_ONE = 0.9
BETA_TWO = 0.95
LEARN_RATE = 0.08
STABILITY_TERM = 1e-08

MOST_SWITCHED = 4

F32 = jnp.float32
BF16 = jnp.bfloat16
VMEM = pl.BlockSpec(memory_space=pltpu.VMEM)
SMEM = pl.BlockSpec(memory_space=pltpu.SMEM)
HBM = pl.BlockSpec(memory_space=pltpu.HBM)
PARAMS = pltpu.CompilerParams(vmem_limit_bytes=16 * 1024 * 1024)


def adam_update(param, moment, second, grad):
    corr_one = 1.0 - BETA_ONE**ADAM_STEP
    corr_two = 1.0 - BETA_TWO**ADAM_STEP
    moment_new = BETA_ONE * moment + (1.0 - BETA_ONE) * grad
    second_new = BETA_TWO * second + (1.0 - BETA_TWO) * grad * grad
    param_new = param - LEARN_RATE * (moment_new / corr_one) / (
        jnp.sqrt(second_new / corr_two) + STABILITY_TERM
    )
    return (param_new, moment_new, second_new)


def swap(x, axis, n, k):
    return lax.ppermute(x, axis, [(i, i ^ k) for i in range(n)])


def held(x):
    return pltpu.with_memory_space_constraint(x, pltpu.VMEM)


def left(x):
    return pltpu.with_memory_space_constraint(x, pltpu.HBM)


def estimate(nbytes, flops=0):
    return pl.CostEstimate(flops=flops, bytes_accessed=nbytes, transcendentals=0)


def pack_kernel(n_dp, ranks, cols_a, grad_a, grad_b, *refs):
    outs, rows, sems = refs[: n_dp - 1], refs[n_dp - 1], refs[n_dp]
    me = lax.axis_index("dp")
    copies = []
    for k in range(1, n_dp):
        start = pl.multiple_of((me ^ k) * ranks, ranks)
        pair = (
            pltpu.make_async_copy(
                grad_a.at[0, 0, pl.ds(start, ranks), :],
                rows.at[k - 1, :, pl.ds(0, cols_a)],
                sems.at[k - 1, 0],
            ),
            pltpu.make_async_copy(
                grad_b.at[0, 0, pl.ds(start, ranks), :],
                rows.at[k - 1, :, pl.ds(cols_a, rows.shape[2] - cols_a)],
                sems.at[k - 1, 1],
            ),
        )
        for copy in pair:
            copy.start()
        copies.append(pair)
    for k, pair in enumerate(copies):
        for copy in pair:
            copy.wait()
        outs[k][...] = rows[k].astype(BF16)


def load_kernel(ranks, cols_a, slots_in, *refs):
    grad_a, grad_b, fa, fb, ma, mb, sa, sb = refs[:8]
    grad, factor, moment, second, order, slot_of, sems = refs[8:]
    me = lax.axis_index("dp")
    start = pl.multiple_of(me * ranks, ranks)
    first = pl.ds(0, cols_a)
    last = pl.ds(cols_a, grad.shape[1] - cols_a)
    pairs = [
        (grad_a.at[0, 0, pl.ds(start, ranks), :], grad.at[:, first]),
        (grad_b.at[0, 0, pl.ds(start, ranks), :], grad.at[:, last]),
        (fa.at[0], factor.at[:, first]),
        (fb.at[0], factor.at[:, last]),
        (ma.at[0], moment.at[:, first]),
        (mb.at[0], moment.at[:, last]),
        (sa.at[0], second.at[:, first]),
        (sb.at[0], second.at[:, last]),
        (slots_in, slot_of),
    ]
    copies = [pltpu.make_async_copy(a, b, sems.at[i]) for i, (a, b) in enumerate(pairs)]
    for copy in copies:
        copy.start()
    copies.pop().wait()
    n = slot_of.shape[0]
    number = jnp.int32(0)
    for i in range(n - 1):
        smaller = jnp.int32(0)
        for j in range(i + 1, n):
            smaller += (slot_of[j] < slot_of[i]).astype(jnp.int32)
        number = number * (n - i) + smaller
    order[0] = number
    for copy in copies:
        copy.wait()


def panel_kernel(weight, mine, panel, kept, sems):
    copies = [
        pltpu.make_async_copy(weight.at[0], panel, sems.at[0]),
        pltpu.make_async_copy(mine, kept, sems.at[1]),
    ]
    for copy in copies:
        copy.start()
    for copy in copies:
        copy.wait()


def send_kernel(*refs):
    grad, factor, moment, second = refs[:4]
    total = grad[...]
    for piece in refs[4:-1]:
        total = total + piece[...].astype(F32)
    refs[-1][...] = adam_update(factor[...], moment[...], second[...], total)[0].astype(BF16)


def state_kernel(n_got, cols_a, *refs):
    ins = refs[: 4 + n_got]
    outs = refs[4 + n_got :]
    width = 128

    def some_columns(start, outs, at):
        here = pl.ds(pl.multiple_of(start, width), width)
        there = pl.ds(pl.multiple_of(at, width), width)
        grad, factor, moment, second = (ref[:, here] for ref in ins[:4])
        for piece in ins[4:]:
            grad = grad + piece[:, here].astype(F32)
        for out, new in zip(outs, adam_update(factor, moment, second, grad)):
            out[0, :, there] = new

    @pl.loop(0, cols_a // width)
    def _(i):
        some_columns(i * width, outs[::2], i * width)

    @pl.loop(0, (ins[0].shape[1] - cols_a) // width)
    def _(i):
        some_columns(cols_a + i * width, outs[1::2], i * width)


def join_kernel(cols_a, *refs):
    parts = refs[:-4]
    rows_a, flipped = refs[-3:-1]
    ranks = parts[0].shape[0]
    for i, part in enumerate(parts):
        rows_a[pl.ds(i * ranks, ranks), :] = part[:, :cols_a]
    rows_b = jnp.concatenate([part[:, cols_a:].astype(F32) for part in parts], axis=0)
    flipped[...] = (rows_b * ADAPTER_SCALE).T.astype(BF16)


def merge_kernel(k, width, *refs):
    panel, rows_a, flipped = refs[:3]
    out, tiles, sems = refs[-3:]
    cols = rows_a.shape[1]
    base = (lax.axis_index("tensor") ^ k) * cols
    copies = []
    for step in range(cols // width):
        columns = pl.ds(pl.multiple_of(base + step * width, width), width)
        increment = jnp.dot(
            flipped[...], rows_a[:, step * width : (step + 1) * width], preferred_element_type=F32
        )
        tiles[step] = (panel[:, columns].astype(F32) + increment).astype(BF16)
        copy = pltpu.make_async_copy(tiles.at[step], out.at[0, :, columns], sems.at[step])
        copy.start()
        copies.append(copy)
    for copy in copies:
        copy.wait()


def per_device(
    n_dp,
    n_expert,
    n_tensor,
    weight,
    factor_a,
    factor_b,
    moment_a,
    second_a,
    first_moment_factor_b,
    second_b,
    grad_a,
    grad_b,
    slot_of,
):
    ranks, cols_a = factor_a.shape[1:]
    cols_b = factor_b.shape[2]
    cols = cols_a + cols_b

    pieces = pl.pallas_call(
        functools.partial(pack_kernel, n_dp, ranks, cols_a),
        in_specs=[HBM, HBM],
        out_specs=[VMEM] * (n_dp - 1),
        out_shape=[pltpu.VMEM((ranks, cols), BF16)] * (n_dp - 1),
        scratch_shapes=[
            pltpu.VMEM((n_dp - 1, ranks, cols), F32),
            pltpu.SemaphoreType.DMA((n_dp - 1, 2)),
        ],
        compiler_params=PARAMS,
        name="pack",
    )(left(grad_a), left(grad_b))
    got = [held(swap(piece, "dp", n_dp, k)) for k, piece in enumerate(pieces, 1)]

    *state, order = pl.pallas_call(
        functools.partial(load_kernel, ranks, cols_a),
        in_specs=[HBM] * 9,
        out_specs=[VMEM] * 4 + [SMEM],
        out_shape=[pltpu.VMEM((ranks, cols), F32)] * 4 + [pltpu.SMEM((1,), jnp.int32)],
        scratch_shapes=[pltpu.SMEM(slot_of.shape, jnp.int32), pltpu.SemaphoreType.DMA((9,))],
        compiler_params=PARAMS,
        cost_estimate=estimate(4 * ranks * cols * 4),
        name="load",
    )(
        *map(
            left,
            (
                slot_of,
                grad_a,
                grad_b,
                factor_a,
                factor_b,
                moment_a,
                first_moment_factor_b,
                second_a,
                second_b,
            ),
        ),
    )
    state = [held(x) for x in state]

    send = pl.pallas_call(
        send_kernel,
        in_specs=[VMEM] * (3 + n_dp),
        out_specs=VMEM,
        out_shape=pltpu.VMEM((ranks, cols), BF16),
        compiler_params=PARAMS,
        name="send",
    )(*state, *got)

    def move(slots):
        def branch(send, state, got):
            mine = lax.ppermute(send, "expert", list(enumerate(slots)))
            new = pl.pallas_call(
                functools.partial(state_kernel, n_dp - 1, cols_a),
                in_specs=[VMEM] * (3 + n_dp),
                out_specs=[VMEM] * 6,
                out_shape=[
                    jax.ShapeDtypeStruct(factor_a.shape, F32),
                    jax.ShapeDtypeStruct(factor_b.shape, F32),
                ]
                * 3,
                compiler_params=PARAMS,
                cost_estimate=estimate(3 * ranks * cols * 4),
                name="state",
            )(*map(held, state), *map(held, got))
            return mine, new

        return branch

    if n_expert <= MOST_SWITCHED:
        orders = list(itertools.permutations(range(n_expert)))
        mine, new = lax.switch(order[0], [move(slots) for slots in orders], send, state, got)
    else:
        mine, new = move(range(n_expert))(send, state, got)
        here = lax.axis_index("expert")
        experts = jnp.arange(n_expert, dtype=jnp.int32)
        wanted = jnp.sum(jnp.where(slot_of == here, experts, 0)) ^ here
        for k in range(1, n_expert):
            mine = jnp.where(wanted == k, swap(send, "expert", n_expert, k), mine)
    new_a, new_b, new_moment_a, new_moment_b, new_second_a, new_second_b = new

    panel_shape = weight.shape[1:]
    parts = [swap(mine, "dp", n_dp, k) for k in range(n_dp - 1, 0, -1)]
    panel, mine = pl.pallas_call(
        panel_kernel,
        in_specs=[HBM] * 2,
        out_specs=[VMEM] * 2,
        out_shape=[pltpu.VMEM(panel_shape, BF16), pltpu.VMEM((ranks, cols), BF16)],
        scratch_shapes=[pltpu.SemaphoreType.DMA((2,))],
        compiler_params=PARAMS,
        cost_estimate=estimate(weight.size * 4),
        name="panel",
    )(left(weight), left(mine))
    parts.append(mine)
    rows_a, flipped, panel = pl.pallas_call(
        functools.partial(join_kernel, cols_a),
        in_specs=[VMEM] * (n_dp + 1),
        out_specs=[VMEM] * 3,
        out_shape=[
            pltpu.VMEM((ranks * n_dp, cols_a), BF16),
            pltpu.VMEM((cols_b, ranks * n_dp), BF16),
            pltpu.VMEM(panel_shape, BF16),
        ],
        input_output_aliases={n_dp: 2},
        compiler_params=PARAMS,
        name="join",
    )(*map(held, parts), held(panel))

    merged = None
    width = 256
    for k in range(n_tensor):
        block = held(rows_a if k == 0 else swap(rows_a, "tensor", n_tensor, k))
        operands = [held(panel), block, held(flipped)] + ([] if merged is None else [merged])
        merged = pl.pallas_call(
            functools.partial(merge_kernel, k, width),
            in_specs=[VMEM] * 3 + [HBM] * (len(operands) - 3),
            out_specs=HBM,
            out_shape=jax.ShapeDtypeStruct(weight.shape, BF16),
            scratch_shapes=[
                pltpu.VMEM((cols_a // width, panel_shape[0], width), BF16),
                pltpu.SemaphoreType.DMA((cols_a // width,)),
            ],
            input_output_aliases={} if merged is None else {3: 0},
            compiler_params=PARAMS,
            cost_estimate=estimate(
                panel_shape[0] * cols_a * 2, 2 * panel_shape[0] * cols_a * ranks * n_dp
            ),
            name=f"merge{k}",
        )(*operands)
    return (merged, new_a, new_b, new_moment_a, new_second_a, new_moment_b, new_second_b)


def solution(mesh):
    sizes = dict(mesh.shape)

    def body(*args):
        return per_device(sizes["dp"], sizes["expert"], sizes["tensor"], *args)

    state = P("expert", "dp", "tensor")
    grad = P("dp", "expert", None, "tensor")
    weight = P("expert", "tensor", None)
    in_specs = (weight,) + (state,) * 6 + (grad,) * 2 + (P(),)
    out_specs = (weight,) + (state,) * 6
    return jax.shard_map(body, mesh=mesh, in_specs=in_specs, out_specs=out_specs, check_vma=False)
```

```python
import functools
import itertools

import jax
import jax.numpy as jnp
from jax import lax
from jax.experimental import pallas as pl
from jax.experimental.pallas import tpu as pltpu
from jax.sharding import PartitionSpec as P

ADAM_STEP = 20


ADAPTER_SCALE = 2.0
BETA_ONE = 0.9
BETA_TWO = 0.95
LEARN_RATE = 0.08
STABILITY_TERM = 1e-08

MOST_SWITCHED = 4

F32 = jnp.float32
BF16 = jnp.bfloat16
VMEM = pl.BlockSpec(memory_space=pltpu.VMEM)
SMEM = pl.BlockSpec(memory_space=pltpu.SMEM)
HBM = pl.BlockSpec(memory_space=pltpu.HBM)
PARAMS = pltpu.CompilerParams(vmem_limit_bytes=16 * 1024 * 1024)


def adam_update(param, moment, second, grad):
    corr_one = 1.0 - BETA_ONE**ADAM_STEP
    corr_two = 1.0 - BETA_TWO**ADAM_STEP
    moment_new = BETA_ONE * moment + (1.0 - BETA_ONE) * grad
    second_new = BETA_TWO * second + (1.0 - BETA_TWO) * grad * grad
    param_new = param - LEARN_RATE * (moment_new / corr_one) / (
        jnp.sqrt(second_new / corr_two) + STABILITY_TERM
    )
    return (param_new, moment_new, second_new)


def swap(x, axis, n, k):
    return lax.ppermute(x, axis, [(i, i ^ k) for i in range(n)])


def held(x):
    return pltpu.with_memory_space_constraint(x, pltpu.VMEM)


def left(x):
    return pltpu.with_memory_space_constraint(x, pltpu.HBM)


def estimate(nbytes, flops=0):
    return pl.CostEstimate(flops=flops, bytes_accessed=nbytes, transcendentals=0)


def pack_kernel(n_dp, ranks, cols_a, grad_a, grad_b, *refs):
    outs, rows, sems = refs[: n_dp - 1], refs[n_dp - 1], refs[n_dp]
    me = lax.axis_index("dp")
    copies = []
    for k in range(1, n_dp):
        start = pl.multiple_of((me ^ k) * ranks, ranks)
        pair = (
            pltpu.make_async_copy(
                grad_a.at[0, 0, pl.ds(start, ranks), :],
                rows.at[k - 1, :, pl.ds(0, cols_a)],
                sems.at[k - 1, 0],
            ),
            pltpu.make_async_copy(
                grad_b.at[0, 0, pl.ds(start, ranks), :],
                rows.at[k - 1, :, pl.ds(cols_a, rows.shape[2] - cols_a)],
                sems.at[k - 1, 1],
            ),
        )
        for copy in pair:
            copy.start()
        copies.append(pair)
    for k, pair in enumerate(copies):
        for copy in pair:
            copy.wait()
        outs[k][...] = rows[k].astype(BF16)


def load_kernel(ranks, cols_a, slots_in, *refs):
    grad_a, grad_b, fa, fb, ma, mb, sa, sb, weight = refs[:9]
    grad, factor, moment, second, panel, order, slot_of, sems = refs[9:]
    me = lax.axis_index("dp")
    start = pl.multiple_of(me * ranks, ranks)
    first = pl.ds(0, cols_a)
    last = pl.ds(cols_a, grad.shape[1] - cols_a)
    pairs = [
        (grad_a.at[0, 0, pl.ds(start, ranks), :], grad.at[:, first]),
        (grad_b.at[0, 0, pl.ds(start, ranks), :], grad.at[:, last]),
        (fa.at[0], factor.at[:, first]),
        (fb.at[0], factor.at[:, last]),
        (ma.at[0], moment.at[:, first]),
        (mb.at[0], moment.at[:, last]),
        (sa.at[0], second.at[:, first]),
        (sb.at[0], second.at[:, last]),
        (weight.at[0], panel),
        (slots_in, slot_of),
    ]
    copies = [pltpu.make_async_copy(a, b, sems.at[i]) for i, (a, b) in enumerate(pairs)]
    for copy in copies:
        copy.start()
    copies.pop().wait()
    n = slot_of.shape[0]
    number = jnp.int32(0)
    for i in range(n - 1):
        smaller = jnp.int32(0)
        for j in range(i + 1, n):
            smaller += (slot_of[j] < slot_of[i]).astype(jnp.int32)
        number = number * (n - i) + smaller
    order[0] = number
    for copy in copies:
        copy.wait()


def keep_kernel(mine, mark, kept, sem):
    copy = pltpu.make_async_copy(mine, kept, sem)
    copy.start()
    copy.wait()


def send_kernel(*refs):
    grad, factor, moment, second = refs[:4]
    total = grad[...]
    for piece in refs[4:-1]:
        total = total + piece[...].astype(F32)
    refs[-1][...] = adam_update(factor[...], moment[...], second[...], total)[0].astype(BF16)


def state_kernel(n_got, cols_a, *refs):
    grad, factor, moment, second = refs[:4]
    outs = refs[4 + n_got : -1]
    refs[-1][...] = jnp.zeros_like(refs[-1])
    total = grad[...]
    for piece in refs[4 : 4 + n_got]:
        total = total + piece[...].astype(F32)
    for i, new in enumerate(adam_update(factor[...], moment[...], second[...], total)):
        outs[2 * i][0] = new[:, :cols_a]
        outs[2 * i + 1][0] = new[:, cols_a:]


def join_kernel(cols_a, *refs):
    parts = refs[:-4]
    rows_a, flipped = refs[-3:-1]
    ranks = parts[0].shape[0]
    for i, part in enumerate(parts):
        rows_a[pl.ds(i * ranks, ranks), :] = part[:, :cols_a]
    rows_b = jnp.concatenate([part[:, cols_a:].astype(F32) for part in parts], axis=0)
    flipped[...] = (rows_b * ADAPTER_SCALE).T.astype(BF16)


def merge_kernel(k, width, *refs):
    panel, rows_a, flipped = refs[:3]
    out, tiles, sems = refs[-3:]
    cols = rows_a.shape[1]
    base = (lax.axis_index("tensor") ^ k) * cols
    copies = []
    for step in range(cols // width):
        columns = pl.ds(pl.multiple_of(base + step * width, width), width)
        increment = jnp.dot(
            flipped[...], rows_a[:, step * width : (step + 1) * width], preferred_element_type=F32
        )
        tiles[step] = (panel[:, columns].astype(F32) + increment).astype(BF16)
        copy = pltpu.make_async_copy(tiles.at[step], out.at[0, :, columns], sems.at[step])
        copy.start()
        copies.append(copy)
    for copy in copies:
        copy.wait()


def per_device(
    n_dp,
    n_expert,
    n_tensor,
    weight,
    factor_a,
    factor_b,
    moment_a,
    second_a,
    first_moment_factor_b,
    second_b,
    grad_a,
    grad_b,
    slot_of,
):
    ranks, cols_a = factor_a.shape[1:]
    cols_b = factor_b.shape[2]
    cols = cols_a + cols_b

    pieces = pl.pallas_call(
        functools.partial(pack_kernel, n_dp, ranks, cols_a),
        in_specs=[HBM, HBM],
        out_specs=[VMEM] * (n_dp - 1),
        out_shape=[pltpu.VMEM((ranks, cols), BF16)] * (n_dp - 1),
        scratch_shapes=[
            pltpu.VMEM((n_dp - 1, ranks, cols), F32),
            pltpu.SemaphoreType.DMA((n_dp - 1, 2)),
        ],
        compiler_params=PARAMS,
        name="pack",
    )(left(grad_a), left(grad_b))
    got = [held(swap(piece, "dp", n_dp, k)) for k, piece in enumerate(pieces, 1)]

    panel_shape = weight.shape[1:]
    *state, panel, order = pl.pallas_call(
        functools.partial(load_kernel, ranks, cols_a),
        in_specs=[HBM] * 10,
        out_specs=[VMEM] * 5 + [SMEM],
        out_shape=[pltpu.VMEM((ranks, cols), F32)] * 4
        + [pltpu.VMEM(panel_shape, BF16), pltpu.SMEM((1,), jnp.int32)],
        scratch_shapes=[pltpu.SMEM(slot_of.shape, jnp.int32), pltpu.SemaphoreType.DMA((10,))],
        compiler_params=PARAMS,
        cost_estimate=estimate(weight.size * 2 + 4 * ranks * cols * 4),
        name="load",
    )(
        *map(
            left,
            (
                slot_of,
                grad_a,
                grad_b,
                factor_a,
                factor_b,
                moment_a,
                first_moment_factor_b,
                second_a,
                second_b,
                weight,
            ),
        ),
    )
    state = [held(x) for x in state]

    send = pl.pallas_call(
        send_kernel,
        in_specs=[VMEM] * (3 + n_dp),
        out_specs=VMEM,
        out_shape=pltpu.VMEM((ranks, cols), BF16),
        compiler_params=PARAMS,
        name="send",
    )(*state, *got)

    def move(slots):
        return lambda x: lax.ppermute(x, "expert", list(enumerate(slots)))

    if n_expert <= MOST_SWITCHED:
        orders = list(itertools.permutations(range(n_expert)))
        mine = lax.switch(order[0], [move(slots) for slots in orders], send)
    else:
        mine = send
        here = lax.axis_index("expert")
        experts = jnp.arange(n_expert, dtype=jnp.int32)
        wanted = jnp.sum(jnp.where(slot_of == here, experts, 0)) ^ here
        for k in range(1, n_expert):
            mine = jnp.where(wanted == k, swap(send, "expert", n_expert, k), mine)

    parts = [swap(mine, "dp", n_dp, k) for k in range(1, n_dp)]
    *new, mark = pl.pallas_call(
        functools.partial(state_kernel, n_dp - 1, cols_a),
        in_specs=[VMEM] * (3 + n_dp),
        out_specs=[VMEM] * 7,
        out_shape=[
            jax.ShapeDtypeStruct(factor_a.shape, F32),
            jax.ShapeDtypeStruct(factor_b.shape, F32),
        ]
        * 3
        + [pltpu.VMEM((8, 128), F32)],
        compiler_params=PARAMS,
        cost_estimate=estimate(3 * ranks * cols * 4),
        name="state",
    )(*state, *got)
    new_a, new_b, new_moment_a, new_moment_b, new_second_a, new_second_b = new
    mine = pl.pallas_call(
        keep_kernel,
        in_specs=[HBM, VMEM],
        out_specs=VMEM,
        out_shape=pltpu.VMEM((ranks, cols), BF16),
        scratch_shapes=[pltpu.SemaphoreType.DMA],
        compiler_params=PARAMS,
        cost_estimate=estimate(ranks * cols * 4),
        name="keep",
    )(left(mine), held(mark))
    parts = [mine] + parts
    rows_a, flipped, panel = pl.pallas_call(
        functools.partial(join_kernel, cols_a),
        in_specs=[VMEM] * (n_dp + 1),
        out_specs=[VMEM] * 3,
        out_shape=[
            pltpu.VMEM((ranks * n_dp, cols_a), BF16),
            pltpu.VMEM((cols_b, ranks * n_dp), BF16),
            pltpu.VMEM(panel_shape, BF16),
        ],
        input_output_aliases={n_dp: 2},
        compiler_params=PARAMS,
        name="join",
    )(*map(held, parts), held(panel))

    merged = None
    width = 512
    for k in range(n_tensor):
        block = held(rows_a if k == 0 else swap(rows_a, "tensor", n_tensor, k))
        operands = [held(panel), block, held(flipped)] + ([] if merged is None else [merged])
        merged = pl.pallas_call(
            functools.partial(merge_kernel, k, width),
            in_specs=[VMEM] * 3 + [HBM] * (len(operands) - 3),
            out_specs=HBM,
            out_shape=jax.ShapeDtypeStruct(weight.shape, BF16),
            scratch_shapes=[
                pltpu.VMEM((cols_a // width, panel_shape[0], width), BF16),
                pltpu.SemaphoreType.DMA((cols_a // width,)),
            ],
            input_output_aliases={} if merged is None else {3: 0},
            compiler_params=PARAMS,
            cost_estimate=estimate(
                panel_shape[0] * cols_a * 2, 2 * panel_shape[0] * cols_a * ranks * n_dp
            ),
            name=f"merge{k}",
        )(*operands)
    return (merged, new_a, new_b, new_moment_a, new_second_a, new_moment_b, new_second_b)


def solution(mesh):
    sizes = dict(mesh.shape)

    def body(*args):
        return per_device(sizes["dp"], sizes["expert"], sizes["tensor"], *args)

    state = P("expert", "dp", "tensor")
    grad = P("dp", "expert", None, "tensor")
    weight = P("expert", "tensor", None)
    in_specs = (weight,) + (state,) * 6 + (grad,) * 2 + (P(),)
    out_specs = (weight,) + (state,) * 6
    return jax.shard_map(body, mesh=mesh, in_specs=in_specs, out_specs=out_specs, check_vma=False)
```

```python
import functools
import itertools

import jax
import jax.numpy as jnp
from jax import lax
from jax.experimental import pallas as pl
from jax.experimental.pallas import tpu as pltpu
from jax.sharding import PartitionSpec as P

ADAM_STEP = 20


ADAPTER_SCALE = 2.0
BETA_ONE = 0.9
BETA_TWO = 0.95
LEARN_RATE = 0.08
STABILITY_TERM = 1e-08

MOST_SWITCHED = 4

F32 = jnp.float32
BF16 = jnp.bfloat16
VMEM = pl.BlockSpec(memory_space=pltpu.VMEM)
SMEM = pl.BlockSpec(memory_space=pltpu.SMEM)
HBM = pl.BlockSpec(memory_space=pltpu.HBM)
PARAMS = pltpu.CompilerParams(vmem_limit_bytes=16 * 1024 * 1024)


def adam_update(param, moment, second, grad):
    corr_one = 1.0 - BETA_ONE**ADAM_STEP
    corr_two = 1.0 - BETA_TWO**ADAM_STEP
    moment_new = BETA_ONE * moment + (1.0 - BETA_ONE) * grad
    second_new = BETA_TWO * second + (1.0 - BETA_TWO) * grad * grad
    param_new = param - LEARN_RATE * (moment_new / corr_one) / (
        jnp.sqrt(second_new / corr_two) + STABILITY_TERM
    )
    return (param_new, moment_new, second_new)


def swap(x, axis, n, k):
    return lax.ppermute(x, axis, [(i, i ^ k) for i in range(n)])


def held(x):
    return pltpu.with_memory_space_constraint(x, pltpu.VMEM)


def left(x):
    return pltpu.with_memory_space_constraint(x, pltpu.HBM)


def estimate(nbytes, flops=0):
    return pl.CostEstimate(flops=flops, bytes_accessed=nbytes, transcendentals=0)


def pack_kernel(n_dp, ranks, cols_a, grad_a, grad_b, *refs):
    outs, rows, sems = refs[: n_dp - 1], refs[n_dp - 1], refs[n_dp]
    me = lax.axis_index("dp")
    copies = []
    for k in range(1, n_dp):
        start = pl.multiple_of((me ^ k) * ranks, ranks)
        pair = (
            pltpu.make_async_copy(
                grad_a.at[0, 0, pl.ds(start, ranks), :],
                rows.at[k - 1, :, pl.ds(0, cols_a)],
                sems.at[k - 1, 0],
            ),
            pltpu.make_async_copy(
                grad_b.at[0, 0, pl.ds(start, ranks), :],
                rows.at[k - 1, :, pl.ds(cols_a, rows.shape[2] - cols_a)],
                sems.at[k - 1, 1],
            ),
        )
        for copy in pair:
            copy.start()
        copies.append(pair)
    for k, pair in enumerate(copies):
        for copy in pair:
            copy.wait()
        outs[k][...] = rows[k].astype(BF16)


def load_kernel(ranks, cols_a, slots_in, *refs):
    grad_a, grad_b, fa, fb, ma, mb, sa, sb = refs[:8]
    grad, factor, moment, second, order, slot_of, sems = refs[8:]
    me = lax.axis_index("dp")
    start = pl.multiple_of(me * ranks, ranks)
    first = pl.ds(0, cols_a)
    last = pl.ds(cols_a, grad.shape[1] - cols_a)
    pairs = [
        (grad_a.at[0, 0, pl.ds(start, ranks), :], grad.at[:, first]),
        (grad_b.at[0, 0, pl.ds(start, ranks), :], grad.at[:, last]),
        (fa.at[0], factor.at[:, first]),
        (fb.at[0], factor.at[:, last]),
        (ma.at[0], moment.at[:, first]),
        (mb.at[0], moment.at[:, last]),
        (sa.at[0], second.at[:, first]),
        (sb.at[0], second.at[:, last]),
        (slots_in, slot_of),
    ]
    copies = [pltpu.make_async_copy(a, b, sems.at[i]) for i, (a, b) in enumerate(pairs)]
    for copy in copies:
        copy.start()
    copies.pop().wait()
    n = slot_of.shape[0]
    number = jnp.int32(0)
    for i in range(n - 1):
        smaller = jnp.int32(0)
        for j in range(i + 1, n):
            smaller += (slot_of[j] < slot_of[i]).astype(jnp.int32)
        number = number * (n - i) + smaller
    order[0] = number
    for copy in copies:
        copy.wait()


def panel_kernel(weight, mine, panel, kept, sems):
    copies = [
        pltpu.make_async_copy(weight.at[0], panel, sems.at[0]),
        pltpu.make_async_copy(mine, kept, sems.at[1]),
    ]
    for copy in copies:
        copy.start()
    for copy in copies:
        copy.wait()


def send_kernel(*refs):
    grad, factor, moment, second = refs[:4]
    total = grad[...]
    for piece in refs[4:-1]:
        total = total + piece[...].astype(F32)
    refs[-1][...] = adam_update(factor[...], moment[...], second[...], total)[0].astype(BF16)


def state_kernel(n_got, cols_a, *refs):
    ins = refs[: 4 + n_got]
    outs = refs[4 + n_got :]
    width = 128

    def some_columns(start, outs, at):
        here = pl.ds(pl.multiple_of(start, width), width)
        there = pl.ds(pl.multiple_of(at, width), width)
        grad, factor, moment, second = (ref[:, here] for ref in ins[:4])
        for piece in ins[4:]:
            grad = grad + piece[:, here].astype(F32)
        for out, new in zip(outs, adam_update(factor, moment, second, grad)):
            out[0, :, there] = new

    @pl.loop(0, cols_a // width)
    def _(i):
        some_columns(i * width, outs[::2], i * width)

    @pl.loop(0, (ins[0].shape[1] - cols_a) // width)
    def _(i):
        some_columns(cols_a + i * width, outs[1::2], i * width)


def join_kernel(cols_a, *refs):
    parts = refs[:-4]
    rows_a, flipped = refs[-3:-1]
    ranks = parts[0].shape[0]
    for i, part in enumerate(parts):
        rows_a[pl.ds(i * ranks, ranks), :] = part[:, :cols_a]
    rows_b = jnp.concatenate([part[:, cols_a:].astype(F32) for part in parts], axis=0)
    flipped[...] = (rows_b * ADAPTER_SCALE).T.astype(BF16)


def merge_kernel(k, width, *refs):
    panel, rows_a, flipped = refs[:3]
    out, tiles, sems = refs[-3:]
    cols = rows_a.shape[1]
    base = (lax.axis_index("tensor") ^ k) * cols
    copies = []
    for step in range(cols // width):
        columns = pl.ds(pl.multiple_of(base + step * width, width), width)
        increment = jnp.dot(
            flipped[...], rows_a[:, step * width : (step + 1) * width], preferred_element_type=F32
        )
        tiles[step] = (panel[:, columns].astype(F32) + increment).astype(BF16)
        copy = pltpu.make_async_copy(tiles.at[step], out.at[0, :, columns], sems.at[step])
        copy.start()
        copies.append(copy)
    for copy in copies:
        copy.wait()


def per_device(
    n_dp,
    n_expert,
    n_tensor,
    weight,
    factor_a,
    factor_b,
    moment_a,
    second_a,
    first_moment_factor_b,
    second_b,
    grad_a,
    grad_b,
    slot_of,
):
    ranks, cols_a = factor_a.shape[1:]
    cols_b = factor_b.shape[2]
    cols = cols_a + cols_b

    pieces = pl.pallas_call(
        functools.partial(pack_kernel, n_dp, ranks, cols_a),
        in_specs=[HBM, HBM],
        out_specs=[VMEM] * (n_dp - 1),
        out_shape=[pltpu.VMEM((ranks, cols), BF16)] * (n_dp - 1),
        scratch_shapes=[
            pltpu.VMEM((n_dp - 1, ranks, cols), F32),
            pltpu.SemaphoreType.DMA((n_dp - 1, 2)),
        ],
        compiler_params=PARAMS,
        name="pack",
    )(left(grad_a), left(grad_b))
    got = [held(swap(pieces[k - 1], "dp", n_dp, k)) for k in range(n_dp - 1, 0, -1)]

    *state, order = pl.pallas_call(
        functools.partial(load_kernel, ranks, cols_a),
        in_specs=[HBM] * 9,
        out_specs=[VMEM] * 4 + [SMEM],
        out_shape=[pltpu.VMEM((ranks, cols), F32)] * 4 + [pltpu.SMEM((1,), jnp.int32)],
        scratch_shapes=[pltpu.SMEM(slot_of.shape, jnp.int32), pltpu.SemaphoreType.DMA((9,))],
        compiler_params=PARAMS,
        cost_estimate=estimate(4 * ranks * cols * 4),
        name="load",
    )(
        *map(
            left,
            (
                slot_of,
                grad_a,
                grad_b,
                factor_a,
                factor_b,
                moment_a,
                first_moment_factor_b,
                second_a,
                second_b,
            ),
        ),
    )
    state = [held(x) for x in state]

    send = pl.pallas_call(
        send_kernel,
        in_specs=[VMEM] * (3 + n_dp),
        out_specs=VMEM,
        out_shape=pltpu.VMEM((ranks, cols), BF16),
        compiler_params=PARAMS,
        name="send",
    )(*state, *got)

    def move(slots):
        def branch(send, state, got):
            mine = lax.ppermute(send, "expert", list(enumerate(slots)))
            new = pl.pallas_call(
                functools.partial(state_kernel, n_dp - 1, cols_a),
                in_specs=[VMEM] * (3 + n_dp),
                out_specs=[VMEM] * 6,
                out_shape=[
                    jax.ShapeDtypeStruct(factor_a.shape, F32),
                    jax.ShapeDtypeStruct(factor_b.shape, F32),
                ]
                * 3,
                compiler_params=PARAMS,
                cost_estimate=estimate(3 * ranks * cols * 4),
                name="state",
            )(*map(held, state), *map(held, got))
            return mine, new

        return branch

    if n_expert <= MOST_SWITCHED:
        orders = list(itertools.permutations(range(n_expert)))
        mine, new = lax.switch(order[0], [move(slots) for slots in orders], send, state, got)
    else:
        mine, new = move(range(n_expert))(send, state, got)
        here = lax.axis_index("expert")
        experts = jnp.arange(n_expert, dtype=jnp.int32)
        wanted = jnp.sum(jnp.where(slot_of == here, experts, 0)) ^ here
        for k in range(1, n_expert):
            mine = jnp.where(wanted == k, swap(send, "expert", n_expert, k), mine)
    new_a, new_b, new_moment_a, new_moment_b, new_second_a, new_second_b = new

    panel_shape = weight.shape[1:]
    parts = [swap(mine, "dp", n_dp, k) for k in range(1, n_dp)]
    panel, mine = pl.pallas_call(
        panel_kernel,
        in_specs=[HBM] * 2,
        out_specs=[VMEM] * 2,
        out_shape=[pltpu.VMEM(panel_shape, BF16), pltpu.VMEM((ranks, cols), BF16)],
        scratch_shapes=[pltpu.SemaphoreType.DMA((2,))],
        compiler_params=PARAMS,
        cost_estimate=estimate(weight.size * 4),
        name="panel",
    )(left(weight), left(mine))
    parts = [mine] + parts
    rows_a, flipped, panel = pl.pallas_call(
        functools.partial(join_kernel, cols_a),
        in_specs=[VMEM] * (n_dp + 1),
        out_specs=[VMEM] * 3,
        out_shape=[
            pltpu.VMEM((ranks * n_dp, cols_a), BF16),
            pltpu.VMEM((cols_b, ranks * n_dp), BF16),
            pltpu.VMEM(panel_shape, BF16),
        ],
        input_output_aliases={n_dp: 2},
        compiler_params=PARAMS,
        name="join",
    )(*map(held, parts), held(panel))

    merged = None
    width = 512
    for k in range(n_tensor):
        block = held(rows_a if k == 0 else swap(rows_a, "tensor", n_tensor, k))
        operands = [held(panel), block, held(flipped)] + ([] if merged is None else [merged])
        merged = pl.pallas_call(
            functools.partial(merge_kernel, k, width),
            in_specs=[VMEM] * 3 + [HBM] * (len(operands) - 3),
            out_specs=HBM,
            out_shape=jax.ShapeDtypeStruct(weight.shape, BF16),
            scratch_shapes=[
                pltpu.VMEM((cols_a // width, panel_shape[0], width), BF16),
                pltpu.SemaphoreType.DMA((cols_a // width,)),
            ],
            input_output_aliases={} if merged is None else {3: 0},
            compiler_params=PARAMS,
            cost_estimate=estimate(
                panel_shape[0] * cols_a * 2, 2 * panel_shape[0] * cols_a * ranks * n_dp
            ),
            name=f"merge{k}",
        )(*operands)
    return (merged, new_a, new_b, new_moment_a, new_second_a, new_moment_b, new_second_b)


def solution(mesh):
    sizes = dict(mesh.shape)

    def body(*args):
        return per_device(sizes["dp"], sizes["expert"], sizes["tensor"], *args)

    state = P("expert", "dp", "tensor")
    grad = P("dp", "expert", None, "tensor")
    weight = P("expert", "tensor", None)
    in_specs = (weight,) + (state,) * 6 + (grad,) * 2 + (P(),)
    out_specs = (weight,) + (state,) * 6
    return jax.shard_map(body, mesh=mesh, in_specs=in_specs, out_specs=out_specs, check_vma=False)
```

```python
import functools
import itertools

import jax
import jax.numpy as jnp
from jax import lax
from jax.experimental import pallas as pl
from jax.experimental.pallas import tpu as pltpu
from jax.sharding import PartitionSpec as P

ADAM_STEP = 20


ADAPTER_SCALE = 2.0
BETA_ONE = 0.9
BETA_TWO = 0.95
LEARN_RATE = 0.08
STABILITY_TERM = 1e-08

MOST_SWITCHED = 4

F32 = jnp.float32
BF16 = jnp.bfloat16
VMEM = pl.BlockSpec(memory_space=pltpu.VMEM)
SMEM = pl.BlockSpec(memory_space=pltpu.SMEM)
HBM = pl.BlockSpec(memory_space=pltpu.HBM)
PARAMS = pltpu.CompilerParams(vmem_limit_bytes=16 * 1024 * 1024)


def adam_update(param, moment, second, grad):
    corr_one = 1.0 - BETA_ONE**ADAM_STEP
    corr_two = 1.0 - BETA_TWO**ADAM_STEP
    moment_new = BETA_ONE * moment + (1.0 - BETA_ONE) * grad
    second_new = BETA_TWO * second + (1.0 - BETA_TWO) * grad * grad
    param_new = param - LEARN_RATE * (moment_new / corr_one) / (
        jnp.sqrt(second_new / corr_two) + STABILITY_TERM
    )
    return (param_new, moment_new, second_new)


def swap(x, axis, n, k):
    return lax.ppermute(x, axis, [(i, i ^ k) for i in range(n)])


def held(x):
    return pltpu.with_memory_space_constraint(x, pltpu.VMEM)


def left(x):
    return pltpu.with_memory_space_constraint(x, pltpu.HBM)


def estimate(nbytes, flops=0):
    return pl.CostEstimate(flops=flops, bytes_accessed=nbytes, transcendentals=0)


def pack_kernel(n_dp, ranks, cols_a, grad_a, grad_b, *refs):
    outs, rows, sems = refs[: n_dp - 1], refs[n_dp - 1], refs[n_dp]
    me = lax.axis_index("dp")
    copies = []
    for k in range(1, n_dp):
        start = pl.multiple_of((me ^ k) * ranks, ranks)
        pair = (
            pltpu.make_async_copy(
                grad_a.at[0, 0, pl.ds(start, ranks), :],
                rows.at[k - 1, :, pl.ds(0, cols_a)],
                sems.at[k - 1, 0],
            ),
            pltpu.make_async_copy(
                grad_b.at[0, 0, pl.ds(start, ranks), :],
                rows.at[k - 1, :, pl.ds(cols_a, rows.shape[2] - cols_a)],
                sems.at[k - 1, 1],
            ),
        )
        for copy in pair:
            copy.start()
        copies.append(pair)
    for k, pair in enumerate(copies):
        for copy in pair:
            copy.wait()
        outs[k][...] = rows[k].astype(BF16)


def load_kernel(ranks, cols_a, slots_in, *refs):
    grad_a, grad_b, fa, fb, ma, mb, sa, sb = refs[:8]
    grad, factor, moment, second, order, slot_of, sems = refs[8:]
    me = lax.axis_index("dp")
    start = pl.multiple_of(me * ranks, ranks)
    first = pl.ds(0, cols_a)
    last = pl.ds(cols_a, grad.shape[1] - cols_a)
    pairs = [
        (grad_a.at[0, 0, pl.ds(start, ranks), :], grad.at[:, first]),
        (grad_b.at[0, 0, pl.ds(start, ranks), :], grad.at[:, last]),
        (fa.at[0], factor.at[:, first]),
        (fb.at[0], factor.at[:, last]),
        (ma.at[0], moment.at[:, first]),
        (mb.at[0], moment.at[:, last]),
        (sa.at[0], second.at[:, first]),
        (sb.at[0], second.at[:, last]),
        (slots_in, slot_of),
    ]
    copies = [pltpu.make_async_copy(a, b, sems.at[i]) for i, (a, b) in enumerate(pairs)]
    for copy in copies:
        copy.start()
    copies.pop().wait()
    n = slot_of.shape[0]
    number = jnp.int32(0)
    for i in range(n - 1):
        smaller = jnp.int32(0)
        for j in range(i + 1, n):
            smaller += (slot_of[j] < slot_of[i]).astype(jnp.int32)
        number = number * (n - i) + smaller
    order[0] = number
    for copy in copies:
        copy.wait()


def panel_kernel(weight, panel, sem):
    copy = pltpu.make_async_copy(weight.at[0], panel, sem)
    copy.start()
    copy.wait()


def keep_kernel(piece, kept):
    kept[...] = piece[...]


def send_kernel(*refs):
    grad, factor, moment, second = refs[:4]
    total = grad[...]
    for piece in refs[4:-1]:
        total = total + piece[...].astype(F32)
    refs[-1][...] = adam_update(factor[...], moment[...], second[...], total)[0].astype(BF16)


def state_kernel(n_got, cols_a, *refs):
    grad, factor, moment, second = refs[:4]
    outs = refs[4 + n_got : -1]
    refs[-1][...] = jnp.zeros_like(refs[-1])
    total = grad[...]
    for piece in refs[4 : 4 + n_got]:
        total = total + piece[...].astype(F32)
    for i, new in enumerate(adam_update(factor[...], moment[...], second[...], total)):
        outs[2 * i][0] = new[:, :cols_a]
        outs[2 * i + 1][0] = new[:, cols_a:]


def join_kernel(cols_a, *refs):
    parts = refs[:-5]
    rows_a, flipped = refs[-3:-1]
    ranks = parts[0].shape[0]
    for i, part in enumerate(parts):
        rows_a[pl.ds(i * ranks, ranks), :] = part[:, :cols_a]
    rows_b = jnp.concatenate([part[:, cols_a:].astype(F32) for part in parts], axis=0)
    flipped[...] = (rows_b * ADAPTER_SCALE).T.astype(BF16)


def merge_kernel(k, width, *refs):
    panel, rows_a, flipped = refs[:3]
    out, tiles, sems = refs[-3:]
    cols = rows_a.shape[1]
    base = (lax.axis_index("tensor") ^ k) * cols
    copies = []
    for step in range(cols // width):
        columns = pl.ds(pl.multiple_of(base + step * width, width), width)
        increment = jnp.dot(
            flipped[...], rows_a[:, step * width : (step + 1) * width], preferred_element_type=F32
        )
        tiles[step] = (panel[:, columns].astype(F32) + increment).astype(BF16)
        copy = pltpu.make_async_copy(tiles.at[step], out.at[0, :, columns], sems.at[step])
        copy.start()
        copies.append(copy)
    for copy in copies:
        copy.wait()


def per_device(
    n_dp,
    n_expert,
    n_tensor,
    weight,
    factor_a,
    factor_b,
    moment_a,
    second_a,
    first_moment_factor_b,
    second_b,
    grad_a,
    grad_b,
    slot_of,
):
    ranks, cols_a = factor_a.shape[1:]
    cols_b = factor_b.shape[2]
    cols = cols_a + cols_b

    pieces = pl.pallas_call(
        functools.partial(pack_kernel, n_dp, ranks, cols_a),
        in_specs=[HBM, HBM],
        out_specs=[VMEM] * (n_dp - 1),
        out_shape=[pltpu.VMEM((ranks, cols), BF16)] * (n_dp - 1),
        scratch_shapes=[
            pltpu.VMEM((n_dp - 1, ranks, cols), F32),
            pltpu.SemaphoreType.DMA((n_dp - 1, 2)),
        ],
        compiler_params=PARAMS,
        name="pack",
    )(left(grad_a), left(grad_b))
    got = [held(swap(pieces[k - 1], "dp", n_dp, k)) for k in range(n_dp - 1, 0, -1)]

    *state, order = pl.pallas_call(
        functools.partial(load_kernel, ranks, cols_a),
        in_specs=[HBM] * 9,
        out_specs=[VMEM] * 4 + [SMEM],
        out_shape=[pltpu.VMEM((ranks, cols), F32)] * 4 + [pltpu.SMEM((1,), jnp.int32)],
        scratch_shapes=[pltpu.SMEM(slot_of.shape, jnp.int32), pltpu.SemaphoreType.DMA((9,))],
        compiler_params=PARAMS,
        cost_estimate=estimate(4 * ranks * cols * 4),
        name="load",
    )(
        *map(
            left,
            (
                slot_of,
                grad_a,
                grad_b,
                factor_a,
                factor_b,
                moment_a,
                first_moment_factor_b,
                second_a,
                second_b,
            ),
        ),
    )
    state = [held(x) for x in state]

    send = pl.pallas_call(
        send_kernel,
        in_specs=[VMEM] * (3 + n_dp),
        out_specs=VMEM,
        out_shape=pltpu.VMEM((ranks, cols), BF16),
        compiler_params=PARAMS,
        name="send",
    )(*state, *got)

    def move(slots):
        def branch(send):
            return pl.pallas_call(
                keep_kernel,
                in_specs=[VMEM],
                out_specs=VMEM,
                out_shape=pltpu.VMEM((ranks, cols), BF16),
                compiler_params=PARAMS,
                name="keep",
            )(held(lax.ppermute(send, "expert", list(enumerate(slots)))))

        return branch

    if n_expert <= MOST_SWITCHED:
        orders = itertools.permutations(range(n_expert))
        mine = lax.switch(order[0], [move(slots) for slots in orders], send)
        mine = jnp.where(order[0] >= 0, mine, jnp.zeros_like(mine))
    else:
        mine = send
        here = lax.axis_index("expert")
        experts = jnp.arange(n_expert, dtype=jnp.int32)
        wanted = jnp.sum(jnp.where(slot_of == here, experts, 0)) ^ here
        for k in range(1, n_expert):
            mine = jnp.where(wanted == k, swap(send, "expert", n_expert, k), mine)

    parts = [mine] + [swap(mine, "dp", n_dp, k) for k in range(1, n_dp)]
    panel_shape = weight.shape[1:]
    panel = pl.pallas_call(
        panel_kernel,
        in_specs=[HBM],
        out_specs=VMEM,
        out_shape=pltpu.VMEM(panel_shape, BF16),
        scratch_shapes=[pltpu.SemaphoreType.DMA],
        compiler_params=PARAMS,
        cost_estimate=estimate(weight.size * 4),
        name="panel",
    )(left(weight))
    *new, mark = pl.pallas_call(
        functools.partial(state_kernel, n_dp - 1, cols_a),
        in_specs=[VMEM] * (3 + n_dp),
        out_specs=[VMEM] * 7,
        out_shape=[
            jax.ShapeDtypeStruct(factor_a.shape, F32),
            jax.ShapeDtypeStruct(factor_b.shape, F32),
        ]
        * 3
        + [pltpu.VMEM((8, 128), F32)],
        compiler_params=PARAMS,
        cost_estimate=estimate(3 * ranks * cols * 4),
        name="state",
    )(*state, *got)
    new_a, new_b, new_moment_a, new_moment_b, new_second_a, new_second_b = new
    rows_a, flipped, panel = pl.pallas_call(
        functools.partial(join_kernel, cols_a),
        in_specs=[VMEM] * (n_dp + 2),
        out_specs=[VMEM] * 3,
        out_shape=[
            pltpu.VMEM((ranks * n_dp, cols_a), BF16),
            pltpu.VMEM((cols_b, ranks * n_dp), BF16),
            pltpu.VMEM(panel_shape, BF16),
        ],
        input_output_aliases={n_dp: 2},
        compiler_params=PARAMS,
        name="join",
    )(*map(held, parts), held(panel), held(mark))

    merged = None
    width = 512
    for k in range(n_tensor):
        block = held(rows_a if k == 0 else swap(rows_a, "tensor", n_tensor, k))
        operands = [held(panel), block, held(flipped)] + ([] if merged is None else [merged])
        merged = pl.pallas_call(
            functools.partial(merge_kernel, k, width),
            in_specs=[VMEM] * 3 + [HBM] * (len(operands) - 3),
            out_specs=HBM,
            out_shape=jax.ShapeDtypeStruct(weight.shape, BF16),
            scratch_shapes=[
                pltpu.VMEM((cols_a // width, panel_shape[0], width), BF16),
                pltpu.SemaphoreType.DMA((cols_a // width,)),
            ],
            input_output_aliases={} if merged is None else {3: 0},
            compiler_params=PARAMS,
            cost_estimate=estimate(
                panel_shape[0] * cols_a * 2, 2 * panel_shape[0] * cols_a * ranks * n_dp
            ),
            name=f"merge{k}",
        )(*operands)
    return (merged, new_a, new_b, new_moment_a, new_second_a, new_moment_b, new_second_b)


def solution(mesh):
    sizes = dict(mesh.shape)

    def body(*args):
        return per_device(sizes["dp"], sizes["expert"], sizes["tensor"], *args)

    state = P("expert", "dp", "tensor")
    grad = P("dp", "expert", None, "tensor")
    weight = P("expert", "tensor", None)
    in_specs = (weight,) + (state,) * 6 + (grad,) * 2 + (P(),)
    out_specs = (weight,) + (state,) * 6
    return jax.shard_map(body, mesh=mesh, in_specs=in_specs, out_specs=out_specs, check_vma=False)
```

```python
import functools
import itertools

import jax
import jax.numpy as jnp
from jax import lax
from jax.experimental import pallas as pl
from jax.experimental.pallas import tpu as pltpu
from jax.sharding import PartitionSpec as P

ADAM_STEP = 20


ADAPTER_SCALE = 2.0
BETA_ONE = 0.9
BETA_TWO = 0.95
LEARN_RATE = 0.08
STABILITY_TERM = 1e-08

MOST_SWITCHED = 4

F32 = jnp.float32
BF16 = jnp.bfloat16
VMEM = pl.BlockSpec(memory_space=pltpu.VMEM)
SMEM = pl.BlockSpec(memory_space=pltpu.SMEM)
HBM = pl.BlockSpec(memory_space=pltpu.HBM)
PARAMS = pltpu.CompilerParams(vmem_limit_bytes=16 * 1024 * 1024)


def adam_update(param, moment, second, grad):
    corr_one = 1.0 - BETA_ONE**ADAM_STEP
    corr_two = 1.0 - BETA_TWO**ADAM_STEP
    moment_new = BETA_ONE * moment + (1.0 - BETA_ONE) * grad
    second_new = BETA_TWO * second + (1.0 - BETA_TWO) * grad * grad
    param_new = param - LEARN_RATE * (moment_new / corr_one) / (
        jnp.sqrt(second_new / corr_two) + STABILITY_TERM
    )
    return (param_new, moment_new, second_new)


def swap(x, axis, n, k):
    return lax.ppermute(x, axis, [(i, i ^ k) for i in range(n)])


def held(x):
    return pltpu.with_memory_space_constraint(x, pltpu.VMEM)


def left(x):
    return pltpu.with_memory_space_constraint(x, pltpu.HBM)


def estimate(nbytes, flops=0):
    return pl.CostEstimate(flops=flops, bytes_accessed=nbytes, transcendentals=0)


def pack_kernel(n_dp, ranks, cols_a, grad_a, grad_b, *refs):
    outs, rows, sems = refs[: n_dp - 1], refs[n_dp - 1], refs[n_dp]
    me = lax.axis_index("dp")
    copies = []
    for k in range(1, n_dp):
        start = pl.multiple_of((me ^ k) * ranks, ranks)
        pair = (
            pltpu.make_async_copy(
                grad_a.at[0, 0, pl.ds(start, ranks), :],
                rows.at[k - 1, :, pl.ds(0, cols_a)],
                sems.at[k - 1, 0],
            ),
            pltpu.make_async_copy(
                grad_b.at[0, 0, pl.ds(start, ranks), :],
                rows.at[k - 1, :, pl.ds(cols_a, rows.shape[2] - cols_a)],
                sems.at[k - 1, 1],
            ),
        )
        for copy in pair:
            copy.start()
        copies.append(pair)
    for k, pair in enumerate(copies):
        for copy in pair:
            copy.wait()
        outs[k][...] = rows[k].astype(BF16)


def load_kernel(ranks, cols_a, slots_in, *refs):
    grad_a, grad_b, fa, fb, ma, mb, sa, sb = refs[:8]
    grad, factor, moment, second, order, slot_of, sems = refs[8:]
    me = lax.axis_index("dp")
    start = pl.multiple_of(me * ranks, ranks)
    first = pl.ds(0, cols_a)
    last = pl.ds(cols_a, grad.shape[1] - cols_a)
    pairs = [
        (grad_a.at[0, 0, pl.ds(start, ranks), :], grad.at[:, first]),
        (grad_b.at[0, 0, pl.ds(start, ranks), :], grad.at[:, last]),
        (fa.at[0], factor.at[:, first]),
        (fb.at[0], factor.at[:, last]),
        (ma.at[0], moment.at[:, first]),
        (mb.at[0], moment.at[:, last]),
        (sa.at[0], second.at[:, first]),
        (sb.at[0], second.at[:, last]),
        (slots_in, slot_of),
    ]
    copies = [pltpu.make_async_copy(a, b, sems.at[i]) for i, (a, b) in enumerate(pairs)]
    for copy in copies:
        copy.start()
    copies.pop().wait()
    n = slot_of.shape[0]
    number = jnp.int32(0)
    for i in range(n - 1):
        smaller = jnp.int32(0)
        for j in range(i + 1, n):
            smaller += (slot_of[j] < slot_of[i]).astype(jnp.int32)
        number = number * (n - i) + smaller
    order[0] = number
    for copy in copies:
        copy.wait()


def panel_kernel(weight, panel, sem):
    copy = pltpu.make_async_copy(weight.at[0], panel, sem)
    copy.start()
    copy.wait()


def keep_kernel(piece, kept):
    kept[...] = piece[...]


def send_kernel(*refs):
    grad, factor, moment, second = refs[:4]
    total = grad[...]
    for piece in refs[4:-1]:
        total = total + piece[...].astype(F32)
    refs[-1][...] = adam_update(factor[...], moment[...], second[...], total)[0].astype(BF16)


def state_kernel(n_got, cols_a, *refs):
    ins = refs[: 4 + n_got]
    outs = refs[4 + n_got :]
    cols_b = ins[0].shape[1] - cols_a
    width = 256 if cols_a % 256 == 0 and cols_b % 256 == 0 else 128

    def some_columns(start, outs, at):
        here = pl.ds(pl.multiple_of(start, width), width)
        there = pl.ds(pl.multiple_of(at, width), width)
        grad, factor, moment, second = (ref[:, here] for ref in ins[:4])
        for piece in ins[4:]:
            grad = grad + piece[:, here].astype(F32)
        for out, new in zip(outs, adam_update(factor, moment, second, grad)):
            out[0, :, there] = new

    @pl.loop(0, cols_a // width)
    def _(i):
        some_columns(i * width, outs[::2], i * width)

    @pl.loop(0, cols_b // width)
    def _(i):
        some_columns(cols_a + i * width, outs[1::2], i * width)


def join_kernel(cols_a, *refs):
    parts = refs[:-4]
    rows_a, flipped = refs[-3:-1]
    ranks = parts[0].shape[0]
    for i, part in enumerate(parts):
        rows_a[pl.ds(i * ranks, ranks), :] = part[:, :cols_a]
    rows_b = jnp.concatenate([part[:, cols_a:].astype(F32) for part in parts], axis=0)
    flipped[...] = (rows_b * ADAPTER_SCALE).T.astype(BF16)


def merge_kernel(k, width, *refs):
    panel, rows_a, flipped = refs[:3]
    out, tiles, sems = refs[-3:]
    cols = rows_a.shape[1]
    base = (lax.axis_index("tensor") ^ k) * cols
    copies = []
    for step in range(cols // width):
        columns = pl.ds(pl.multiple_of(base + step * width, width), width)
        increment = jnp.dot(
            flipped[...], rows_a[:, step * width : (step + 1) * width], preferred_element_type=F32
        )
        tiles[step] = (panel[:, columns].astype(F32) + increment).astype(BF16)
        copy = pltpu.make_async_copy(tiles.at[step], out.at[0, :, columns], sems.at[step])
        copy.start()
        copies.append(copy)
    for copy in copies:
        copy.wait()


def per_device(
    n_dp,
    n_expert,
    n_tensor,
    weight,
    factor_a,
    factor_b,
    moment_a,
    second_a,
    first_moment_factor_b,
    second_b,
    grad_a,
    grad_b,
    slot_of,
):
    ranks, cols_a = factor_a.shape[1:]
    cols_b = factor_b.shape[2]
    cols = cols_a + cols_b

    pieces = pl.pallas_call(
        functools.partial(pack_kernel, n_dp, ranks, cols_a),
        in_specs=[HBM, HBM],
        out_specs=[VMEM] * (n_dp - 1),
        out_shape=[pltpu.VMEM((ranks, cols), BF16)] * (n_dp - 1),
        scratch_shapes=[
            pltpu.VMEM((n_dp - 1, ranks, cols), F32),
            pltpu.SemaphoreType.DMA((n_dp - 1, 2)),
        ],
        compiler_params=PARAMS,
        name="pack",
    )(left(grad_a), left(grad_b))
    got = [held(swap(pieces[k - 1], "dp", n_dp, k)) for k in range(n_dp - 1, 0, -1)]

    *state, order = pl.pallas_call(
        functools.partial(load_kernel, ranks, cols_a),
        in_specs=[HBM] * 9,
        out_specs=[VMEM] * 4 + [SMEM],
        out_shape=[pltpu.VMEM((ranks, cols), F32)] * 4 + [pltpu.SMEM((1,), jnp.int32)],
        scratch_shapes=[pltpu.SMEM(slot_of.shape, jnp.int32), pltpu.SemaphoreType.DMA((9,))],
        compiler_params=PARAMS,
        cost_estimate=estimate(4 * ranks * cols * 4),
        name="load",
    )(
        *map(
            left,
            (
                slot_of,
                grad_a,
                grad_b,
                factor_a,
                factor_b,
                moment_a,
                first_moment_factor_b,
                second_a,
                second_b,
            ),
        ),
    )
    state = [held(x) for x in state]

    send = pl.pallas_call(
        send_kernel,
        in_specs=[VMEM] * (3 + n_dp),
        out_specs=VMEM,
        out_shape=pltpu.VMEM((ranks, cols), BF16),
        compiler_params=PARAMS,
        name="send",
    )(*state, *got)

    def move(slots):
        def branch(send, state, got):
            mine = lax.ppermute(send, "expert", list(enumerate(slots)))
            new = pl.pallas_call(
                functools.partial(state_kernel, n_dp - 1, cols_a),
                in_specs=[VMEM] * (3 + n_dp),
                out_specs=[VMEM] * 6,
                out_shape=[
                    jax.ShapeDtypeStruct(factor_a.shape, F32),
                    jax.ShapeDtypeStruct(factor_b.shape, F32),
                ]
                * 3,
                compiler_params=PARAMS,
                cost_estimate=estimate(3 * ranks * cols * 4),
                name="state",
            )(*map(held, state), *map(held, got))
            mine = pl.pallas_call(
                keep_kernel,
                in_specs=[VMEM],
                out_specs=VMEM,
                out_shape=pltpu.VMEM((ranks, cols), BF16),
                compiler_params=PARAMS,
                name="keep",
            )(held(mine))
            return mine, new

        return branch

    if n_expert <= MOST_SWITCHED:
        orders = itertools.permutations(range(n_expert))
        mine, new = lax.switch(order[0], [move(slots) for slots in orders], send, state, got)
        mine = jnp.where(order[0] >= 0, mine, jnp.zeros_like(mine))
    else:
        mine, new = move(range(n_expert))(send, state, got)
        here = lax.axis_index("expert")
        experts = jnp.arange(n_expert, dtype=jnp.int32)
        wanted = jnp.sum(jnp.where(slot_of == here, experts, 0)) ^ here
        for k in range(1, n_expert):
            mine = jnp.where(wanted == k, swap(send, "expert", n_expert, k), mine)
    new_a, new_b, new_moment_a, new_moment_b, new_second_a, new_second_b = new

    parts = [mine] + [swap(mine, "dp", n_dp, k) for k in range(1, n_dp)]
    panel_shape = weight.shape[1:]
    panel = pl.pallas_call(
        panel_kernel,
        in_specs=[HBM],
        out_specs=VMEM,
        out_shape=pltpu.VMEM(panel_shape, BF16),
        scratch_shapes=[pltpu.SemaphoreType.DMA],
        compiler_params=PARAMS,
        cost_estimate=estimate(weight.size * 4),
        name="panel",
    )(left(weight))
    rows_a, flipped, panel = pl.pallas_call(
        functools.partial(join_kernel, cols_a),
        in_specs=[VMEM] * (n_dp + 1),
        out_specs=[VMEM] * 3,
        out_shape=[
            pltpu.VMEM((ranks * n_dp, cols_a), BF16),
            pltpu.VMEM((cols_b, ranks * n_dp), BF16),
            pltpu.VMEM(panel_shape, BF16),
        ],
        input_output_aliases={n_dp: 2},
        compiler_params=PARAMS,
        name="join",
    )(*map(held, parts), held(panel))

    merged = None
    width = 512
    for k in range(n_tensor):
        block = held(rows_a if k == 0 else swap(rows_a, "tensor", n_tensor, k))
        operands = [held(panel), block, held(flipped)] + ([] if merged is None else [merged])
        merged = pl.pallas_call(
            functools.partial(merge_kernel, k, width),
            in_specs=[VMEM] * 3 + [HBM] * (len(operands) - 3),
            out_specs=HBM,
            out_shape=jax.ShapeDtypeStruct(weight.shape, BF16),
            scratch_shapes=[
                pltpu.VMEM((cols_a // width, panel_shape[0], width), BF16),
                pltpu.SemaphoreType.DMA((cols_a // width,)),
            ],
            input_output_aliases={} if merged is None else {3: 0},
            compiler_params=PARAMS,
            cost_estimate=estimate(
                panel_shape[0] * cols_a * 2, 2 * panel_shape[0] * cols_a * ranks * n_dp
            ),
            name=f"merge{k}",
        )(*operands)
    return (merged, new_a, new_b, new_moment_a, new_second_a, new_moment_b, new_second_b)


def solution(mesh):
    sizes = dict(mesh.shape)

    def body(*args):
        return per_device(sizes["dp"], sizes["expert"], sizes["tensor"], *args)

    state = P("expert", "dp", "tensor")
    grad = P("dp", "expert", None, "tensor")
    weight = P("expert", "tensor", None)
    in_specs = (weight,) + (state,) * 6 + (grad,) * 2 + (P(),)
    out_specs = (weight,) + (state,) * 6
    return jax.shard_map(body, mesh=mesh, in_specs=in_specs, out_specs=out_specs, check_vma=False)
```

```python
import functools
import itertools

import jax
import jax.numpy as jnp
from jax import lax
from jax.experimental import pallas as pl
from jax.experimental.pallas import tpu as pltpu
from jax.sharding import PartitionSpec as P

ADAM_STEP = 20


ADAPTER_SCALE = 2.0
BETA_ONE = 0.9
BETA_TWO = 0.95
LEARN_RATE = 0.08
STABILITY_TERM = 1e-08

MOST_SWITCHED = 4

F32 = jnp.float32
BF16 = jnp.bfloat16
VMEM = pl.BlockSpec(memory_space=pltpu.VMEM)
SMEM = pl.BlockSpec(memory_space=pltpu.SMEM)
HBM = pl.BlockSpec(memory_space=pltpu.HBM)
PARAMS = pltpu.CompilerParams(vmem_limit_bytes=16 * 1024 * 1024)


def adam_update(param, moment, second, grad):
    corr_one = 1.0 - BETA_ONE**ADAM_STEP
    corr_two = 1.0 - BETA_TWO**ADAM_STEP
    moment_new = BETA_ONE * moment + (1.0 - BETA_ONE) * grad
    second_new = BETA_TWO * second + (1.0 - BETA_TWO) * grad * grad
    param_new = param - LEARN_RATE * (moment_new / corr_one) / (
        jnp.sqrt(second_new / corr_two) + STABILITY_TERM
    )
    return (param_new, moment_new, second_new)


def swap(x, axis, n, k):
    return lax.ppermute(x, axis, [(i, i ^ k) for i in range(n)])


def held(x):
    return pltpu.with_memory_space_constraint(x, pltpu.VMEM)


def left(x):
    return pltpu.with_memory_space_constraint(x, pltpu.HBM)


def estimate(nbytes, flops=0):
    return pl.CostEstimate(flops=flops, bytes_accessed=nbytes, transcendentals=0)


def pack_kernel(n_dp, ranks, cols_a, grad_a, grad_b, *refs):
    outs, rows, sems = refs[: n_dp - 1], refs[n_dp - 1], refs[n_dp]
    me = lax.axis_index("dp")
    copies = []
    for k in range(1, n_dp):
        start = pl.multiple_of((me ^ k) * ranks, ranks)
        pair = (
            pltpu.make_async_copy(
                grad_a.at[0, 0, pl.ds(start, ranks), :],
                rows.at[k - 1, :, pl.ds(0, cols_a)],
                sems.at[k - 1, 0],
            ),
            pltpu.make_async_copy(
                grad_b.at[0, 0, pl.ds(start, ranks), :],
                rows.at[k - 1, :, pl.ds(cols_a, rows.shape[2] - cols_a)],
                sems.at[k - 1, 1],
            ),
        )
        for copy in pair:
            copy.start()
        copies.append(pair)
    for k, pair in enumerate(copies):
        for copy in pair:
            copy.wait()
        outs[k][...] = rows[k].astype(BF16)


def load_kernel(ranks, cols_a, slots_in, *refs):
    grad_a, grad_b, fa, fb, ma, mb, sa, sb = refs[:8]
    grad, factor, moment, second, order, slot_of, sems = refs[8:]
    me = lax.axis_index("dp")
    start = pl.multiple_of(me * ranks, ranks)
    first = pl.ds(0, cols_a)
    last = pl.ds(cols_a, grad.shape[1] - cols_a)
    pairs = [
        (grad_a.at[0, 0, pl.ds(start, ranks), :], grad.at[:, first]),
        (grad_b.at[0, 0, pl.ds(start, ranks), :], grad.at[:, last]),
        (fa.at[0], factor.at[:, first]),
        (fb.at[0], factor.at[:, last]),
        (ma.at[0], moment.at[:, first]),
        (mb.at[0], moment.at[:, last]),
        (sa.at[0], second.at[:, first]),
        (sb.at[0], second.at[:, last]),
        (slots_in, slot_of),
    ]
    copies = [pltpu.make_async_copy(a, b, sems.at[i]) for i, (a, b) in enumerate(pairs)]
    for copy in copies:
        copy.start()
    copies.pop().wait()
    n = slot_of.shape[0]
    number = jnp.int32(0)
    for i in range(n - 1):
        smaller = jnp.int32(0)
        for j in range(i + 1, n):
            smaller += (slot_of[j] < slot_of[i]).astype(jnp.int32)
        number = number * (n - i) + smaller
    order[0] = number
    for copy in copies:
        copy.wait()


def keep_kernel(piece, kept):
    kept[...] = piece[...]


def send_kernel(*refs):
    grad, factor, moment, second = refs[:4]
    total = grad[...]
    for piece in refs[4:-1]:
        total = total + piece[...].astype(F32)
    refs[-1][...] = adam_update(factor[...], moment[...], second[...], total)[0].astype(BF16)


def state_kernel(n_got, cols_a, weight, *refs):
    ins = refs[: 4 + n_got]
    outs = refs[4 + n_got : 10 + n_got]
    panel = refs[10 + n_got]
    parts = refs[11 + n_got : 17 + n_got]
    sems = refs[-1]
    cols_b = ins[0].shape[1] - cols_a
    width = 256 if cols_a % 256 == 0 and cols_b % 256 == 0 else 128
    load = pltpu.make_async_copy(weight.at[0], panel, sems.at[0])
    load.start()

    def some_columns(start, into, at):
        here = pl.ds(pl.multiple_of(start, width), width)
        there = pl.ds(pl.multiple_of(at, width), width)
        grad, factor, moment, second = (ref[:, here] for ref in ins[:4])
        for piece in ins[4:]:
            grad = grad + piece[:, here].astype(F32)
        for out, new in zip(into, adam_update(factor, moment, second, grad)):
            out[:, there] = new

    @pl.loop(0, cols_a // width)
    def _(i):
        some_columns(i * width, parts[::2], i * width)

    @pl.loop(0, cols_b // width)
    def _(i):
        some_columns(cols_a + i * width, parts[1::2], i * width)

    copies = [
        pltpu.make_async_copy(part, out.at[0], sems.at[1 + i])
        for i, (part, out) in enumerate(zip(parts, outs))
    ]
    for copy in copies:
        copy.start()
    for copy in copies:
        copy.wait()
    load.wait()


def join_kernel(cols_a, *refs):
    parts = refs[:-4]
    rows_a, flipped = refs[-3:-1]
    ranks = parts[0].shape[0]
    for i, part in enumerate(parts):
        rows_a[pl.ds(i * ranks, ranks), :] = part[:, :cols_a]
    rows_b = jnp.concatenate([part[:, cols_a:].astype(F32) for part in parts], axis=0)
    flipped[...] = (rows_b * ADAPTER_SCALE).T.astype(BF16)


def merge_kernel(k, width, *refs):
    panel, rows_a, flipped = refs[:3]
    out, tiles, sems = refs[-3:]
    cols = rows_a.shape[1]
    base = (lax.axis_index("tensor") ^ k) * cols
    steps = cols // width

    def copy(step):
        columns = pl.ds(pl.multiple_of(base + step * width, width), width)
        return pltpu.make_async_copy(tiles.at[step], out.at[0, :, columns], sems.at[step])

    @pl.loop(0, steps)
    def _(step):
        span = pl.ds(pl.multiple_of(step * width, width), width)
        columns = pl.ds(pl.multiple_of(base + step * width, width), width)
        increment = jnp.dot(flipped[...], rows_a[:, span], preferred_element_type=F32)
        tiles[step] = (panel[:, columns].astype(F32) + increment).astype(BF16)
        copy(step).start()

    @pl.loop(0, steps)
    def _(step):
        copy(step).wait()


def per_device(
    n_dp,
    n_expert,
    n_tensor,
    weight,
    factor_a,
    factor_b,
    moment_a,
    second_a,
    first_moment_factor_b,
    second_b,
    grad_a,
    grad_b,
    slot_of,
):
    ranks, cols_a = factor_a.shape[1:]
    cols_b = factor_b.shape[2]
    cols = cols_a + cols_b

    pieces = pl.pallas_call(
        functools.partial(pack_kernel, n_dp, ranks, cols_a),
        in_specs=[HBM, HBM],
        out_specs=[VMEM] * (n_dp - 1),
        out_shape=[pltpu.VMEM((ranks, cols), BF16)] * (n_dp - 1),
        scratch_shapes=[
            pltpu.VMEM((n_dp - 1, ranks, cols), F32),
            pltpu.SemaphoreType.DMA((n_dp - 1, 2)),
        ],
        compiler_params=PARAMS,
        name="pack",
    )(left(grad_a), left(grad_b))
    got = [held(swap(pieces[k - 1], "dp", n_dp, k)) for k in range(n_dp - 1, 0, -1)]

    *state, order = pl.pallas_call(
        functools.partial(load_kernel, ranks, cols_a),
        in_specs=[HBM] * 9,
        out_specs=[VMEM] * 4 + [SMEM],
        out_shape=[pltpu.VMEM((ranks, cols), F32)] * 4 + [pltpu.SMEM((1,), jnp.int32)],
        scratch_shapes=[pltpu.SMEM(slot_of.shape, jnp.int32), pltpu.SemaphoreType.DMA((9,))],
        compiler_params=PARAMS,
        cost_estimate=estimate(4 * ranks * cols * 4),
        name="load",
    )(
        *map(
            left,
            (
                slot_of,
                grad_a,
                grad_b,
                factor_a,
                factor_b,
                moment_a,
                first_moment_factor_b,
                second_a,
                second_b,
            ),
        ),
    )
    state = [held(x) for x in state]

    send = pl.pallas_call(
        send_kernel,
        in_specs=[VMEM] * (3 + n_dp),
        out_specs=VMEM,
        out_shape=pltpu.VMEM((ranks, cols), BF16),
        compiler_params=PARAMS,
        name="send",
    )(*state, *got)

    def move(slots):
        def branch(send):
            return pl.pallas_call(
                keep_kernel,
                in_specs=[VMEM],
                out_specs=VMEM,
                out_shape=pltpu.VMEM((ranks, cols), BF16),
                compiler_params=PARAMS,
                name="keep",
            )(held(lax.ppermute(send, "expert", list(enumerate(slots)))))

        return branch

    if n_expert <= MOST_SWITCHED:
        orders = itertools.permutations(range(n_expert))
        mine = lax.switch(order[0], [move(slots) for slots in orders], send)
        mine = jnp.where(order[0] >= 0, mine, jnp.zeros_like(mine))
    else:
        mine = send
        here = lax.axis_index("expert")
        experts = jnp.arange(n_expert, dtype=jnp.int32)
        wanted = jnp.sum(jnp.where(slot_of == here, experts, 0)) ^ here
        for k in range(1, n_expert):
            mine = jnp.where(wanted == k, swap(send, "expert", n_expert, k), mine)

    parts = [mine] + [swap(mine, "dp", n_dp, k) for k in range(1, n_dp)]
    panel_shape = weight.shape[1:]
    shapes = [factor_a.shape, factor_b.shape] * 3
    *new, panel = pl.pallas_call(
        functools.partial(state_kernel, n_dp - 1, cols_a),
        in_specs=[HBM] + [VMEM] * (3 + n_dp),
        out_specs=[HBM] * 6 + [VMEM],
        out_shape=[jax.ShapeDtypeStruct(shape, F32) for shape in shapes]
        + [pltpu.VMEM(panel_shape, BF16)],
        scratch_shapes=[pltpu.VMEM(shape[1:], F32) for shape in shapes]
        + [pltpu.SemaphoreType.DMA((7,))],
        compiler_params=PARAMS,
        cost_estimate=estimate(weight.size * 4),
        name="state",
    )(left(weight), *state, *got)
    new_a, new_b, new_moment_a, new_moment_b, new_second_a, new_second_b = new
    rows_a, flipped, panel = pl.pallas_call(
        functools.partial(join_kernel, cols_a),
        in_specs=[VMEM] * (n_dp + 1),
        out_specs=[VMEM] * 3,
        out_shape=[
            pltpu.VMEM((ranks * n_dp, cols_a), BF16),
            pltpu.VMEM((cols_b, ranks * n_dp), BF16),
            pltpu.VMEM(panel_shape, BF16),
        ],
        input_output_aliases={n_dp: 2},
        compiler_params=PARAMS,
        name="join",
    )(*map(held, parts), held(panel))

    merged = None
    width = 256
    for k in range(n_tensor):
        block = held(rows_a if k == 0 else swap(rows_a, "tensor", n_tensor, k))
        operands = [held(panel), block, held(flipped)] + ([] if merged is None else [merged])
        merged = pl.pallas_call(
            functools.partial(merge_kernel, k, width),
            in_specs=[VMEM] * 3 + [HBM] * (len(operands) - 3),
            out_specs=HBM,
            out_shape=jax.ShapeDtypeStruct(weight.shape, BF16),
            scratch_shapes=[
                pltpu.VMEM((cols_a // width, panel_shape[0], width), BF16),
                pltpu.SemaphoreType.DMA((cols_a // width,)),
            ],
            input_output_aliases={} if merged is None else {3: 0},
            compiler_params=PARAMS,
            cost_estimate=estimate(
                panel_shape[0] * cols_a * 2, 2 * panel_shape[0] * cols_a * ranks * n_dp
            ),
            name=f"merge{k}",
        )(*operands)
    return (merged, new_a, new_b, new_moment_a, new_second_a, new_moment_b, new_second_b)


def solution(mesh):
    sizes = dict(mesh.shape)

    def body(*args):
        return per_device(sizes["dp"], sizes["expert"], sizes["tensor"], *args)

    state = P("expert", "dp", "tensor")
    grad = P("dp", "expert", None, "tensor")
    weight = P("expert", "tensor", None)
    in_specs = (weight,) + (state,) * 6 + (grad,) * 2 + (P(),)
    out_specs = (weight,) + (state,) * 6
    return jax.shard_map(body, mesh=mesh, in_specs=in_specs, out_specs=out_specs, check_vma=False)
```

```python
import functools
import itertools

import jax
import jax.numpy as jnp
from jax import lax
from jax.experimental import pallas as pl
from jax.experimental.pallas import tpu as pltpu
from jax.sharding import PartitionSpec as P

ADAM_STEP = 20


ADAPTER_SCALE = 2.0
BETA_ONE = 0.9
BETA_TWO = 0.95
LEARN_RATE = 0.08
STABILITY_TERM = 1e-08

MOST_SWITCHED = 4

F32 = jnp.float32
BF16 = jnp.bfloat16
VMEM = pl.BlockSpec(memory_space=pltpu.VMEM)
SMEM = pl.BlockSpec(memory_space=pltpu.SMEM)
HBM = pl.BlockSpec(memory_space=pltpu.HBM)
PARAMS = pltpu.CompilerParams(vmem_limit_bytes=16 * 1024 * 1024)


def adam_update(param, moment, second, grad):
    corr_one = 1.0 - BETA_ONE**ADAM_STEP
    corr_two = 1.0 - BETA_TWO**ADAM_STEP
    moment_new = BETA_ONE * moment + (1.0 - BETA_ONE) * grad
    second_new = BETA_TWO * second + (1.0 - BETA_TWO) * grad * grad
    param_new = param - LEARN_RATE * (moment_new / corr_one) / (
        jnp.sqrt(second_new / corr_two) + STABILITY_TERM
    )
    return (param_new, moment_new, second_new)


def swap(x, axis, n, k):
    return lax.ppermute(x, axis, [(i, i ^ k) for i in range(n)])


def held(x):
    return pltpu.with_memory_space_constraint(x, pltpu.VMEM)


def left(x):
    return pltpu.with_memory_space_constraint(x, pltpu.HBM)


def estimate(nbytes, flops=0):
    return pl.CostEstimate(flops=flops, bytes_accessed=nbytes, transcendentals=0)


def pack_kernel(n_dp, ranks, cols_a, grad_a, grad_b, *refs):
    outs, rows, sems = refs[: n_dp - 1], refs[n_dp - 1], refs[n_dp]
    me = lax.axis_index("dp")
    copies = []
    for k in range(1, n_dp):
        start = pl.multiple_of((me ^ k) * ranks, ranks)
        pair = (
            pltpu.make_async_copy(
                grad_a.at[0, 0, pl.ds(start, ranks), :],
                rows.at[k - 1, :, pl.ds(0, cols_a)],
                sems.at[k - 1, 0],
            ),
            pltpu.make_async_copy(
                grad_b.at[0, 0, pl.ds(start, ranks), :],
                rows.at[k - 1, :, pl.ds(cols_a, rows.shape[2] - cols_a)],
                sems.at[k - 1, 1],
            ),
        )
        for copy in pair:
            copy.start()
        copies.append(pair)
    for k, pair in enumerate(copies):
        for copy in pair:
            copy.wait()
        outs[k][...] = rows[k].astype(BF16)


def load_kernel(ranks, cols_a, slots_in, *refs):
    grad_a, grad_b, fa, fb, ma, mb, sa, sb = refs[:8]
    grad, factor, moment, second, order, slot_of, sems = refs[8:]
    me = lax.axis_index("dp")
    start = pl.multiple_of(me * ranks, ranks)
    first = pl.ds(0, cols_a)
    last = pl.ds(cols_a, grad.shape[1] - cols_a)
    pairs = [
        (grad_a.at[0, 0, pl.ds(start, ranks), :], grad.at[:, first]),
        (grad_b.at[0, 0, pl.ds(start, ranks), :], grad.at[:, last]),
        (fa.at[0], factor.at[:, first]),
        (fb.at[0], factor.at[:, last]),
        (ma.at[0], moment.at[:, first]),
        (mb.at[0], moment.at[:, last]),
        (sa.at[0], second.at[:, first]),
        (sb.at[0], second.at[:, last]),
        (slots_in, slot_of),
    ]
    copies = [pltpu.make_async_copy(a, b, sems.at[i]) for i, (a, b) in enumerate(pairs)]
    for copy in copies:
        copy.start()
    copies.pop().wait()
    n = slot_of.shape[0]
    number = jnp.int32(0)
    for i in range(n - 1):
        smaller = jnp.int32(0)
        for j in range(i + 1, n):
            smaller += (slot_of[j] < slot_of[i]).astype(jnp.int32)
        number = number * (n - i) + smaller
    order[0] = number
    for copy in copies:
        copy.wait()


def keep_kernel(piece, kept):
    kept[...] = piece[...]


def send_kernel(*refs):
    grad, factor, moment, second = refs[:4]
    total = grad[...]
    for piece in refs[4:-1]:
        total = total + piece[...].astype(F32)
    refs[-1][...] = adam_update(factor[...], moment[...], second[...], total)[0].astype(BF16)


def state_kernel(n_got, cols_a, weight, *refs):
    ins = refs[: 4 + n_got]
    outs = refs[4 + n_got : 10 + n_got]
    panel = refs[10 + n_got]
    parts = refs[11 + n_got : 17 + n_got]
    sems = refs[-1]
    cols_b = ins[0].shape[1] - cols_a
    width = 256 if cols_a % 256 == 0 and cols_b % 256 == 0 else 128
    load = pltpu.make_async_copy(weight.at[0], panel, sems.at[0])
    load.start()

    def some_columns(start, into, at):
        here = pl.ds(pl.multiple_of(start, width), width)
        there = pl.ds(pl.multiple_of(at, width), width)
        grad, factor, moment, second = (ref[:, here] for ref in ins[:4])
        for piece in ins[4:]:
            grad = grad + piece[:, here].astype(F32)
        for out, new in zip(into, adam_update(factor, moment, second, grad)):
            out[:, there] = new

    @pl.loop(0, cols_a // width)
    def _(i):
        some_columns(i * width, parts[::2], i * width)

    @pl.loop(0, cols_b // width)
    def _(i):
        some_columns(cols_a + i * width, parts[1::2], i * width)

    copies = [
        pltpu.make_async_copy(part, out.at[0], sems.at[1 + i])
        for i, (part, out) in enumerate(zip(parts, outs))
    ]
    for copy in copies:
        copy.start()
    for copy in copies:
        copy.wait()
    load.wait()


def join_kernel(cols_a, *refs):
    parts = refs[:-4]
    rows_a, flipped = refs[-3:-1]
    ranks = parts[0].shape[0]
    for i, part in enumerate(parts):
        rows_a[pl.ds(i * ranks, ranks), :] = part[:, :cols_a]
    rows_b = jnp.concatenate([part[:, cols_a:].astype(F32) for part in parts], axis=0)
    flipped[...] = (rows_b * ADAPTER_SCALE).T.astype(BF16)


def merge_kernel(k, width, *refs):
    panel, rows_a, flipped = refs[:3]
    out, tiles, sems = refs[-3:]
    cols = rows_a.shape[1]
    base = (lax.axis_index("tensor") ^ k) * cols
    copies = []
    for step in range(cols // width):
        span = slice(step * width, (step + 1) * width)
        columns = pl.ds(pl.multiple_of(base + step * width, width), width)
        increment = jnp.dot(flipped[...], rows_a[:, span], preferred_element_type=F32)
        tiles[step] = (panel[:, columns].astype(F32) + increment).astype(BF16)
        copy = pltpu.make_async_copy(tiles.at[step], out.at[0, :, columns], sems.at[step])
        copy.start()
        copies.append(copy)
    for copy in copies:
        copy.wait()


def per_device(
    n_dp,
    n_expert,
    n_tensor,
    weight,
    factor_a,
    factor_b,
    moment_a,
    second_a,
    first_moment_factor_b,
    second_b,
    grad_a,
    grad_b,
    slot_of,
):
    ranks, cols_a = factor_a.shape[1:]
    cols_b = factor_b.shape[2]
    cols = cols_a + cols_b

    pieces = pl.pallas_call(
        functools.partial(pack_kernel, n_dp, ranks, cols_a),
        in_specs=[HBM, HBM],
        out_specs=[VMEM] * (n_dp - 1),
        out_shape=[pltpu.VMEM((ranks, cols), BF16)] * (n_dp - 1),
        scratch_shapes=[
            pltpu.VMEM((n_dp - 1, ranks, cols), F32),
            pltpu.SemaphoreType.DMA((n_dp - 1, 2)),
        ],
        compiler_params=PARAMS,
        name="pack",
    )(left(grad_a), left(grad_b))
    got = [held(swap(pieces[k - 1], "dp", n_dp, k)) for k in range(n_dp - 1, 0, -1)]

    *state, order = pl.pallas_call(
        functools.partial(load_kernel, ranks, cols_a),
        in_specs=[HBM] * 9,
        out_specs=[VMEM] * 4 + [SMEM],
        out_shape=[pltpu.VMEM((ranks, cols), F32)] * 4 + [pltpu.SMEM((1,), jnp.int32)],
        scratch_shapes=[pltpu.SMEM(slot_of.shape, jnp.int32), pltpu.SemaphoreType.DMA((9,))],
        compiler_params=PARAMS,
        cost_estimate=estimate(4 * ranks * cols * 4),
        name="load",
    )(
        *map(
            left,
            (
                slot_of,
                grad_a,
                grad_b,
                factor_a,
                factor_b,
                moment_a,
                first_moment_factor_b,
                second_a,
                second_b,
            ),
        ),
    )
    state = [held(x) for x in state]

    send = pl.pallas_call(
        send_kernel,
        in_specs=[VMEM] * (3 + n_dp),
        out_specs=VMEM,
        out_shape=pltpu.VMEM((ranks, cols), BF16),
        compiler_params=PARAMS,
        name="send",
    )(*state, *got)

    def move(slots):
        def branch(send):
            return pl.pallas_call(
                keep_kernel,
                in_specs=[VMEM],
                out_specs=VMEM,
                out_shape=pltpu.VMEM((ranks, cols), BF16),
                compiler_params=PARAMS,
                name="keep",
            )(held(lax.ppermute(send, "expert", list(enumerate(slots)))))

        return branch

    if n_expert <= MOST_SWITCHED:
        orders = itertools.permutations(range(n_expert))
        mine = lax.switch(order[0], [move(slots) for slots in orders], send)
        mine = jnp.where(order[0] >= 0, mine, jnp.zeros_like(mine))
    else:
        mine = send
        here = lax.axis_index("expert")
        experts = jnp.arange(n_expert, dtype=jnp.int32)
        wanted = jnp.sum(jnp.where(slot_of == here, experts, 0)) ^ here
        for k in range(1, n_expert):
            mine = jnp.where(wanted == k, swap(send, "expert", n_expert, k), mine)

    parts = [mine] + [swap(mine, "dp", n_dp, k) for k in range(1, n_dp)]
    panel_shape = weight.shape[1:]
    shapes = [factor_a.shape, factor_b.shape] * 3
    *new, panel = pl.pallas_call(
        functools.partial(state_kernel, n_dp - 1, cols_a),
        in_specs=[HBM] + [VMEM] * (3 + n_dp),
        out_specs=[HBM] * 6 + [VMEM],
        out_shape=[jax.ShapeDtypeStruct(shape, F32) for shape in shapes]
        + [pltpu.VMEM(panel_shape, BF16)],
        scratch_shapes=[pltpu.VMEM(shape[1:], F32) for shape in shapes]
        + [pltpu.SemaphoreType.DMA((7,))],
        compiler_params=PARAMS,
        cost_estimate=estimate(weight.size * 4),
        name="state",
    )(left(weight), *state, *got)
    new_a, new_b, new_moment_a, new_moment_b, new_second_a, new_second_b = new
    rows_a, flipped, panel = pl.pallas_call(
        functools.partial(join_kernel, cols_a),
        in_specs=[VMEM] * (n_dp + 1),
        out_specs=[VMEM] * 3,
        out_shape=[
            pltpu.VMEM((ranks * n_dp, cols_a), BF16),
            pltpu.VMEM((cols_b, ranks * n_dp), BF16),
            pltpu.VMEM(panel_shape, BF16),
        ],
        input_output_aliases={n_dp: 2},
        compiler_params=PARAMS,
        name="join",
    )(*map(held, parts), held(panel))

    merged = None
    width = 512
    for k in range(n_tensor):
        block = held(rows_a if k == 0 else swap(rows_a, "tensor", n_tensor, k))
        operands = [held(panel), block, held(flipped)] + ([] if merged is None else [merged])
        merged = pl.pallas_call(
            functools.partial(merge_kernel, k, width),
            in_specs=[VMEM] * 3 + [HBM] * (len(operands) - 3),
            out_specs=HBM,
            out_shape=jax.ShapeDtypeStruct(weight.shape, BF16),
            scratch_shapes=[
                pltpu.VMEM((cols_a // width, panel_shape[0], width), BF16),
                pltpu.SemaphoreType.DMA((cols_a // width,)),
            ],
            input_output_aliases={} if merged is None else {3: 0},
            compiler_params=PARAMS,
            cost_estimate=estimate(
                panel_shape[0] * cols_a * 2, 2 * panel_shape[0] * cols_a * ranks * n_dp
            ),
            name=f"merge{k}",
        )(*operands)
    return (merged, new_a, new_b, new_moment_a, new_second_a, new_moment_b, new_second_b)


def solution(mesh):
    sizes = dict(mesh.shape)

    def body(*args):
        return per_device(sizes["dp"], sizes["expert"], sizes["tensor"], *args)

    state = P("expert", "dp", "tensor")
    grad = P("dp", "expert", None, "tensor")
    weight = P("expert", "tensor", None)
    in_specs = (weight,) + (state,) * 6 + (grad,) * 2 + (P(),)
    out_specs = (weight,) + (state,) * 6
    return jax.shard_map(body, mesh=mesh, in_specs=in_specs, out_specs=out_specs, check_vma=False)
```

```python
import functools
import itertools

import jax
import jax.numpy as jnp
from jax import lax
from jax.experimental import pallas as pl
from jax.experimental.pallas import tpu as pltpu
from jax.sharding import PartitionSpec as P

ADAM_STEP = 20


ADAPTER_SCALE = 2.0
BETA_ONE = 0.9
BETA_TWO = 0.95
LEARN_RATE = 0.08
STABILITY_TERM = 1e-08

MOST_SWITCHED = 4

F32 = jnp.float32
BF16 = jnp.bfloat16
VMEM = pl.BlockSpec(memory_space=pltpu.VMEM)
SMEM = pl.BlockSpec(memory_space=pltpu.SMEM)
HBM = pl.BlockSpec(memory_space=pltpu.HBM)
PARAMS = pltpu.CompilerParams(vmem_limit_bytes=16 * 1024 * 1024)


def adam_update(param, moment, second, grad):
    corr_one = 1.0 - BETA_ONE**ADAM_STEP
    corr_two = 1.0 - BETA_TWO**ADAM_STEP
    moment_new = BETA_ONE * moment + (1.0 - BETA_ONE) * grad
    second_new = BETA_TWO * second + (1.0 - BETA_TWO) * grad * grad
    param_new = param - LEARN_RATE * (moment_new / corr_one) / (
        jnp.sqrt(second_new / corr_two) + STABILITY_TERM
    )
    return (param_new, moment_new, second_new)


def swap(x, axis, n, k):
    return lax.ppermute(x, axis, [(i, i ^ k) for i in range(n)])


def held(x):
    return pltpu.with_memory_space_constraint(x, pltpu.VMEM)


def left(x):
    return pltpu.with_memory_space_constraint(x, pltpu.HBM)


def estimate(nbytes, flops=0):
    return pl.CostEstimate(flops=flops, bytes_accessed=nbytes, transcendentals=0)


def pack_kernel(n_dp, ranks, cols_a, grad_a, grad_b, *refs):
    outs, rows, sems = refs[: n_dp - 1], refs[n_dp - 1], refs[n_dp]
    me = lax.axis_index("dp")
    copies = []
    for k in range(1, n_dp):
        start = pl.multiple_of((me ^ k) * ranks, ranks)
        pair = (
            pltpu.make_async_copy(
                grad_a.at[0, 0, pl.ds(start, ranks), :],
                rows.at[k - 1, :, pl.ds(0, cols_a)],
                sems.at[k - 1, 0],
            ),
            pltpu.make_async_copy(
                grad_b.at[0, 0, pl.ds(start, ranks), :],
                rows.at[k - 1, :, pl.ds(cols_a, rows.shape[2] - cols_a)],
                sems.at[k - 1, 1],
            ),
        )
        for copy in pair:
            copy.start()
        copies.append(pair)
    for k, pair in enumerate(copies):
        for copy in pair:
            copy.wait()
        outs[k][...] = rows[k].astype(BF16)


def load_kernel(ranks, cols_a, slots_in, *refs):
    grad_a, grad_b, fa, fb, ma, mb, sa, sb = refs[:8]
    grad, factor, moment, second, order, slot_of, sems = refs[8:]
    me = lax.axis_index("dp")
    start = pl.multiple_of(me * ranks, ranks)
    first = pl.ds(0, cols_a)
    last = pl.ds(cols_a, grad.shape[1] - cols_a)
    pairs = [
        (grad_a.at[0, 0, pl.ds(start, ranks), :], grad.at[:, first]),
        (grad_b.at[0, 0, pl.ds(start, ranks), :], grad.at[:, last]),
        (fa.at[0], factor.at[:, first]),
        (fb.at[0], factor.at[:, last]),
        (ma.at[0], moment.at[:, first]),
        (mb.at[0], moment.at[:, last]),
        (sa.at[0], second.at[:, first]),
        (sb.at[0], second.at[:, last]),
        (slots_in, slot_of),
    ]
    copies = [pltpu.make_async_copy(a, b, sems.at[i]) for i, (a, b) in enumerate(pairs)]
    for copy in copies:
        copy.start()
    copies.pop().wait()
    n = slot_of.shape[0]
    number = jnp.int32(0)
    for i in range(n - 1):
        smaller = jnp.int32(0)
        for j in range(i + 1, n):
            smaller += (slot_of[j] < slot_of[i]).astype(jnp.int32)
        number = number * (n - i) + smaller
    order[0] = number
    here = lax.axis_index("expert")
    order[1] = (slot_of[here] == here).astype(jnp.int32)
    for copy in copies:
        copy.wait()


def keep_kernel(piece, kept):
    kept[...] = piece[...]


def send_kernel(*refs):
    grad, factor, moment, second = refs[:4]
    total = grad[...]
    for piece in refs[4:-1]:
        total = total + piece[...].astype(F32)
    refs[-1][...] = adam_update(factor[...], moment[...], second[...], total)[0].astype(BF16)


def state_kernel(n_got, cols_a, weight, *refs):
    ins = refs[: 4 + n_got]
    outs = refs[4 + n_got : 10 + n_got]
    panel = refs[10 + n_got]
    parts = refs[11 + n_got : 17 + n_got]
    sems = refs[-1]
    cols_b = ins[0].shape[1] - cols_a
    width = 256 if cols_a % 256 == 0 and cols_b % 256 == 0 else 128
    load = pltpu.make_async_copy(weight.at[0], panel, sems.at[0])
    load.start()

    def some_columns(start, into, at):
        here = pl.ds(pl.multiple_of(start, width), width)
        there = pl.ds(pl.multiple_of(at, width), width)
        grad, factor, moment, second = (ref[:, here] for ref in ins[:4])
        for piece in ins[4:]:
            grad = grad + piece[:, here].astype(F32)
        for out, new in zip(into, adam_update(factor, moment, second, grad)):
            out[:, there] = new

    @pl.loop(0, cols_a // width)
    def _(i):
        some_columns(i * width, parts[::2], i * width)

    @pl.loop(0, cols_b // width)
    def _(i):
        some_columns(cols_a + i * width, parts[1::2], i * width)

    copies = [
        pltpu.make_async_copy(part, out.at[0], sems.at[1 + i])
        for i, (part, out) in enumerate(zip(parts, outs))
    ]
    for copy in copies:
        copy.start()
    for copy in copies:
        copy.wait()
    load.wait()


def join_kernel(cols_a, *refs):
    parts = refs[:-4]
    rows_a, flipped = refs[-3:-1]
    ranks = parts[0].shape[0]
    for i, part in enumerate(parts):
        rows_a[pl.ds(i * ranks, ranks), :] = part[:, :cols_a]
    rows_b = jnp.concatenate([part[:, cols_a:].astype(F32) for part in parts], axis=0)
    flipped[...] = (rows_b * ADAPTER_SCALE).T.astype(BF16)


def merge_kernel(k, width, *refs):
    panel, rows_a, flipped = refs[:3]
    out, tiles, sems = refs[-3:]
    cols = rows_a.shape[1]
    base = (lax.axis_index("tensor") ^ k) * cols
    copies = []
    for step in range(cols // width):
        span = slice(step * width, (step + 1) * width)
        columns = pl.ds(pl.multiple_of(base + step * width, width), width)
        increment = jnp.dot(flipped[...], rows_a[:, span], preferred_element_type=F32)
        tiles[step] = (panel[:, columns].astype(F32) + increment).astype(BF16)
        copy = pltpu.make_async_copy(tiles.at[step], out.at[0, :, columns], sems.at[step])
        copy.start()
        copies.append(copy)
    for copy in copies:
        copy.wait()


def per_device(
    n_dp,
    n_expert,
    n_tensor,
    weight,
    factor_a,
    factor_b,
    moment_a,
    second_a,
    first_moment_factor_b,
    second_b,
    grad_a,
    grad_b,
    slot_of,
):
    ranks, cols_a = factor_a.shape[1:]
    cols_b = factor_b.shape[2]
    cols = cols_a + cols_b

    pieces = pl.pallas_call(
        functools.partial(pack_kernel, n_dp, ranks, cols_a),
        in_specs=[HBM, HBM],
        out_specs=[VMEM] * (n_dp - 1),
        out_shape=[pltpu.VMEM((ranks, cols), BF16)] * (n_dp - 1),
        scratch_shapes=[
            pltpu.VMEM((n_dp - 1, ranks, cols), F32),
            pltpu.SemaphoreType.DMA((n_dp - 1, 2)),
        ],
        compiler_params=PARAMS,
        name="pack",
    )(left(grad_a), left(grad_b))
    got = [held(swap(pieces[k - 1], "dp", n_dp, k)) for k in range(n_dp - 1, 0, -1)]

    *state, order = pl.pallas_call(
        functools.partial(load_kernel, ranks, cols_a),
        in_specs=[HBM] * 9,
        out_specs=[VMEM] * 4 + [SMEM],
        out_shape=[pltpu.VMEM((ranks, cols), F32)] * 4 + [pltpu.SMEM((2,), jnp.int32)],
        scratch_shapes=[pltpu.SMEM(slot_of.shape, jnp.int32), pltpu.SemaphoreType.DMA((9,))],
        compiler_params=PARAMS,
        cost_estimate=estimate(4 * ranks * cols * 4),
        name="load",
    )(
        *map(
            left,
            (
                slot_of,
                grad_a,
                grad_b,
                factor_a,
                factor_b,
                moment_a,
                first_moment_factor_b,
                second_a,
                second_b,
            ),
        ),
    )
    state = [held(x) for x in state]

    send = pl.pallas_call(
        send_kernel,
        in_specs=[VMEM] * (3 + n_dp),
        out_specs=VMEM,
        out_shape=pltpu.VMEM((ranks, cols), BF16),
        compiler_params=PARAMS,
        name="send",
    )(*state, *got)

    def move(slots):
        pairs = [(expert, slot) for expert, slot in enumerate(slots) if expert != slot]

        def branch(send):
            mine = lax.ppermute(send, "expert", pairs) if pairs else send
            return pl.pallas_call(
                keep_kernel,
                in_specs=[VMEM],
                out_specs=VMEM,
                out_shape=pltpu.VMEM((ranks, cols), BF16),
                compiler_params=PARAMS,
                name="keep",
            )(held(mine))

        return branch

    if n_expert <= MOST_SWITCHED:
        orders = itertools.permutations(range(n_expert))
        mine = lax.switch(order[0], [move(slots) for slots in orders], send)
        mine = jnp.where(order[1] == 1, send, mine)
    else:
        mine = send
        here = lax.axis_index("expert")
        experts = jnp.arange(n_expert, dtype=jnp.int32)
        wanted = jnp.sum(jnp.where(slot_of == here, experts, 0)) ^ here
        for k in range(1, n_expert):
            mine = jnp.where(wanted == k, swap(send, "expert", n_expert, k), mine)

    parts = [mine] + [swap(mine, "dp", n_dp, k) for k in range(1, n_dp)]
    panel_shape = weight.shape[1:]
    shapes = [factor_a.shape, factor_b.shape] * 3
    *new, panel = pl.pallas_call(
        functools.partial(state_kernel, n_dp - 1, cols_a),
        in_specs=[HBM] + [VMEM] * (3 + n_dp),
        out_specs=[HBM] * 6 + [VMEM],
        out_shape=[jax.ShapeDtypeStruct(shape, F32) for shape in shapes]
        + [pltpu.VMEM(panel_shape, BF16)],
        scratch_shapes=[pltpu.VMEM(shape[1:], F32) for shape in shapes]
        + [pltpu.SemaphoreType.DMA((7,))],
        compiler_params=PARAMS,
        cost_estimate=estimate(weight.size * 4),
        name="state",
    )(left(weight), *state, *got)
    new_a, new_b, new_moment_a, new_moment_b, new_second_a, new_second_b = new
    rows_a, flipped, panel = pl.pallas_call(
        functools.partial(join_kernel, cols_a),
        in_specs=[VMEM] * (n_dp + 1),
        out_specs=[VMEM] * 3,
        out_shape=[
            pltpu.VMEM((ranks * n_dp, cols_a), BF16),
            pltpu.VMEM((cols_b, ranks * n_dp), BF16),
            pltpu.VMEM(panel_shape, BF16),
        ],
        input_output_aliases={n_dp: 2},
        compiler_params=PARAMS,
        name="join",
    )(*map(held, parts), held(panel))

    merged = None
    width = 512
    for k in range(n_tensor):
        block = held(rows_a if k == 0 else swap(rows_a, "tensor", n_tensor, k))
        operands = [held(panel), block, held(flipped)] + ([] if merged is None else [merged])
        merged = pl.pallas_call(
            functools.partial(merge_kernel, k, width),
            in_specs=[VMEM] * 3 + [HBM] * (len(operands) - 3),
            out_specs=HBM,
            out_shape=jax.ShapeDtypeStruct(weight.shape, BF16),
            scratch_shapes=[
                pltpu.VMEM((cols_a // width, panel_shape[0], width), BF16),
                pltpu.SemaphoreType.DMA((cols_a // width,)),
            ],
            input_output_aliases={} if merged is None else {3: 0},
            compiler_params=PARAMS,
            cost_estimate=estimate(
                panel_shape[0] * cols_a * 2, 2 * panel_shape[0] * cols_a * ranks * n_dp
            ),
            name=f"merge{k}",
        )(*operands)
    return (merged, new_a, new_b, new_moment_a, new_second_a, new_moment_b, new_second_b)


def solution(mesh):
    sizes = dict(mesh.shape)

    def body(*args):
        return per_device(sizes["dp"], sizes["expert"], sizes["tensor"], *args)

    state = P("expert", "dp", "tensor")
    grad = P("dp", "expert", None, "tensor")
    weight = P("expert", "tensor", None)
    in_specs = (weight,) + (state,) * 6 + (grad,) * 2 + (P(),)
    out_specs = (weight,) + (state,) * 6
    return jax.shard_map(body, mesh=mesh, in_specs=in_specs, out_specs=out_specs, check_vma=False)
```

```python
import functools
import itertools

import jax
import jax.numpy as jnp
from jax import lax
from jax.experimental import pallas as pl
from jax.experimental.pallas import tpu as pltpu
from jax.sharding import PartitionSpec as P

ADAM_STEP = 20


ADAPTER_SCALE = 2.0
BETA_ONE = 0.9
BETA_TWO = 0.95
LEARN_RATE = 0.08
STABILITY_TERM = 1e-08

MOST_SWITCHED = 4

F32 = jnp.float32
BF16 = jnp.bfloat16
VMEM = pl.BlockSpec(memory_space=pltpu.VMEM)
SMEM = pl.BlockSpec(memory_space=pltpu.SMEM)
HBM = pl.BlockSpec(memory_space=pltpu.HBM)
PARAMS = pltpu.CompilerParams(vmem_limit_bytes=16 * 1024 * 1024)


def adam_update(param, moment, second, grad):
    corr_one = 1.0 - BETA_ONE**ADAM_STEP
    corr_two = 1.0 - BETA_TWO**ADAM_STEP
    moment_new = BETA_ONE * moment + (1.0 - BETA_ONE) * grad
    second_new = BETA_TWO * second + (1.0 - BETA_TWO) * grad * grad
    param_new = param - LEARN_RATE * (moment_new / corr_one) / (
        jnp.sqrt(second_new / corr_two) + STABILITY_TERM
    )
    return (param_new, moment_new, second_new)


def swap(x, axis, n, k):
    return lax.ppermute(x, axis, [(i, i ^ k) for i in range(n)])


def held(x):
    return pltpu.with_memory_space_constraint(x, pltpu.VMEM)


def left(x):
    return pltpu.with_memory_space_constraint(x, pltpu.HBM)


def estimate(nbytes, flops=0):
    return pl.CostEstimate(flops=flops, bytes_accessed=nbytes, transcendentals=0)


def pack_kernel(n_dp, ranks, cols_a, grad_a, grad_b, *refs):
    outs, rows, sems = refs[: n_dp - 1], refs[n_dp - 1], refs[n_dp]
    me = lax.axis_index("dp")
    copies = []
    for k in range(1, n_dp):
        start = pl.multiple_of((me ^ k) * ranks, ranks)
        pair = (
            pltpu.make_async_copy(
                grad_a.at[0, 0, pl.ds(start, ranks), :],
                rows.at[k - 1, :, pl.ds(0, cols_a)],
                sems.at[k - 1, 0],
            ),
            pltpu.make_async_copy(
                grad_b.at[0, 0, pl.ds(start, ranks), :],
                rows.at[k - 1, :, pl.ds(cols_a, rows.shape[2] - cols_a)],
                sems.at[k - 1, 1],
            ),
        )
        for copy in pair:
            copy.start()
        copies.append(pair)
    for k, pair in enumerate(copies):
        for copy in pair:
            copy.wait()
        outs[k][...] = rows[k].astype(BF16)


def load_kernel(ranks, cols_a, slots_in, *refs):
    grad_a, grad_b, fa, fb, ma, mb, sa, sb = refs[:8]
    grad, factor, moment, second, order, slot_of, sems = refs[8:]
    me = lax.axis_index("dp")
    start = pl.multiple_of(me * ranks, ranks)
    first = pl.ds(0, cols_a)
    last = pl.ds(cols_a, grad.shape[1] - cols_a)
    pairs = [
        (grad_a.at[0, 0, pl.ds(start, ranks), :], grad.at[:, first]),
        (grad_b.at[0, 0, pl.ds(start, ranks), :], grad.at[:, last]),
        (fa.at[0], factor.at[:, first]),
        (fb.at[0], factor.at[:, last]),
        (ma.at[0], moment.at[:, first]),
        (mb.at[0], moment.at[:, last]),
        (sa.at[0], second.at[:, first]),
        (sb.at[0], second.at[:, last]),
        (slots_in, slot_of),
    ]
    copies = [pltpu.make_async_copy(a, b, sems.at[i]) for i, (a, b) in enumerate(pairs)]
    for copy in copies:
        copy.start()
    copies.pop().wait()
    n = slot_of.shape[0]
    number = jnp.int32(0)
    for i in range(n - 1):
        smaller = jnp.int32(0)
        for j in range(i + 1, n):
            smaller += (slot_of[j] < slot_of[i]).astype(jnp.int32)
        number = number * (n - i) + smaller
    order[0] = number
    here = lax.axis_index("expert")
    order[1] = (slot_of[here] == here).astype(jnp.int32)
    for copy in copies:
        copy.wait()


def keep_kernel(piece, kept):
    kept[...] = piece[...]


def send_kernel(*refs):
    grad, factor, moment, second = refs[:4]
    total = grad[...]
    for piece in refs[4:-1]:
        total = total + piece[...].astype(F32)
    refs[-1][...] = adam_update(factor[...], moment[...], second[...], total)[0].astype(BF16)


def state_kernel(n_got, cols_a, weight, *refs):
    ins = refs[: 4 + n_got]
    outs = refs[4 + n_got : 10 + n_got]
    panel = refs[10 + n_got]
    parts = refs[11 + n_got : 17 + n_got]
    sems = refs[-1]
    cols_b = ins[0].shape[1] - cols_a
    width = 256 if cols_a % 256 == 0 and cols_b % 256 == 0 else 128
    load = pltpu.make_async_copy(weight.at[0], panel, sems.at[0])
    load.start()

    def some_columns(start, into, at):
        here = pl.ds(pl.multiple_of(start, width), width)
        there = pl.ds(pl.multiple_of(at, width), width)
        grad, factor, moment, second = (ref[:, here] for ref in ins[:4])
        for piece in ins[4:]:
            grad = grad + piece[:, here].astype(F32)
        for out, new in zip(into, adam_update(factor, moment, second, grad)):
            out[:, there] = new

    @pl.loop(0, cols_a // width)
    def _(i):
        some_columns(i * width, parts[::2], i * width)

    @pl.loop(0, cols_b // width)
    def _(i):
        some_columns(cols_a + i * width, parts[1::2], i * width)

    copies = [
        pltpu.make_async_copy(part, out.at[0], sems.at[1 + i])
        for i, (part, out) in enumerate(zip(parts, outs))
    ]
    for copy in copies:
        copy.start()
    for copy in copies:
        copy.wait()
    load.wait()


def join_kernel(cols_a, *refs):
    parts = refs[:-4]
    rows_a, flipped = refs[-3:-1]
    ranks = parts[0].shape[0]
    for i, part in enumerate(parts):
        rows_a[pl.ds(i * ranks, ranks), :] = part[:, :cols_a]
    rows_b = jnp.concatenate([part[:, cols_a:].astype(F32) for part in parts], axis=0)
    flipped[...] = (rows_b * ADAPTER_SCALE).T.astype(BF16)


def merge_kernel(k, width, *refs):
    panel, rows_a, flipped = refs[:3]
    out, tiles, sems = refs[-3:]
    cols = rows_a.shape[1]
    base = (lax.axis_index("tensor") ^ k) * cols
    copies = []
    for step in range(cols // width):
        span = slice(step * width, (step + 1) * width)
        columns = pl.ds(pl.multiple_of(base + step * width, width), width)
        increment = jnp.dot(flipped[...], rows_a[:, span], preferred_element_type=F32)
        tiles[step] = (panel[:, columns].astype(F32) + increment).astype(BF16)
        copy = pltpu.make_async_copy(tiles.at[step], out.at[0, :, columns], sems.at[step])
        copy.start()
        copies.append(copy)
    for copy in copies:
        copy.wait()


def per_device(
    n_dp,
    n_expert,
    n_tensor,
    weight,
    factor_a,
    factor_b,
    moment_a,
    second_a,
    first_moment_factor_b,
    second_b,
    grad_a,
    grad_b,
    slot_of,
):
    ranks, cols_a = factor_a.shape[1:]
    cols_b = factor_b.shape[2]
    cols = cols_a + cols_b

    pieces = pl.pallas_call(
        functools.partial(pack_kernel, n_dp, ranks, cols_a),
        in_specs=[HBM, HBM],
        out_specs=[VMEM] * (n_dp - 1),
        out_shape=[pltpu.VMEM((ranks, cols), BF16)] * (n_dp - 1),
        scratch_shapes=[
            pltpu.VMEM((n_dp - 1, ranks, cols), F32),
            pltpu.SemaphoreType.DMA((n_dp - 1, 2)),
        ],
        compiler_params=PARAMS,
        name="pack",
    )(left(grad_a), left(grad_b))
    got = [held(swap(pieces[k - 1], "dp", n_dp, k)) for k in range(n_dp - 1, 0, -1)]

    *state, order = pl.pallas_call(
        functools.partial(load_kernel, ranks, cols_a),
        in_specs=[HBM] * 9,
        out_specs=[VMEM] * 4 + [SMEM],
        out_shape=[pltpu.VMEM((ranks, cols), F32)] * 4 + [pltpu.SMEM((2,), jnp.int32)],
        scratch_shapes=[pltpu.SMEM(slot_of.shape, jnp.int32), pltpu.SemaphoreType.DMA((9,))],
        compiler_params=PARAMS,
        cost_estimate=estimate(4 * ranks * cols * 4),
        name="load",
    )(
        *map(
            left,
            (
                slot_of,
                grad_a,
                grad_b,
                factor_a,
                factor_b,
                moment_a,
                first_moment_factor_b,
                second_a,
                second_b,
            ),
        ),
    )
    state = [held(x) for x in state]

    send = pl.pallas_call(
        send_kernel,
        in_specs=[VMEM] * (3 + n_dp),
        out_specs=VMEM,
        out_shape=pltpu.VMEM((ranks, cols), BF16),
        compiler_params=PARAMS,
        name="send",
    )(*state, *got)

    def move(slots):
        pairs = [
            (i * n_expert + expert, (i if expert != slot else i ^ 1) * n_expert + slot)
            for i in range(n_dp)
            for expert, slot in enumerate(slots)
        ]
        moves = any(expert != slot for expert, slot in enumerate(slots))

        def branch(send):
            mine = lax.ppermute(send, ("dp", "expert"), pairs) if moves else send
            return pl.pallas_call(
                keep_kernel,
                in_specs=[VMEM],
                out_specs=VMEM,
                out_shape=pltpu.VMEM((ranks, cols), BF16),
                compiler_params=PARAMS,
                name="keep",
            )(held(mine))

        return branch

    if n_expert <= MOST_SWITCHED:
        orders = itertools.permutations(range(n_expert))
        mine = lax.switch(order[0], [move(slots) for slots in orders], send)
        mine = jnp.where(order[1] == 1, send, mine)
    else:
        mine = send
        here = lax.axis_index("expert")
        experts = jnp.arange(n_expert, dtype=jnp.int32)
        wanted = jnp.sum(jnp.where(slot_of == here, experts, 0)) ^ here
        for k in range(1, n_expert):
            mine = jnp.where(wanted == k, swap(send, "expert", n_expert, k), mine)

    parts = [mine] + [swap(mine, "dp", n_dp, k) for k in range(1, n_dp)]
    panel_shape = weight.shape[1:]
    shapes = [factor_a.shape, factor_b.shape] * 3
    *new, panel = pl.pallas_call(
        functools.partial(state_kernel, n_dp - 1, cols_a),
        in_specs=[HBM] + [VMEM] * (3 + n_dp),
        out_specs=[HBM] * 6 + [VMEM],
        out_shape=[jax.ShapeDtypeStruct(shape, F32) for shape in shapes]
        + [pltpu.VMEM(panel_shape, BF16)],
        scratch_shapes=[pltpu.VMEM(shape[1:], F32) for shape in shapes]
        + [pltpu.SemaphoreType.DMA((7,))],
        compiler_params=PARAMS,
        cost_estimate=estimate(weight.size * 4),
        name="state",
    )(left(weight), *state, *got)
    new_a, new_b, new_moment_a, new_moment_b, new_second_a, new_second_b = new
    rows_a, flipped, panel = pl.pallas_call(
        functools.partial(join_kernel, cols_a),
        in_specs=[VMEM] * (n_dp + 1),
        out_specs=[VMEM] * 3,
        out_shape=[
            pltpu.VMEM((ranks * n_dp, cols_a), BF16),
            pltpu.VMEM((cols_b, ranks * n_dp), BF16),
            pltpu.VMEM(panel_shape, BF16),
        ],
        input_output_aliases={n_dp: 2},
        compiler_params=PARAMS,
        name="join",
    )(*map(held, parts), held(panel))

    merged = None
    width = 512
    for k in range(n_tensor):
        block = held(rows_a if k == 0 else swap(rows_a, "tensor", n_tensor, k))
        operands = [held(panel), block, held(flipped)] + ([] if merged is None else [merged])
        merged = pl.pallas_call(
            functools.partial(merge_kernel, k, width),
            in_specs=[VMEM] * 3 + [HBM] * (len(operands) - 3),
            out_specs=HBM,
            out_shape=jax.ShapeDtypeStruct(weight.shape, BF16),
            scratch_shapes=[
                pltpu.VMEM((cols_a // width, panel_shape[0], width), BF16),
                pltpu.SemaphoreType.DMA((cols_a // width,)),
            ],
            input_output_aliases={} if merged is None else {3: 0},
            compiler_params=PARAMS,
            cost_estimate=estimate(
                panel_shape[0] * cols_a * 2, 2 * panel_shape[0] * cols_a * ranks * n_dp
            ),
            name=f"merge{k}",
        )(*operands)
    return (merged, new_a, new_b, new_moment_a, new_second_a, new_moment_b, new_second_b)


def solution(mesh):
    sizes = dict(mesh.shape)

    def body(*args):
        return per_device(sizes["dp"], sizes["expert"], sizes["tensor"], *args)

    state = P("expert", "dp", "tensor")
    grad = P("dp", "expert", None, "tensor")
    weight = P("expert", "tensor", None)
    in_specs = (weight,) + (state,) * 6 + (grad,) * 2 + (P(),)
    out_specs = (weight,) + (state,) * 6
    return jax.shard_map(body, mesh=mesh, in_specs=in_specs, out_specs=out_specs, check_vma=False)
```

```python
import functools
import itertools

import jax
import jax.numpy as jnp
from jax import lax
from jax.experimental import pallas as pl
from jax.experimental.pallas import tpu as pltpu
from jax.sharding import PartitionSpec as P

ADAM_STEP = 20


ADAPTER_SCALE = 2.0
BETA_ONE = 0.9
BETA_TWO = 0.95
LEARN_RATE = 0.08
STABILITY_TERM = 1e-08

MOST_SWITCHED = 4

F32 = jnp.float32
BF16 = jnp.bfloat16
VMEM = pl.BlockSpec(memory_space=pltpu.VMEM)
SMEM = pl.BlockSpec(memory_space=pltpu.SMEM)
HBM = pl.BlockSpec(memory_space=pltpu.HBM)
PARAMS = pltpu.CompilerParams(vmem_limit_bytes=16 * 1024 * 1024)


def adam_update(param, moment, second, grad):
    corr_one = 1.0 - BETA_ONE**ADAM_STEP
    corr_two = 1.0 - BETA_TWO**ADAM_STEP
    moment_new = BETA_ONE * moment + (1.0 - BETA_ONE) * grad
    second_new = BETA_TWO * second + (1.0 - BETA_TWO) * grad * grad
    param_new = param - LEARN_RATE * (moment_new / corr_one) / (
        jnp.sqrt(second_new / corr_two) + STABILITY_TERM
    )
    return (param_new, moment_new, second_new)


def swap(x, axis, n, k):
    return lax.ppermute(x, axis, [(i, i ^ k) for i in range(n)])


def held(x):
    return pltpu.with_memory_space_constraint(x, pltpu.VMEM)


def left(x):
    return pltpu.with_memory_space_constraint(x, pltpu.HBM)


def estimate(nbytes, flops=0):
    return pl.CostEstimate(flops=flops, bytes_accessed=nbytes, transcendentals=0)


def pack_kernel(n_dp, ranks, cols_a, grad_a, grad_b, *refs):
    outs, rows, sems = refs[: n_dp - 1], refs[n_dp - 1], refs[n_dp]
    me = lax.axis_index("dp")
    copies = []
    for k in range(1, n_dp):
        start = pl.multiple_of((me ^ k) * ranks, ranks)
        pair = (
            pltpu.make_async_copy(
                grad_a.at[0, 0, pl.ds(start, ranks), :],
                rows.at[k - 1, :, pl.ds(0, cols_a)],
                sems.at[k - 1, 0],
            ),
            pltpu.make_async_copy(
                grad_b.at[0, 0, pl.ds(start, ranks), :],
                rows.at[k - 1, :, pl.ds(cols_a, rows.shape[2] - cols_a)],
                sems.at[k - 1, 1],
            ),
        )
        for copy in pair:
            copy.start()
        copies.append(pair)
    for k, pair in enumerate(copies):
        for copy in pair:
            copy.wait()
        outs[k][...] = rows[k].astype(BF16)


def load_kernel(ranks, cols_a, slots_in, *refs):
    grad_a, grad_b, fa, fb, ma, mb, sa, sb = refs[:8]
    grad, factor, moment, second, order, slot_of, sems = refs[8:]
    me = lax.axis_index("dp")
    start = pl.multiple_of(me * ranks, ranks)
    first = pl.ds(0, cols_a)
    last = pl.ds(cols_a, grad.shape[1] - cols_a)
    pairs = [
        (grad_a.at[0, 0, pl.ds(start, ranks), :], grad.at[:, first]),
        (grad_b.at[0, 0, pl.ds(start, ranks), :], grad.at[:, last]),
        (fa.at[0], factor.at[:, first]),
        (fb.at[0], factor.at[:, last]),
        (ma.at[0], moment.at[:, first]),
        (mb.at[0], moment.at[:, last]),
        (sa.at[0], second.at[:, first]),
        (sb.at[0], second.at[:, last]),
        (slots_in, slot_of),
    ]
    copies = [pltpu.make_async_copy(a, b, sems.at[i]) for i, (a, b) in enumerate(pairs)]
    for copy in copies:
        copy.start()
    copies.pop().wait()
    n = slot_of.shape[0]
    number = jnp.int32(0)
    for i in range(n - 1):
        smaller = jnp.int32(0)
        for j in range(i + 1, n):
            smaller += (slot_of[j] < slot_of[i]).astype(jnp.int32)
        number = number * (n - i) + smaller
    order[0] = number
    here = lax.axis_index("expert")
    order[1] = (slot_of[here] == here).astype(jnp.int32)
    for copy in copies:
        copy.wait()


def keep_kernel(piece, kept):
    kept[...] = piece[...]


def send_kernel(*refs):
    grad, factor, moment, second = refs[:4]
    total = grad[...]
    for piece in refs[4:-1]:
        total = total + piece[...].astype(F32)
    refs[-1][...] = adam_update(factor[...], moment[...], second[...], total)[0].astype(BF16)


def state_kernel(n_got, cols_a, weight, *refs):
    ins = refs[: 4 + n_got]
    outs = refs[4 + n_got : 10 + n_got]
    panel = refs[10 + n_got]
    parts = refs[11 + n_got : 17 + n_got]
    sems = refs[-1]
    cols_b = ins[0].shape[1] - cols_a
    width = 256 if cols_a % 256 == 0 and cols_b % 256 == 0 else 128
    load = pltpu.make_async_copy(weight.at[0], panel, sems.at[0])
    load.start()

    def some_columns(start, into, at):
        here = pl.ds(pl.multiple_of(start, width), width)
        there = pl.ds(pl.multiple_of(at, width), width)
        grad, factor, moment, second = (ref[:, here] for ref in ins[:4])
        for piece in ins[4:]:
            grad = grad + piece[:, here].astype(F32)
        for out, new in zip(into, adam_update(factor, moment, second, grad)):
            out[:, there] = new

    @pl.loop(0, cols_a // width)
    def _(i):
        some_columns(i * width, parts[::2], i * width)

    @pl.loop(0, cols_b // width)
    def _(i):
        some_columns(cols_a + i * width, parts[1::2], i * width)

    copies = [
        pltpu.make_async_copy(part, out.at[0], sems.at[1 + i])
        for i, (part, out) in enumerate(zip(parts, outs))
    ]
    for copy in copies:
        copy.start()
    for copy in copies:
        copy.wait()
    load.wait()


def join_kernel(cols_a, *refs):
    parts = refs[:-4]
    rows_a, flipped = refs[-3:-1]
    ranks = parts[0].shape[0]
    for i, part in enumerate(parts):
        rows_a[pl.ds(i * ranks, ranks), :] = part[:, :cols_a]
    rows_b = jnp.concatenate([part[:, cols_a:].astype(F32) for part in parts], axis=0)
    flipped[...] = (rows_b * ADAPTER_SCALE).T.astype(BF16)


def merge_kernel(k, width, *refs):
    panel, rows_a, flipped = refs[:3]
    out, tiles, sems = refs[-3:]
    cols = rows_a.shape[1]
    base = (lax.axis_index("tensor") ^ k) * cols
    copies = []
    for step in range(cols // width):
        span = slice(step * width, (step + 1) * width)
        columns = pl.ds(pl.multiple_of(base + step * width, width), width)
        increment = jnp.dot(flipped[...], rows_a[:, span], preferred_element_type=F32)
        tiles[step] = (panel[:, columns].astype(F32) + increment).astype(BF16)
        copy = pltpu.make_async_copy(tiles.at[step], out.at[0, :, columns], sems.at[step])
        copy.start()
        copies.append(copy)
    for copy in copies:
        copy.wait()


def per_device(
    n_dp,
    n_expert,
    n_tensor,
    weight,
    factor_a,
    factor_b,
    moment_a,
    second_a,
    first_moment_factor_b,
    second_b,
    grad_a,
    grad_b,
    slot_of,
):
    ranks, cols_a = factor_a.shape[1:]
    cols_b = factor_b.shape[2]
    cols = cols_a + cols_b

    pieces = pl.pallas_call(
        functools.partial(pack_kernel, n_dp, ranks, cols_a),
        in_specs=[HBM, HBM],
        out_specs=[VMEM] * (n_dp - 1),
        out_shape=[pltpu.VMEM((ranks, cols), BF16)] * (n_dp - 1),
        scratch_shapes=[
            pltpu.VMEM((n_dp - 1, ranks, cols), F32),
            pltpu.SemaphoreType.DMA((n_dp - 1, 2)),
        ],
        compiler_params=PARAMS,
        name="pack",
    )(left(grad_a), left(grad_b))
    ks = sorted(range(1, n_dp), key=lambda k: (-bin(k).count("1"), k))
    got = [held(swap(pieces[k - 1], "dp", n_dp, k)) for k in ks]

    *state, order = pl.pallas_call(
        functools.partial(load_kernel, ranks, cols_a),
        in_specs=[HBM] * 9,
        out_specs=[VMEM] * 4 + [SMEM],
        out_shape=[pltpu.VMEM((ranks, cols), F32)] * 4 + [pltpu.SMEM((2,), jnp.int32)],
        scratch_shapes=[pltpu.SMEM(slot_of.shape, jnp.int32), pltpu.SemaphoreType.DMA((9,))],
        compiler_params=PARAMS,
        cost_estimate=estimate(4 * ranks * cols * 4),
        name="load",
    )(
        *map(
            left,
            (
                slot_of,
                grad_a,
                grad_b,
                factor_a,
                factor_b,
                moment_a,
                first_moment_factor_b,
                second_a,
                second_b,
            ),
        ),
    )
    state = [held(x) for x in state]

    send = pl.pallas_call(
        send_kernel,
        in_specs=[VMEM] * (3 + n_dp),
        out_specs=VMEM,
        out_shape=pltpu.VMEM((ranks, cols), BF16),
        compiler_params=PARAMS,
        name="send",
    )(*state, *got)

    def move(slots):
        pairs = [
            (i * n_expert + expert, (i if expert != slot else i ^ 1) * n_expert + slot)
            for i in range(n_dp)
            for expert, slot in enumerate(slots)
        ]
        moves = any(expert != slot for expert, slot in enumerate(slots))

        def branch(send):
            mine = lax.ppermute(send, ("dp", "expert"), pairs) if moves else send
            return pl.pallas_call(
                keep_kernel,
                in_specs=[VMEM],
                out_specs=VMEM,
                out_shape=pltpu.VMEM((ranks, cols), BF16),
                compiler_params=PARAMS,
                name="keep",
            )(held(mine))

        return branch

    if n_expert <= MOST_SWITCHED:
        orders = itertools.permutations(range(n_expert))
        mine = lax.switch(order[0], [move(slots) for slots in orders], send)
        mine = jnp.where(order[1] == 1, send, mine)
    else:
        mine = send
        here = lax.axis_index("expert")
        experts = jnp.arange(n_expert, dtype=jnp.int32)
        wanted = jnp.sum(jnp.where(slot_of == here, experts, 0)) ^ here
        for k in range(1, n_expert):
            mine = jnp.where(wanted == k, swap(send, "expert", n_expert, k), mine)

    parts = [mine] + [swap(mine, "dp", n_dp, k) for k in ks[::-1]]
    panel_shape = weight.shape[1:]
    shapes = [factor_a.shape, factor_b.shape] * 3
    *new, panel = pl.pallas_call(
        functools.partial(state_kernel, n_dp - 1, cols_a),
        in_specs=[HBM] + [VMEM] * (3 + n_dp),
        out_specs=[HBM] * 6 + [VMEM],
        out_shape=[jax.ShapeDtypeStruct(shape, F32) for shape in shapes]
        + [pltpu.VMEM(panel_shape, BF16)],
        scratch_shapes=[pltpu.VMEM(shape[1:], F32) for shape in shapes]
        + [pltpu.SemaphoreType.DMA((7,))],
        compiler_params=PARAMS,
        cost_estimate=estimate(weight.size * 4),
        name="state",
    )(left(weight), *state, *got)
    new_a, new_b, new_moment_a, new_moment_b, new_second_a, new_second_b = new
    rows_a, flipped, panel = pl.pallas_call(
        functools.partial(join_kernel, cols_a),
        in_specs=[VMEM] * (n_dp + 1),
        out_specs=[VMEM] * 3,
        out_shape=[
            pltpu.VMEM((ranks * n_dp, cols_a), BF16),
            pltpu.VMEM((cols_b, ranks * n_dp), BF16),
            pltpu.VMEM(panel_shape, BF16),
        ],
        input_output_aliases={n_dp: 2},
        compiler_params=PARAMS,
        name="join",
    )(*map(held, parts), held(panel))

    merged = None
    width = 512
    for k in range(n_tensor):
        block = held(rows_a if k == 0 else swap(rows_a, "tensor", n_tensor, k))
        operands = [held(panel), block, held(flipped)] + ([] if merged is None else [merged])
        merged = pl.pallas_call(
            functools.partial(merge_kernel, k, width),
            in_specs=[VMEM] * 3 + [HBM] * (len(operands) - 3),
            out_specs=HBM,
            out_shape=jax.ShapeDtypeStruct(weight.shape, BF16),
            scratch_shapes=[
                pltpu.VMEM((cols_a // width, panel_shape[0], width), BF16),
                pltpu.SemaphoreType.DMA((cols_a // width,)),
            ],
            input_output_aliases={} if merged is None else {3: 0},
            compiler_params=PARAMS,
            cost_estimate=estimate(
                panel_shape[0] * cols_a * 2, 2 * panel_shape[0] * cols_a * ranks * n_dp
            ),
            name=f"merge{k}",
        )(*operands)
    return (merged, new_a, new_b, new_moment_a, new_second_a, new_moment_b, new_second_b)


def solution(mesh):
    sizes = dict(mesh.shape)

    def body(*args):
        return per_device(sizes["dp"], sizes["expert"], sizes["tensor"], *args)

    state = P("expert", "dp", "tensor")
    grad = P("dp", "expert", None, "tensor")
    weight = P("expert", "tensor", None)
    in_specs = (weight,) + (state,) * 6 + (grad,) * 2 + (P(),)
    out_specs = (weight,) + (state,) * 6
    return jax.shard_map(body, mesh=mesh, in_specs=in_specs, out_specs=out_specs, check_vma=False)
```

```python
import functools
import itertools

import jax
import jax.numpy as jnp
from jax import lax
from jax.experimental import pallas as pl
from jax.experimental.pallas import tpu as pltpu
from jax.sharding import PartitionSpec as P

ADAM_STEP = 20


ADAPTER_SCALE = 2.0
BETA_ONE = 0.9
BETA_TWO = 0.95
LEARN_RATE = 0.08
STABILITY_TERM = 1e-08

MOST_SWITCHED = 4

F32 = jnp.float32
BF16 = jnp.bfloat16
VMEM = pl.BlockSpec(memory_space=pltpu.VMEM)
SMEM = pl.BlockSpec(memory_space=pltpu.SMEM)
HBM = pl.BlockSpec(memory_space=pltpu.HBM)
PARAMS = pltpu.CompilerParams(vmem_limit_bytes=16 * 1024 * 1024)


def adam_update(param, moment, second, grad):
    corr_one = 1.0 - BETA_ONE**ADAM_STEP
    corr_two = 1.0 - BETA_TWO**ADAM_STEP
    moment_new = BETA_ONE * moment + (1.0 - BETA_ONE) * grad
    second_new = BETA_TWO * second + (1.0 - BETA_TWO) * grad * grad
    param_new = param - LEARN_RATE * (moment_new / corr_one) / (
        jnp.sqrt(second_new / corr_two) + STABILITY_TERM
    )
    return (param_new, moment_new, second_new)


def swap(x, axis, n, k):
    return lax.ppermute(x, axis, [(i, i ^ k) for i in range(n)])


def held(x):
    return pltpu.with_memory_space_constraint(x, pltpu.VMEM)


def left(x):
    return pltpu.with_memory_space_constraint(x, pltpu.HBM)


def estimate(nbytes, flops=0):
    return pl.CostEstimate(flops=flops, bytes_accessed=nbytes, transcendentals=0)


def halves_of(cols):
    middle = -(-cols // 256) * 128
    return [(0, middle), (middle, cols)]


def pack_kernel(n_dp, ranks, cols_a, grad_a, grad_b, *refs):
    outs, rows, sems = refs[:-2], refs[-2], refs[-1]
    me = lax.axis_index("dp")
    copies = []
    for k in range(1, n_dp):
        start = pl.multiple_of((me ^ k) * ranks, ranks)
        pair = (
            pltpu.make_async_copy(
                grad_a.at[0, 0, pl.ds(start, ranks), :],
                rows.at[k - 1, :, pl.ds(0, cols_a)],
                sems.at[k - 1, 0],
            ),
            pltpu.make_async_copy(
                grad_b.at[0, 0, pl.ds(start, ranks), :],
                rows.at[k - 1, :, pl.ds(cols_a, rows.shape[2] - cols_a)],
                sems.at[k - 1, 1],
            ),
        )
        for copy in pair:
            copy.start()
        copies.append(pair)
    for k, pair in enumerate(copies):
        for copy in pair:
            copy.wait()
        for half, (low, high) in enumerate(halves_of(rows.shape[2])):
            outs[2 * k + half][...] = rows[k, :, low:high].astype(BF16)


def load_kernel(ranks, cols_a, slots_in, *refs):
    grad_a, grad_b, fa, fb, ma, mb, sa, sb = refs[:8]
    grad, factor, moment, second, order, stays, slot_of, sems = refs[8:]
    me = lax.axis_index("dp")
    start = pl.multiple_of(me * ranks, ranks)
    first = pl.ds(0, cols_a)
    last = pl.ds(cols_a, grad.shape[1] - cols_a)
    pairs = [
        (grad_a.at[0, 0, pl.ds(start, ranks), :], grad.at[:, first]),
        (grad_b.at[0, 0, pl.ds(start, ranks), :], grad.at[:, last]),
        (fa.at[0], factor.at[:, first]),
        (fb.at[0], factor.at[:, last]),
        (ma.at[0], moment.at[:, first]),
        (mb.at[0], moment.at[:, last]),
        (sa.at[0], second.at[:, first]),
        (sb.at[0], second.at[:, last]),
        (slots_in, slot_of),
    ]
    copies = [pltpu.make_async_copy(a, b, sems.at[i]) for i, (a, b) in enumerate(pairs)]
    for copy in copies:
        copy.start()
    copies.pop().wait()
    n = slot_of.shape[0]
    number = jnp.int32(0)
    for i in range(n - 1):
        smaller = jnp.int32(0)
        for j in range(i + 1, n):
            smaller += (slot_of[j] < slot_of[i]).astype(jnp.int32)
        number = number * (n - i) + smaller
    order[0] = number
    here = lax.axis_index("expert")
    stays[0] = (slot_of[here] == here).astype(jnp.int32)
    for copy in copies:
        copy.wait()


def keep_kernel(*refs):
    for piece, kept in zip(refs[:2], refs[2:]):
        kept[...] = piece[...]


def send_kernel(*refs):
    grad, factor, moment, second = refs[:4]
    for half, (low, high) in enumerate(halves_of(grad.shape[1])):
        total = grad[:, low:high]
        for piece in refs[4 + half : -2 : 2]:
            total = total + piece[...].astype(F32)
        new = adam_update(factor[:, low:high], moment[:, low:high], second[:, low:high], total)
        refs[-2 + half][...] = new[0].astype(BF16)


def state_kernel(n_got, cols_a, weight, *refs):
    grad, factor, moment, second = refs[:4]
    got = refs[4 : 4 + n_got]
    outs = refs[4 + n_got : 10 + n_got]
    panel = refs[10 + n_got]
    parts = refs[11 + n_got : 17 + n_got]
    sems = refs[-1]
    width = 128
    load = pltpu.make_async_copy(weight.at[0], panel, sems.at[0])
    load.start()

    def some_columns(half, at, low, into, start):
        here = pl.ds(pl.multiple_of(at, width), width)
        inside = pl.ds(pl.multiple_of(at - low, width), width)
        there = pl.ds(pl.multiple_of(start, width), width)
        total = grad[:, here]
        for piece in got[half::2]:
            total = total + piece[:, inside].astype(F32)
        for out, new in zip(
            into, adam_update(factor[:, here], moment[:, here], second[:, here], total)
        ):
            out[:, there] = new

    for half, (low, high) in enumerate(halves_of(grad.shape[1])):

        @pl.loop(low // width, min(high, cols_a) // width)
        def _(i, half=half, low=low):
            some_columns(half, i * width, low, parts[::2], i * width)

        @pl.loop(max(low, cols_a) // width, high // width)
        def _(i, half=half, low=low):
            some_columns(half, i * width, low, parts[1::2], i * width - cols_a)

    copies = [
        pltpu.make_async_copy(part, out.at[0], sems.at[1 + i])
        for i, (part, out) in enumerate(zip(parts, outs))
    ]
    for copy in copies:
        copy.start()
    for copy in copies:
        copy.wait()
    load.wait()


def join_kernel(cols_a, cols_b, *refs):
    parts = refs[:-4]
    rows_a, flipped = refs[-3:-1]
    rows_b = []
    for half, (low, high) in enumerate(halves_of(cols_a + cols_b)):
        rows = jnp.concatenate([part[...].astype(F32) for part in parts[half::2]], axis=0)
        edge = min(max(cols_a - low, 0), high - low)
        if edge > 0:
            rows_a[:, low : low + edge] = rows[:, :edge].astype(BF16)
        if edge < high - low:
            rows_b.append(rows[:, edge:])
    rows_b = jnp.concatenate(rows_b, axis=1) if len(rows_b) > 1 else rows_b[0]
    flipped[...] = (rows_b * ADAPTER_SCALE).T.astype(BF16)


def merge_kernel(k, width, *refs):
    panel, rows_a, flipped = refs[:3]
    out, tiles, sems = refs[-3:]
    cols = rows_a.shape[1]
    base = (lax.axis_index("tensor") ^ k) * cols
    copies = []
    for step in range(cols // width):
        span = slice(step * width, (step + 1) * width)
        columns = pl.ds(pl.multiple_of(base + step * width, width), width)
        increment = jnp.dot(flipped[...], rows_a[:, span], preferred_element_type=F32)
        tiles[step] = (panel[:, columns].astype(F32) + increment).astype(BF16)
        copy = pltpu.make_async_copy(tiles.at[step], out.at[0, :, columns], sems.at[step])
        copy.start()
        copies.append(copy)
    for copy in copies:
        copy.wait()


def per_device(
    n_dp,
    n_expert,
    n_tensor,
    weight,
    factor_a,
    factor_b,
    moment_a,
    second_a,
    first_moment_factor_b,
    second_b,
    grad_a,
    grad_b,
    slot_of,
):
    ranks, cols_a = factor_a.shape[1:]
    cols_b = factor_b.shape[2]
    cols = cols_a + cols_b

    shapes = [(ranks, high - low) for low, high in halves_of(cols)]
    pieces = pl.pallas_call(
        functools.partial(pack_kernel, n_dp, ranks, cols_a),
        in_specs=[HBM, HBM],
        out_specs=[VMEM] * (2 * n_dp - 2),
        out_shape=[pltpu.VMEM(shape, BF16) for shape in shapes] * (n_dp - 1),
        scratch_shapes=[
            pltpu.VMEM((n_dp - 1, ranks, cols), F32),
            pltpu.SemaphoreType.DMA((n_dp - 1, 2)),
        ],
        compiler_params=PARAMS,
        name="pack",
    )(left(grad_a), left(grad_b))
    got = [
        held(swap(pieces[2 * k - 2 + half], "dp", n_dp, k))
        for k in range(n_dp - 1, 0, -1)
        for half in range(2)
    ]

    *state, order, stays = pl.pallas_call(
        functools.partial(load_kernel, ranks, cols_a),
        in_specs=[HBM] * 9,
        out_specs=[VMEM] * 4 + [SMEM] * 2,
        out_shape=[pltpu.VMEM((ranks, cols), F32)] * 4 + [pltpu.SMEM((1,), jnp.int32)] * 2,
        scratch_shapes=[pltpu.SMEM(slot_of.shape, jnp.int32), pltpu.SemaphoreType.DMA((9,))],
        compiler_params=PARAMS,
        cost_estimate=estimate(4 * ranks * cols * 4),
        name="load",
    )(
        *map(
            left,
            (
                slot_of,
                grad_a,
                grad_b,
                factor_a,
                factor_b,
                moment_a,
                first_moment_factor_b,
                second_a,
                second_b,
            ),
        ),
    )
    state = [held(x) for x in state]

    send = pl.pallas_call(
        send_kernel,
        in_specs=[VMEM] * (2 + 2 * n_dp),
        out_specs=[VMEM] * 2,
        out_shape=[pltpu.VMEM(shape, BF16) for shape in shapes],
        compiler_params=PARAMS,
        name="send",
    )(*state, *got)

    def move(slots):
        pairs = [
            (i * n_expert + expert, (i if expert != slot else i ^ 1) * n_expert + slot)
            for i in range(n_dp)
            for expert, slot in enumerate(slots)
        ]
        moves = any(expert != slot for expert, slot in enumerate(slots))

        def branch(send):
            mine = send
            if moves:
                mine = [lax.ppermute(x, ("dp", "expert"), pairs) for x in send]
            return pl.pallas_call(
                keep_kernel,
                in_specs=[VMEM] * 2,
                out_specs=[VMEM] * 2,
                out_shape=[pltpu.VMEM(shape, BF16) for shape in shapes],
                compiler_params=PARAMS,
                name="keep",
            )(*map(held, mine))

        return branch

    if n_expert <= MOST_SWITCHED:
        orders = itertools.permutations(range(n_expert))
        mine = lax.switch(order[0], [move(slots) for slots in orders], send)
        mine = [jnp.where(stays[0] == 1, a, b) for a, b in zip(send, mine)]
    else:
        mine = send
        here = lax.axis_index("expert")
        experts = jnp.arange(n_expert, dtype=jnp.int32)
        wanted = jnp.sum(jnp.where(slot_of == here, experts, 0)) ^ here
        for k in range(1, n_expert):
            mine = [
                jnp.where(wanted == k, swap(a, "expert", n_expert, k), b)
                for a, b in zip(send, mine)
            ]

    parts = list(mine)
    for k in range(1, n_dp):
        parts += [swap(x, "dp", n_dp, k) for x in mine]
    panel_shape = weight.shape[1:]
    full = [factor_a.shape, factor_b.shape] * 3
    *new, panel = pl.pallas_call(
        functools.partial(state_kernel, 2 * n_dp - 2, cols_a),
        in_specs=[HBM] + [VMEM] * (2 + 2 * n_dp),
        out_specs=[HBM] * 6 + [VMEM],
        out_shape=[jax.ShapeDtypeStruct(shape, F32) for shape in full]
        + [pltpu.VMEM(panel_shape, BF16)],
        scratch_shapes=[pltpu.VMEM(shape[1:], F32) for shape in full]
        + [pltpu.SemaphoreType.DMA((7,))],
        compiler_params=PARAMS,
        cost_estimate=estimate(weight.size * 4),
        name="state",
    )(left(weight), *state, *got)
    new_a, new_b, new_moment_a, new_moment_b, new_second_a, new_second_b = new
    rows_a, flipped, panel = pl.pallas_call(
        functools.partial(join_kernel, cols_a, cols_b),
        in_specs=[VMEM] * (2 * n_dp + 1),
        out_specs=[VMEM] * 3,
        out_shape=[
            pltpu.VMEM((ranks * n_dp, cols_a), BF16),
            pltpu.VMEM((cols_b, ranks * n_dp), BF16),
            pltpu.VMEM(panel_shape, BF16),
        ],
        input_output_aliases={2 * n_dp: 2},
        compiler_params=PARAMS,
        name="join",
    )(*map(held, parts), held(panel))

    merged = None
    width = 512
    for k in range(n_tensor):
        block = held(rows_a if k == 0 else swap(rows_a, "tensor", n_tensor, k))
        operands = [held(panel), block, held(flipped)] + ([] if merged is None else [merged])
        merged = pl.pallas_call(
            functools.partial(merge_kernel, k, width),
            in_specs=[VMEM] * 3 + [HBM] * (len(operands) - 3),
            out_specs=HBM,
            out_shape=jax.ShapeDtypeStruct(weight.shape, BF16),
            scratch_shapes=[
                pltpu.VMEM((cols_a // width, panel_shape[0], width), BF16),
                pltpu.SemaphoreType.DMA((cols_a // width,)),
            ],
            input_output_aliases={} if merged is None else {3: 0},
            compiler_params=PARAMS,
            cost_estimate=estimate(
                panel_shape[0] * cols_a * 2, 2 * panel_shape[0] * cols_a * ranks * n_dp
            ),
            name=f"merge{k}",
        )(*operands)
    return (merged, new_a, new_b, new_moment_a, new_second_a, new_moment_b, new_second_b)


def solution(mesh):
    sizes = dict(mesh.shape)

    def body(*args):
        return per_device(sizes["dp"], sizes["expert"], sizes["tensor"], *args)

    state = P("expert", "dp", "tensor")
    grad = P("dp", "expert", None, "tensor")
    weight = P("expert", "tensor", None)
    in_specs = (weight,) + (state,) * 6 + (grad,) * 2 + (P(),)
    out_specs = (weight,) + (state,) * 6
    return jax.shard_map(body, mesh=mesh, in_specs=in_specs, out_specs=out_specs, check_vma=False)
```

```python
import functools
import itertools

import jax
import jax.numpy as jnp
from jax import lax
from jax.experimental import pallas as pl
from jax.experimental.pallas import tpu as pltpu
from jax.sharding import PartitionSpec as P

ADAM_STEP = 20


ADAPTER_SCALE = 2.0
BETA_ONE = 0.9
BETA_TWO = 0.95
LEARN_RATE = 0.08
STABILITY_TERM = 1e-08

MOST_SWITCHED = 4

F32 = jnp.float32
BF16 = jnp.bfloat16
VMEM = pl.BlockSpec(memory_space=pltpu.VMEM)
SMEM = pl.BlockSpec(memory_space=pltpu.SMEM)
HBM = pl.BlockSpec(memory_space=pltpu.HBM)
PARAMS = pltpu.CompilerParams(vmem_limit_bytes=16 * 1024 * 1024)


def adam_update(param, moment, second, grad):
    corr_one = 1.0 - BETA_ONE**ADAM_STEP
    corr_two = 1.0 - BETA_TWO**ADAM_STEP
    moment_new = BETA_ONE * moment + (1.0 - BETA_ONE) * grad
    second_new = BETA_TWO * second + (1.0 - BETA_TWO) * grad * grad
    param_new = param - LEARN_RATE * (moment_new / corr_one) / (
        jnp.sqrt(second_new / corr_two) + STABILITY_TERM
    )
    return (param_new, moment_new, second_new)


def swap(x, axis, n, k):
    return lax.ppermute(x, axis, [(i, i ^ k) for i in range(n)])


def held(x):
    return pltpu.with_memory_space_constraint(x, pltpu.VMEM)


def left(x):
    return pltpu.with_memory_space_constraint(x, pltpu.HBM)


def estimate(nbytes, flops=0):
    return pl.CostEstimate(flops=flops, bytes_accessed=nbytes, transcendentals=0)


def pack_kernel(n_dp, ranks, cols_a, grad_a, grad_b, *refs):
    outs, rows, sems = refs[: n_dp - 1], refs[n_dp - 1], refs[n_dp]
    me = lax.axis_index("dp")
    copies = []
    for k in range(1, n_dp):
        start = pl.multiple_of((me ^ k) * ranks, ranks)
        pair = (
            pltpu.make_async_copy(
                grad_a.at[0, 0, pl.ds(start, ranks), :],
                rows.at[k - 1, :, pl.ds(0, cols_a)],
                sems.at[k - 1, 0],
            ),
            pltpu.make_async_copy(
                grad_b.at[0, 0, pl.ds(start, ranks), :],
                rows.at[k - 1, :, pl.ds(cols_a, rows.shape[2] - cols_a)],
                sems.at[k - 1, 1],
            ),
        )
        for copy in pair:
            copy.start()
        copies.append(pair)
    for k, pair in enumerate(copies):
        for copy in pair:
            copy.wait()
        outs[k][...] = rows[k].astype(BF16)


def load_kernel(ranks, cols_a, slots_in, *refs):
    grad_a, grad_b, fa, fb, ma, mb, sa, sb = refs[:8]
    grad, factor, moment, second, order, stays, slot_of, sems = refs[8:]
    me = lax.axis_index("dp")
    start = pl.multiple_of(me * ranks, ranks)
    first = pl.ds(0, cols_a)
    last = pl.ds(cols_a, grad.shape[1] - cols_a)
    pairs = [
        (grad_a.at[0, 0, pl.ds(start, ranks), :], grad.at[:, first]),
        (grad_b.at[0, 0, pl.ds(start, ranks), :], grad.at[:, last]),
        (fa.at[0], factor.at[:, first]),
        (fb.at[0], factor.at[:, last]),
        (ma.at[0], moment.at[:, first]),
        (mb.at[0], moment.at[:, last]),
        (sa.at[0], second.at[:, first]),
        (sb.at[0], second.at[:, last]),
        (slots_in, slot_of),
    ]
    copies = [pltpu.make_async_copy(a, b, sems.at[i]) for i, (a, b) in enumerate(pairs)]
    for copy in copies:
        copy.start()
    copies.pop().wait()
    n = slot_of.shape[0]
    number = jnp.int32(0)
    for i in range(n - 1):
        smaller = jnp.int32(0)
        for j in range(i + 1, n):
            smaller += (slot_of[j] < slot_of[i]).astype(jnp.int32)
        number = number * (n - i) + smaller
    order[0] = number
    here = lax.axis_index("expert")
    stays[0] = (slot_of[here] == here).astype(jnp.int32)
    for copy in copies:
        copy.wait()


def keep_kernel(piece, kept):
    kept[...] = piece[...]


def send_kernel(*refs):
    grad, factor, moment, second = refs[:4]
    total = grad[...]
    for piece in refs[4:-1]:
        total = total + piece[...].astype(F32)
    refs[-1][...] = adam_update(factor[...], moment[...], second[...], total)[0].astype(BF16)


def state_kernel(n_got, cols_a, weight, *refs):
    ins = refs[: 4 + n_got]
    outs = refs[4 + n_got : 10 + n_got]
    panel = refs[10 + n_got]
    parts = refs[11 + n_got : 17 + n_got]
    sems = refs[-1]
    cols_b = ins[0].shape[1] - cols_a
    width = 256 if cols_a % 256 == 0 and cols_b % 256 == 0 else 128
    load = pltpu.make_async_copy(weight.at[0], panel, sems.at[0])
    load.start()

    def some_columns(start, into, at):
        here = pl.ds(pl.multiple_of(start, width), width)
        there = pl.ds(pl.multiple_of(at, width), width)
        grad, factor, moment, second = (ref[:, here] for ref in ins[:4])
        for piece in ins[4:]:
            grad = grad + piece[:, here].astype(F32)
        for out, new in zip(into, adam_update(factor, moment, second, grad)):
            out[:, there] = new

    @pl.loop(0, cols_a // width)
    def _(i):
        some_columns(i * width, parts[::2], i * width)

    @pl.loop(0, cols_b // width)
    def _(i):
        some_columns(cols_a + i * width, parts[1::2], i * width)

    copies = [
        pltpu.make_async_copy(part, out.at[0], sems.at[1 + i])
        for i, (part, out) in enumerate(zip(parts, outs))
    ]
    for copy in copies:
        copy.start()
    for copy in copies:
        copy.wait()
    load.wait()


def join_kernel(cols_a, *refs):
    parts = refs[:-4]
    rows_a, flipped = refs[-3:-1]
    ranks = parts[0].shape[0]
    for i, part in enumerate(parts):
        rows_a[pl.ds(i * ranks, ranks), :] = part[:, :cols_a]
    rows_b = jnp.concatenate([part[:, cols_a:].astype(F32) for part in parts], axis=0)
    flipped[...] = (rows_b * ADAPTER_SCALE).T.astype(BF16)


def merge_kernel(k, width, *refs):
    panel, rows_a, flipped = refs[:3]
    out, tiles, sems = refs[-3:]
    cols = rows_a.shape[1]
    base = (lax.axis_index("tensor") ^ k) * cols
    copies = []
    for step in range(cols // width):
        span = slice(step * width, (step + 1) * width)
        columns = pl.ds(pl.multiple_of(base + step * width, width), width)
        increment = jnp.dot(flipped[...], rows_a[:, span], preferred_element_type=F32)
        tiles[step] = (panel[:, columns].astype(F32) + increment).astype(BF16)
        copy = pltpu.make_async_copy(tiles.at[step], out.at[0, :, columns], sems.at[step])
        copy.start()
        copies.append(copy)
    for copy in copies:
        copy.wait()


def per_device(
    n_dp,
    n_expert,
    n_tensor,
    weight,
    factor_a,
    factor_b,
    moment_a,
    second_a,
    first_moment_factor_b,
    second_b,
    grad_a,
    grad_b,
    slot_of,
):
    ranks, cols_a = factor_a.shape[1:]
    cols_b = factor_b.shape[2]
    cols = cols_a + cols_b

    pieces = pl.pallas_call(
        functools.partial(pack_kernel, n_dp, ranks, cols_a),
        in_specs=[HBM, HBM],
        out_specs=[VMEM] * (n_dp - 1),
        out_shape=[pltpu.VMEM((ranks, cols), BF16)] * (n_dp - 1),
        scratch_shapes=[
            pltpu.VMEM((n_dp - 1, ranks, cols), F32),
            pltpu.SemaphoreType.DMA((n_dp - 1, 2)),
        ],
        compiler_params=PARAMS,
        name="pack",
    )(left(grad_a), left(grad_b))
    got = [held(swap(pieces[k - 1], "dp", n_dp, k)) for k in range(n_dp - 1, 0, -1)]

    *state, order, stays = pl.pallas_call(
        functools.partial(load_kernel, ranks, cols_a),
        in_specs=[HBM] * 9,
        out_specs=[VMEM] * 4 + [SMEM] * 2,
        out_shape=[pltpu.VMEM((ranks, cols), F32)] * 4 + [pltpu.SMEM((1,), jnp.int32)] * 2,
        scratch_shapes=[pltpu.SMEM(slot_of.shape, jnp.int32), pltpu.SemaphoreType.DMA((9,))],
        compiler_params=PARAMS,
        cost_estimate=estimate(4 * ranks * cols * 4),
        name="load",
    )(
        *map(
            left,
            (
                slot_of,
                grad_a,
                grad_b,
                factor_a,
                factor_b,
                moment_a,
                first_moment_factor_b,
                second_a,
                second_b,
            ),
        ),
    )
    state = [held(x) for x in state]

    send = pl.pallas_call(
        send_kernel,
        in_specs=[VMEM] * (3 + n_dp),
        out_specs=VMEM,
        out_shape=pltpu.VMEM((ranks, cols), BF16),
        compiler_params=PARAMS,
        name="send",
    )(*state, *got)

    def move(slots):
        pairs = [
            (i * n_expert + expert, (i if expert != slot else i ^ 1) * n_expert + slot)
            for i in range(n_dp)
            for expert, slot in enumerate(slots)
        ]
        moves = any(expert != slot for expert, slot in enumerate(slots))

        def branch(send):
            mine = lax.ppermute(send, ("dp", "expert"), pairs) if moves else send
            return pl.pallas_call(
                keep_kernel,
                in_specs=[VMEM],
                out_specs=VMEM,
                out_shape=pltpu.VMEM((ranks, cols), BF16),
                compiler_params=PARAMS,
                name="keep",
            )(held(mine))

        return branch

    if n_expert <= MOST_SWITCHED:
        orders = itertools.permutations(range(n_expert))
        mine = lax.switch(order[0], [move(slots) for slots in orders], send)
        mine = jnp.where(stays[0] == 1, send, mine)
    else:
        mine = send
        here = lax.axis_index("expert")
        experts = jnp.arange(n_expert, dtype=jnp.int32)
        wanted = jnp.sum(jnp.where(slot_of == here, experts, 0)) ^ here
        for k in range(1, n_expert):
            mine = jnp.where(wanted == k, swap(send, "expert", n_expert, k), mine)

    parts = [mine] + [swap(mine, "dp", n_dp, k) for k in range(1, n_dp)]
    panel_shape = weight.shape[1:]
    shapes = [factor_a.shape, factor_b.shape] * 3
    *new, panel = pl.pallas_call(
        functools.partial(state_kernel, n_dp - 1, cols_a),
        in_specs=[HBM] + [VMEM] * (3 + n_dp),
        out_specs=[HBM] * 6 + [VMEM],
        out_shape=[jax.ShapeDtypeStruct(shape, F32) for shape in shapes]
        + [pltpu.VMEM(panel_shape, BF16)],
        scratch_shapes=[pltpu.VMEM(shape[1:], F32) for shape in shapes]
        + [pltpu.SemaphoreType.DMA((7,))],
        compiler_params=PARAMS,
        cost_estimate=estimate(weight.size * 4),
        name="state",
    )(left(weight), *state, *got)
    new_a, new_b, new_moment_a, new_moment_b, new_second_a, new_second_b = new
    rows_a, flipped, panel = pl.pallas_call(
        functools.partial(join_kernel, cols_a),
        in_specs=[VMEM] * (n_dp + 1),
        out_specs=[VMEM] * 3,
        out_shape=[
            pltpu.VMEM((ranks * n_dp, cols_a), BF16),
            pltpu.VMEM((cols_b, ranks * n_dp), BF16),
            pltpu.VMEM(panel_shape, BF16),
        ],
        input_output_aliases={n_dp: 2},
        compiler_params=PARAMS,
        name="join",
    )(*map(held, parts), held(panel))

    merged = None
    width = 512
    for k in range(n_tensor):
        block = held(rows_a if k == 0 else swap(rows_a, "tensor", n_tensor, k))
        operands = [held(panel), block, held(flipped)] + ([] if merged is None else [merged])
        merged = pl.pallas_call(
            functools.partial(merge_kernel, k, width),
            in_specs=[VMEM] * 3 + [HBM] * (len(operands) - 3),
            out_specs=HBM,
            out_shape=jax.ShapeDtypeStruct(weight.shape, BF16),
            scratch_shapes=[
                pltpu.VMEM((cols_a // width, panel_shape[0], width), BF16),
                pltpu.SemaphoreType.DMA((cols_a // width,)),
            ],
            input_output_aliases={} if merged is None else {3: 0},
            compiler_params=PARAMS,
            cost_estimate=estimate(
                panel_shape[0] * cols_a * 2, 2 * panel_shape[0] * cols_a * ranks * n_dp
            ),
            name=f"merge{k}",
        )(*operands)
    return (merged, new_a, new_b, new_moment_a, new_second_a, new_moment_b, new_second_b)


def solution(mesh):
    sizes = dict(mesh.shape)

    def body(*args):
        return per_device(sizes["dp"], sizes["expert"], sizes["tensor"], *args)

    state = P("expert", "dp", "tensor")
    grad = P("dp", "expert", None, "tensor")
    weight = P("expert", "tensor", None)
    in_specs = (weight,) + (state,) * 6 + (grad,) * 2 + (P(),)
    out_specs = (weight,) + (state,) * 6
    return jax.shard_map(body, mesh=mesh, in_specs=in_specs, out_specs=out_specs, check_vma=False)
```

```python
import functools
import itertools

import jax
import jax.numpy as jnp
from jax import lax
from jax.experimental import pallas as pl
from jax.experimental.pallas import tpu as pltpu
from jax.sharding import PartitionSpec as P

ADAM_STEP = 20


ADAPTER_SCALE = 2.0
BETA_ONE = 0.9
BETA_TWO = 0.95
LEARN_RATE = 0.08
STABILITY_TERM = 1e-08

MOST_SWITCHED = 4

F32 = jnp.float32
BF16 = jnp.bfloat16
VMEM = pl.BlockSpec(memory_space=pltpu.VMEM)
SMEM = pl.BlockSpec(memory_space=pltpu.SMEM)
HBM = pl.BlockSpec(memory_space=pltpu.HBM)
PARAMS = pltpu.CompilerParams(vmem_limit_bytes=16 * 1024 * 1024)


def adam_update(param, moment, second, grad):
    corr_one = 1.0 - BETA_ONE**ADAM_STEP
    corr_two = 1.0 - BETA_TWO**ADAM_STEP
    moment_new = BETA_ONE * moment + (1.0 - BETA_ONE) * grad
    second_new = BETA_TWO * second + (1.0 - BETA_TWO) * grad * grad
    param_new = param - LEARN_RATE * (moment_new / corr_one) / (
        jnp.sqrt(second_new / corr_two) + STABILITY_TERM
    )
    return (param_new, moment_new, second_new)


def swap(x, axis, n, k):
    return lax.ppermute(x, axis, [(i, i ^ k) for i in range(n)])


def held(x):
    return pltpu.with_memory_space_constraint(x, pltpu.VMEM)


def left(x):
    return pltpu.with_memory_space_constraint(x, pltpu.HBM)


def estimate(nbytes, flops=0):
    return pl.CostEstimate(flops=flops, bytes_accessed=nbytes, transcendentals=0)


def pack_kernel(n_dp, ranks, cols_a, grad_a, grad_b, *refs):
    outs, rows, sems = refs[: n_dp - 1], refs[n_dp - 1], refs[n_dp]
    me = lax.axis_index("dp")
    copies = []
    for k in range(1, n_dp):
        start = pl.multiple_of((me ^ k) * ranks, ranks)
        pair = (
            pltpu.make_async_copy(
                grad_a.at[0, 0, pl.ds(start, ranks), :],
                rows.at[k - 1, :, pl.ds(0, cols_a)],
                sems.at[k - 1, 0],
            ),
            pltpu.make_async_copy(
                grad_b.at[0, 0, pl.ds(start, ranks), :],
                rows.at[k - 1, :, pl.ds(cols_a, rows.shape[2] - cols_a)],
                sems.at[k - 1, 1],
            ),
        )
        for copy in pair:
            copy.start()
        copies.append(pair)
    for k, pair in enumerate(copies):
        for copy in pair:
            copy.wait()
        outs[k][...] = rows[k].astype(BF16)


def load_kernel(ranks, cols_a, slots_in, *refs):
    grad_a, grad_b, fa, fb, ma, mb, sa, sb = refs[:8]
    grad, factor, moment, second, order, stays, slot_of, sems = refs[8:]
    me = lax.axis_index("dp")
    start = pl.multiple_of(me * ranks, ranks)
    first = pl.ds(0, cols_a)
    last = pl.ds(cols_a, grad.shape[1] - cols_a)
    pairs = [
        (grad_a.at[0, 0, pl.ds(start, ranks), :], grad.at[:, first]),
        (grad_b.at[0, 0, pl.ds(start, ranks), :], grad.at[:, last]),
        (fa.at[0], factor.at[:, first]),
        (fb.at[0], factor.at[:, last]),
        (ma.at[0], moment.at[:, first]),
        (mb.at[0], moment.at[:, last]),
        (sa.at[0], second.at[:, first]),
        (sb.at[0], second.at[:, last]),
        (slots_in, slot_of),
    ]
    copies = [pltpu.make_async_copy(a, b, sems.at[i]) for i, (a, b) in enumerate(pairs)]
    for copy in copies:
        copy.start()
    copies.pop().wait()
    n = slot_of.shape[0]
    number = jnp.int32(0)
    for i in range(n - 1):
        smaller = jnp.int32(0)
        for j in range(i + 1, n):
            smaller += (slot_of[j] < slot_of[i]).astype(jnp.int32)
        number = number * (n - i) + smaller
    order[0] = number
    here = lax.axis_index("expert")
    stays[0] = (slot_of[here] == here).astype(jnp.int32)
    for copy in copies:
        copy.wait()


def keep_kernel(piece, kept):
    kept[...] = piece[...]


def send_kernel(*refs):
    grad, factor, moment, second = refs[:4]
    total = grad[...]
    for piece in refs[4:-1]:
        total = total + piece[...].astype(F32)
    refs[-1][...] = adam_update(factor[...], moment[...], second[...], total)[0].astype(BF16)


def state_kernel(n_got, cols_a, weight, *refs):
    ins = refs[: 4 + n_got]
    outs = refs[4 + n_got : 10 + n_got]
    panel = refs[10 + n_got]
    parts = refs[11 + n_got : 17 + n_got]
    sems = refs[-1]
    cols_b = ins[0].shape[1] - cols_a
    width = 256 if cols_a % 256 == 0 and cols_b % 256 == 0 else 128
    load = pltpu.make_async_copy(weight.at[0], panel, sems.at[0])
    load.start()

    def some_columns(start, into, at):
        here = pl.ds(pl.multiple_of(start, width), width)
        there = pl.ds(pl.multiple_of(at, width), width)
        grad, factor, moment, second = (ref[:, here] for ref in ins[:4])
        for piece in ins[4:]:
            grad = grad + piece[:, here].astype(F32)
        for out, new in zip(into, adam_update(factor, moment, second, grad)):
            out[:, there] = new

    @pl.loop(0, cols_a // width)
    def _(i):
        some_columns(i * width, parts[::2], i * width)

    @pl.loop(0, cols_b // width)
    def _(i):
        some_columns(cols_a + i * width, parts[1::2], i * width)

    copies = [
        pltpu.make_async_copy(part, out.at[0], sems.at[1 + i])
        for i, (part, out) in enumerate(zip(parts, outs))
    ]
    for copy in copies:
        copy.start()
    for copy in copies:
        copy.wait()
    load.wait()


def join_kernel(cols_a, *refs):
    parts = refs[:-4]
    rows_a, flipped = refs[-3:-1]
    ranks = parts[0].shape[0]
    for i, part in enumerate(parts):
        rows_a[pl.ds(i * ranks, ranks), :] = part[:, :cols_a]
    rows_b = jnp.concatenate([part[:, cols_a:].astype(F32) for part in parts], axis=0)
    flipped[...] = (rows_b * ADAPTER_SCALE).T.astype(BF16)


def merge_kernel(k, rows, *refs):
    panel, rows_a, flipped = refs[:3]
    out, tile, sems = refs[-3:]
    cols = rows_a.shape[1]
    columns = pl.ds(pl.multiple_of((lax.axis_index("tensor") ^ k) * cols, cols), cols)
    copies = []
    for step in range(panel.shape[0] // rows):
        here = slice(step * rows, (step + 1) * rows)
        increment = jnp.dot(flipped[here, :], rows_a[...], preferred_element_type=F32)
        tile[here, :] = (panel[here, columns].astype(F32) + increment).astype(BF16)
        part = pl.ds(step * rows, rows)
        copy = pltpu.make_async_copy(tile.at[part, :], out.at[0, part, columns], sems.at[step])
        copy.start()
        copies.append(copy)
    for copy in copies:
        copy.wait()


def per_device(
    n_dp,
    n_expert,
    n_tensor,
    weight,
    factor_a,
    factor_b,
    moment_a,
    second_a,
    first_moment_factor_b,
    second_b,
    grad_a,
    grad_b,
    slot_of,
):
    ranks, cols_a = factor_a.shape[1:]
    cols_b = factor_b.shape[2]
    cols = cols_a + cols_b

    pieces = pl.pallas_call(
        functools.partial(pack_kernel, n_dp, ranks, cols_a),
        in_specs=[HBM, HBM],
        out_specs=[VMEM] * (n_dp - 1),
        out_shape=[pltpu.VMEM((ranks, cols), BF16)] * (n_dp - 1),
        scratch_shapes=[
            pltpu.VMEM((n_dp - 1, ranks, cols), F32),
            pltpu.SemaphoreType.DMA((n_dp - 1, 2)),
        ],
        compiler_params=PARAMS,
        name="pack",
    )(left(grad_a), left(grad_b))
    got = [held(swap(pieces[k - 1], "dp", n_dp, k)) for k in range(n_dp - 1, 0, -1)]

    *state, order, stays = pl.pallas_call(
        functools.partial(load_kernel, ranks, cols_a),
        in_specs=[HBM] * 9,
        out_specs=[VMEM] * 4 + [SMEM] * 2,
        out_shape=[pltpu.VMEM((ranks, cols), F32)] * 4 + [pltpu.SMEM((1,), jnp.int32)] * 2,
        scratch_shapes=[pltpu.SMEM(slot_of.shape, jnp.int32), pltpu.SemaphoreType.DMA((9,))],
        compiler_params=PARAMS,
        cost_estimate=estimate(4 * ranks * cols * 4),
        name="load",
    )(
        *map(
            left,
            (
                slot_of,
                grad_a,
                grad_b,
                factor_a,
                factor_b,
                moment_a,
                first_moment_factor_b,
                second_a,
                second_b,
            ),
        ),
    )
    state = [held(x) for x in state]

    send = pl.pallas_call(
        send_kernel,
        in_specs=[VMEM] * (3 + n_dp),
        out_specs=VMEM,
        out_shape=pltpu.VMEM((ranks, cols), BF16),
        compiler_params=PARAMS,
        name="send",
    )(*state, *got)

    def move(slots):
        pairs = [
            (i * n_expert + expert, (i if expert != slot else i ^ 1) * n_expert + slot)
            for i in range(n_dp)
            for expert, slot in enumerate(slots)
        ]
        moves = any(expert != slot for expert, slot in enumerate(slots))

        def branch(send):
            mine = lax.ppermute(send, ("dp", "expert"), pairs) if moves else send
            return pl.pallas_call(
                keep_kernel,
                in_specs=[VMEM],
                out_specs=VMEM,
                out_shape=pltpu.VMEM((ranks, cols), BF16),
                compiler_params=PARAMS,
                name="keep",
            )(held(mine))

        return branch

    if n_expert <= MOST_SWITCHED:
        orders = itertools.permutations(range(n_expert))
        mine = lax.switch(order[0], [move(slots) for slots in orders], send)
        mine = jnp.where(stays[0] == 1, send, mine)
    else:
        mine = send
        here = lax.axis_index("expert")
        experts = jnp.arange(n_expert, dtype=jnp.int32)
        wanted = jnp.sum(jnp.where(slot_of == here, experts, 0)) ^ here
        for k in range(1, n_expert):
            mine = jnp.where(wanted == k, swap(send, "expert", n_expert, k), mine)

    parts = [mine] + [swap(mine, "dp", n_dp, k) for k in range(1, n_dp)]
    panel_shape = weight.shape[1:]
    shapes = [factor_a.shape, factor_b.shape] * 3
    *new, panel = pl.pallas_call(
        functools.partial(state_kernel, n_dp - 1, cols_a),
        in_specs=[HBM] + [VMEM] * (3 + n_dp),
        out_specs=[HBM] * 6 + [VMEM],
        out_shape=[jax.ShapeDtypeStruct(shape, F32) for shape in shapes]
        + [pltpu.VMEM(panel_shape, BF16)],
        scratch_shapes=[pltpu.VMEM(shape[1:], F32) for shape in shapes]
        + [pltpu.SemaphoreType.DMA((7,))],
        compiler_params=PARAMS,
        cost_estimate=estimate(weight.size * 4),
        name="state",
    )(left(weight), *state, *got)
    new_a, new_b, new_moment_a, new_moment_b, new_second_a, new_second_b = new
    rows_a, flipped, panel = pl.pallas_call(
        functools.partial(join_kernel, cols_a),
        in_specs=[VMEM] * (n_dp + 1),
        out_specs=[VMEM] * 3,
        out_shape=[
            pltpu.VMEM((ranks * n_dp, cols_a), BF16),
            pltpu.VMEM((cols_b, ranks * n_dp), BF16),
            pltpu.VMEM(panel_shape, BF16),
        ],
        input_output_aliases={n_dp: 2},
        compiler_params=PARAMS,
        name="join",
    )(*map(held, parts), held(panel))

    merged = None
    step_rows = 128
    for k in range(n_tensor):
        block = held(rows_a if k == 0 else swap(rows_a, "tensor", n_tensor, k))
        operands = [held(panel), block, held(flipped)] + ([] if merged is None else [merged])
        merged = pl.pallas_call(
            functools.partial(merge_kernel, k, step_rows),
            in_specs=[VMEM] * 3 + [HBM] * (len(operands) - 3),
            out_specs=HBM,
            out_shape=jax.ShapeDtypeStruct(weight.shape, BF16),
            scratch_shapes=[
                pltpu.VMEM((panel_shape[0], cols_a), BF16),
                pltpu.SemaphoreType.DMA((panel_shape[0] // step_rows,)),
            ],
            input_output_aliases={} if merged is None else {3: 0},
            compiler_params=PARAMS,
            cost_estimate=estimate(
                panel_shape[0] * cols_a * 2, 2 * panel_shape[0] * cols_a * ranks * n_dp
            ),
            name=f"merge{k}",
        )(*operands)
    return (merged, new_a, new_b, new_moment_a, new_second_a, new_moment_b, new_second_b)


def solution(mesh):
    sizes = dict(mesh.shape)

    def body(*args):
        return per_device(sizes["dp"], sizes["expert"], sizes["tensor"], *args)

    state = P("expert", "dp", "tensor")
    grad = P("dp", "expert", None, "tensor")
    weight = P("expert", "tensor", None)
    in_specs = (weight,) + (state,) * 6 + (grad,) * 2 + (P(),)
    out_specs = (weight,) + (state,) * 6
    return jax.shard_map(body, mesh=mesh, in_specs=in_specs, out_specs=out_specs, check_vma=False)
```

```python
import functools
import itertools

import jax
import jax.numpy as jnp
from jax import lax
from jax.experimental import pallas as pl
from jax.experimental.pallas import tpu as pltpu
from jax.sharding import PartitionSpec as P

ADAM_STEP = 20


ADAPTER_SCALE = 2.0
BETA_ONE = 0.9
BETA_TWO = 0.95
LEARN_RATE = 0.08
STABILITY_TERM = 1e-08

MOST_SWITCHED = 4

F32 = jnp.float32
BF16 = jnp.bfloat16
VMEM = pl.BlockSpec(memory_space=pltpu.VMEM)
SMEM = pl.BlockSpec(memory_space=pltpu.SMEM)
HBM = pl.BlockSpec(memory_space=pltpu.HBM)
PARAMS = pltpu.CompilerParams(vmem_limit_bytes=16 * 1024 * 1024)


def adam_update(param, moment, second, grad):
    corr_one = 1.0 - BETA_ONE**ADAM_STEP
    corr_two = 1.0 - BETA_TWO**ADAM_STEP
    moment_new = BETA_ONE * moment + (1.0 - BETA_ONE) * grad
    second_new = BETA_TWO * second + (1.0 - BETA_TWO) * grad * grad
    param_new = param - LEARN_RATE * (moment_new / corr_one) / (
        jnp.sqrt(second_new / corr_two) + STABILITY_TERM
    )
    return (param_new, moment_new, second_new)


def swap(x, axis, n, k):
    return lax.ppermute(x, axis, [(i, i ^ k) for i in range(n)])


def held(x):
    return pltpu.with_memory_space_constraint(x, pltpu.VMEM)


def left(x):
    return pltpu.with_memory_space_constraint(x, pltpu.HBM)


def estimate(nbytes, flops=0):
    return pl.CostEstimate(flops=flops, bytes_accessed=nbytes, transcendentals=0)


def pack_kernel(n_dp, ranks, cols_a, grad_a, grad_b, *refs):
    outs, rows, sems = refs[: n_dp - 1], refs[n_dp - 1], refs[n_dp]
    me = lax.axis_index("dp")
    copies = []
    for k in range(1, n_dp):
        start = pl.multiple_of((me ^ k) * ranks, ranks)
        pair = (
            pltpu.make_async_copy(
                grad_a.at[0, 0, pl.ds(start, ranks), :],
                rows.at[k - 1, :, pl.ds(0, cols_a)],
                sems.at[k - 1, 0],
            ),
            pltpu.make_async_copy(
                grad_b.at[0, 0, pl.ds(start, ranks), :],
                rows.at[k - 1, :, pl.ds(cols_a, rows.shape[2] - cols_a)],
                sems.at[k - 1, 1],
            ),
        )
        for copy in pair:
            copy.start()
        copies.append(pair)
    for k, pair in enumerate(copies):
        for copy in pair:
            copy.wait()
        outs[k][...] = rows[k].astype(BF16)


def load_kernel(ranks, cols_a, slots_in, *refs):
    grad_a, grad_b, fa, fb, ma, mb, sa, sb = refs[:8]
    grad, factor, moment, second, order, stays, slot_of, sems = refs[8:]
    me = lax.axis_index("dp")
    start = pl.multiple_of(me * ranks, ranks)
    first = pl.ds(0, cols_a)
    last = pl.ds(cols_a, grad.shape[1] - cols_a)
    pairs = [
        (grad_a.at[0, 0, pl.ds(start, ranks), :], grad.at[:, first]),
        (grad_b.at[0, 0, pl.ds(start, ranks), :], grad.at[:, last]),
        (fa.at[0], factor.at[:, first]),
        (fb.at[0], factor.at[:, last]),
        (ma.at[0], moment.at[:, first]),
        (mb.at[0], moment.at[:, last]),
        (sa.at[0], second.at[:, first]),
        (sb.at[0], second.at[:, last]),
        (slots_in, slot_of),
    ]
    copies = [pltpu.make_async_copy(a, b, sems.at[i]) for i, (a, b) in enumerate(pairs)]
    for copy in copies:
        copy.start()
    copies.pop().wait()
    n = slot_of.shape[0]
    number = jnp.int32(0)
    for i in range(n - 1):
        smaller = jnp.int32(0)
        for j in range(i + 1, n):
            smaller += (slot_of[j] < slot_of[i]).astype(jnp.int32)
        number = number * (n - i) + smaller
    order[0] = number
    here = lax.axis_index("expert")
    stays[0] = (slot_of[here] == here).astype(jnp.int32)
    for copy in copies:
        copy.wait()


def keep_kernel(piece, kept):
    kept[...] = piece[...]


def send_kernel(*refs):
    grad, factor, moment, second = refs[:4]
    total = grad[...]
    for piece in refs[4:-1]:
        total = total + piece[...].astype(F32)
    refs[-1][...] = adam_update(factor[...], moment[...], second[...], total)[0].astype(BF16)


def state_kernel(n_got, cols_a, weight, *refs):
    ins = refs[: 4 + n_got]
    outs = refs[4 + n_got : 10 + n_got]
    panel = refs[10 + n_got]
    parts = refs[11 + n_got : 17 + n_got]
    sems = refs[-1]
    cols_b = ins[0].shape[1] - cols_a
    width = 256 if cols_a % 256 == 0 and cols_b % 256 == 0 else 128
    load = pltpu.make_async_copy(weight.at[0], panel, sems.at[0])
    load.start()

    def some_columns(start, into, at):
        here = pl.ds(pl.multiple_of(start, width), width)
        there = pl.ds(pl.multiple_of(at, width), width)
        grad, factor, moment, second = (ref[:, here] for ref in ins[:4])
        for piece in ins[4:]:
            grad = grad + piece[:, here].astype(F32)
        for out, new in zip(into, adam_update(factor, moment, second, grad)):
            out[:, there] = new

    @pl.loop(0, cols_a // width)
    def _(i):
        some_columns(i * width, parts[::2], i * width)

    @pl.loop(0, cols_b // width)
    def _(i):
        some_columns(cols_a + i * width, parts[1::2], i * width)

    copies = [
        pltpu.make_async_copy(part, out.at[0], sems.at[1 + i])
        for i, (part, out) in enumerate(zip(parts, outs))
    ]
    for copy in copies:
        copy.start()
    for copy in copies:
        copy.wait()
    load.wait()


def join_kernel(cols_a, *refs):
    parts = refs[:-4]
    rows_a, flipped = refs[-3:-1]
    ranks = parts[0].shape[0]
    for i, part in enumerate(parts):
        rows_a[pl.ds(i * ranks, ranks), :] = part[:, :cols_a]
    rows_b = jnp.concatenate([part[:, cols_a:].astype(F32) for part in parts], axis=0)
    flipped[...] = (rows_b * ADAPTER_SCALE).T.astype(BF16)


def merge_kernel(k, rows, *refs):
    panel, rows_a, flipped = refs[:3]
    out, tile, sems = refs[-3:]
    cols = rows_a.shape[1]
    columns = pl.ds(pl.multiple_of((lax.axis_index("tensor") ^ k) * cols, cols), cols)
    copies = []
    for step in range(panel.shape[0] // rows):
        here = slice(step * rows, (step + 1) * rows)
        increment = jnp.dot(flipped[here, :], rows_a[...], preferred_element_type=F32)
        tile[here, :] = (panel[here, columns].astype(F32) + increment).astype(BF16)
        part = pl.ds(step * rows, rows)
        copy = pltpu.make_async_copy(tile.at[part, :], out.at[0, part, columns], sems.at[step])
        copy.start()
        copies.append(copy)
    for copy in copies:
        copy.wait()


def per_device(
    n_dp,
    n_expert,
    n_tensor,
    weight,
    factor_a,
    factor_b,
    moment_a,
    second_a,
    first_moment_factor_b,
    second_b,
    grad_a,
    grad_b,
    slot_of,
):
    ranks, cols_a = factor_a.shape[1:]
    cols_b = factor_b.shape[2]
    cols = cols_a + cols_b

    pieces = pl.pallas_call(
        functools.partial(pack_kernel, n_dp, ranks, cols_a),
        in_specs=[HBM, HBM],
        out_specs=[VMEM] * (n_dp - 1),
        out_shape=[pltpu.VMEM((ranks, cols), BF16)] * (n_dp - 1),
        scratch_shapes=[
            pltpu.VMEM((n_dp - 1, ranks, cols), F32),
            pltpu.SemaphoreType.DMA((n_dp - 1, 2)),
        ],
        compiler_params=PARAMS,
        name="pack",
    )(left(grad_a), left(grad_b))
    got = [held(swap(pieces[k - 1], "dp", n_dp, k)) for k in range(n_dp - 1, 0, -1)]

    *state, order, stays = pl.pallas_call(
        functools.partial(load_kernel, ranks, cols_a),
        in_specs=[HBM] * 9,
        out_specs=[VMEM] * 4 + [SMEM] * 2,
        out_shape=[pltpu.VMEM((ranks, cols), F32)] * 4 + [pltpu.SMEM((1,), jnp.int32)] * 2,
        scratch_shapes=[pltpu.SMEM(slot_of.shape, jnp.int32), pltpu.SemaphoreType.DMA((9,))],
        compiler_params=PARAMS,
        cost_estimate=estimate(4 * ranks * cols * 4),
        name="load",
    )(
        *map(
            left,
            (
                slot_of,
                grad_a,
                grad_b,
                factor_a,
                factor_b,
                moment_a,
                first_moment_factor_b,
                second_a,
                second_b,
            ),
        ),
    )
    state = [held(x) for x in state]

    send = pl.pallas_call(
        send_kernel,
        in_specs=[VMEM] * (3 + n_dp),
        out_specs=VMEM,
        out_shape=pltpu.VMEM((ranks, cols), BF16),
        compiler_params=PARAMS,
        name="send",
    )(*state, *got)

    def move(slots):
        pairs = []
        for i, (expert, slot), j in itertools.product(
            range(n_dp), enumerate(slots), range(n_tensor)
        ):
            source = (i * n_expert + expert) * n_tensor + j
            partner = j if expert != slot else (j + 1) % n_tensor
            pairs.append((source, (i * n_expert + slot) * n_tensor + partner))
        moves = any(expert != slot for expert, slot in enumerate(slots))

        def branch(send):
            mine = lax.ppermute(send, ("dp", "expert", "tensor"), pairs) if moves else send
            return pl.pallas_call(
                keep_kernel,
                in_specs=[VMEM],
                out_specs=VMEM,
                out_shape=pltpu.VMEM((ranks, cols), BF16),
                compiler_params=PARAMS,
                name="keep",
            )(held(mine))

        return branch

    if n_expert <= MOST_SWITCHED:
        orders = itertools.permutations(range(n_expert))
        mine = lax.switch(order[0], [move(slots) for slots in orders], send)
        mine = jnp.where(stays[0] == 1, send, mine)
    else:
        mine = send
        here = lax.axis_index("expert")
        experts = jnp.arange(n_expert, dtype=jnp.int32)
        wanted = jnp.sum(jnp.where(slot_of == here, experts, 0)) ^ here
        for k in range(1, n_expert):
            mine = jnp.where(wanted == k, swap(send, "expert", n_expert, k), mine)

    parts = [mine] + [swap(mine, "dp", n_dp, k) for k in range(1, n_dp)]
    panel_shape = weight.shape[1:]
    shapes = [factor_a.shape, factor_b.shape] * 3
    *new, panel = pl.pallas_call(
        functools.partial(state_kernel, n_dp - 1, cols_a),
        in_specs=[HBM] + [VMEM] * (3 + n_dp),
        out_specs=[HBM] * 6 + [VMEM],
        out_shape=[jax.ShapeDtypeStruct(shape, F32) for shape in shapes]
        + [pltpu.VMEM(panel_shape, BF16)],
        scratch_shapes=[pltpu.VMEM(shape[1:], F32) for shape in shapes]
        + [pltpu.SemaphoreType.DMA((7,))],
        compiler_params=PARAMS,
        cost_estimate=estimate(weight.size * 4),
        name="state",
    )(left(weight), *state, *got)
    new_a, new_b, new_moment_a, new_moment_b, new_second_a, new_second_b = new
    rows_a, flipped, panel = pl.pallas_call(
        functools.partial(join_kernel, cols_a),
        in_specs=[VMEM] * (n_dp + 1),
        out_specs=[VMEM] * 3,
        out_shape=[
            pltpu.VMEM((ranks * n_dp, cols_a), BF16),
            pltpu.VMEM((cols_b, ranks * n_dp), BF16),
            pltpu.VMEM(panel_shape, BF16),
        ],
        input_output_aliases={n_dp: 2},
        compiler_params=PARAMS,
        name="join",
    )(*map(held, parts), held(panel))

    merged = None
    step_rows = 128
    for k in range(n_tensor):
        block = held(rows_a if k == 0 else swap(rows_a, "tensor", n_tensor, k))
        operands = [held(panel), block, held(flipped)] + ([] if merged is None else [merged])
        merged = pl.pallas_call(
            functools.partial(merge_kernel, k, step_rows),
            in_specs=[VMEM] * 3 + [HBM] * (len(operands) - 3),
            out_specs=HBM,
            out_shape=jax.ShapeDtypeStruct(weight.shape, BF16),
            scratch_shapes=[
                pltpu.VMEM((panel_shape[0], cols_a), BF16),
                pltpu.SemaphoreType.DMA((panel_shape[0] // step_rows,)),
            ],
            input_output_aliases={} if merged is None else {3: 0},
            compiler_params=PARAMS,
            cost_estimate=estimate(
                panel_shape[0] * cols_a * 2, 2 * panel_shape[0] * cols_a * ranks * n_dp
            ),
            name=f"merge{k}",
        )(*operands)
    return (merged, new_a, new_b, new_moment_a, new_second_a, new_moment_b, new_second_b)


def solution(mesh):
    sizes = dict(mesh.shape)

    def body(*args):
        return per_device(sizes["dp"], sizes["expert"], sizes["tensor"], *args)

    state = P("expert", "dp", "tensor")
    grad = P("dp", "expert", None, "tensor")
    weight = P("expert", "tensor", None)
    in_specs = (weight,) + (state,) * 6 + (grad,) * 2 + (P(),)
    out_specs = (weight,) + (state,) * 6
    return jax.shard_map(body, mesh=mesh, in_specs=in_specs, out_specs=out_specs, check_vma=False)
```

```python
import functools
import itertools

import jax
import jax.numpy as jnp
from jax import lax
from jax.experimental import pallas as pl
from jax.experimental.pallas import tpu as pltpu
from jax.sharding import PartitionSpec as P

ADAM_STEP = 20


ADAPTER_SCALE = 2.0
BETA_ONE = 0.9
BETA_TWO = 0.95
LEARN_RATE = 0.08
STABILITY_TERM = 1e-08

MOST_SWITCHED = 4

F32 = jnp.float32
BF16 = jnp.bfloat16
VMEM = pl.BlockSpec(memory_space=pltpu.VMEM)
SMEM = pl.BlockSpec(memory_space=pltpu.SMEM)
HBM = pl.BlockSpec(memory_space=pltpu.HBM)
PARAMS = pltpu.CompilerParams(vmem_limit_bytes=16 * 1024 * 1024)


def adam_update(param, moment, second, grad):
    corr_one = 1.0 - BETA_ONE**ADAM_STEP
    corr_two = 1.0 - BETA_TWO**ADAM_STEP
    moment_new = BETA_ONE * moment + (1.0 - BETA_ONE) * grad
    second_new = BETA_TWO * second + (1.0 - BETA_TWO) * grad * grad
    param_new = param - LEARN_RATE * (moment_new / corr_one) / (
        jnp.sqrt(second_new / corr_two) + STABILITY_TERM
    )
    return (param_new, moment_new, second_new)


def swap(x, axis, n, k):
    return lax.ppermute(x, axis, [(i, i ^ k) for i in range(n)])


def held(x):
    return pltpu.with_memory_space_constraint(x, pltpu.VMEM)


def left(x):
    return pltpu.with_memory_space_constraint(x, pltpu.HBM)


def estimate(nbytes, flops=0):
    return pl.CostEstimate(flops=flops, bytes_accessed=nbytes, transcendentals=0)


def pack_kernel(n_dp, ranks, cols_a, grad_a, grad_b, *refs):
    outs, rows, sems = refs[: n_dp - 1], refs[n_dp - 1], refs[n_dp]
    me = lax.axis_index("dp")
    copies = []
    for k in range(1, n_dp):
        start = pl.multiple_of((me ^ k) * ranks, ranks)
        pair = (
            pltpu.make_async_copy(
                grad_a.at[0, 0, pl.ds(start, ranks), :],
                rows.at[k - 1, :, pl.ds(0, cols_a)],
                sems.at[k - 1, 0],
            ),
            pltpu.make_async_copy(
                grad_b.at[0, 0, pl.ds(start, ranks), :],
                rows.at[k - 1, :, pl.ds(cols_a, rows.shape[2] - cols_a)],
                sems.at[k - 1, 1],
            ),
        )
        for copy in pair:
            copy.start()
        copies.append(pair)
    for k, pair in enumerate(copies):
        for copy in pair:
            copy.wait()
        outs[k][...] = rows[k].astype(BF16)


def load_kernel(ranks, cols_a, slots_in, *refs):
    grad_a, grad_b, fa, fb, ma, mb, sa, sb = refs[:8]
    grad, factor, moment, second, order, stays, slot_of, sems = refs[8:]
    me = lax.axis_index("dp")
    start = pl.multiple_of(me * ranks, ranks)
    first = pl.ds(0, cols_a)
    last = pl.ds(cols_a, grad.shape[1] - cols_a)
    pairs = [
        (grad_a.at[0, 0, pl.ds(start, ranks), :], grad.at[:, first]),
        (grad_b.at[0, 0, pl.ds(start, ranks), :], grad.at[:, last]),
        (fa.at[0], factor.at[:, first]),
        (fb.at[0], factor.at[:, last]),
        (ma.at[0], moment.at[:, first]),
        (mb.at[0], moment.at[:, last]),
        (sa.at[0], second.at[:, first]),
        (sb.at[0], second.at[:, last]),
        (slots_in, slot_of),
    ]
    copies = [pltpu.make_async_copy(a, b, sems.at[i]) for i, (a, b) in enumerate(pairs)]
    for copy in copies:
        copy.start()
    copies.pop().wait()
    n = slot_of.shape[0]
    number = jnp.int32(0)
    for i in range(n - 1):
        smaller = jnp.int32(0)
        for j in range(i + 1, n):
            smaller += (slot_of[j] < slot_of[i]).astype(jnp.int32)
        number = number * (n - i) + smaller
    order[0] = number
    here = lax.axis_index("expert")
    stays[0] = (slot_of[here] == here).astype(jnp.int32)
    for copy in copies:
        copy.wait()


def keep_kernel(piece, kept):
    kept[...] = piece[...]


def send_kernel(*refs):
    grad, factor, moment, second = refs[:4]
    total = grad[...]
    for piece in refs[4:-1]:
        total = total + piece[...].astype(F32)
    refs[-1][...] = adam_update(factor[...], moment[...], second[...], total)[0].astype(BF16)


def state_kernel(n_got, cols_a, weight, *refs):
    ins = refs[: 4 + n_got]
    outs = refs[4 + n_got : 10 + n_got]
    panel = refs[10 + n_got]
    parts = refs[11 + n_got : 17 + n_got]
    sems = refs[-1]
    cols_b = ins[0].shape[1] - cols_a
    width = 256 if cols_a % 256 == 0 and cols_b % 256 == 0 else 128
    load = pltpu.make_async_copy(weight.at[0], panel, sems.at[0])
    load.start()

    def some_columns(start, into, at):
        here = pl.ds(pl.multiple_of(start, width), width)
        there = pl.ds(pl.multiple_of(at, width), width)
        grad, factor, moment, second = (ref[:, here] for ref in ins[:4])
        for piece in ins[4:]:
            grad = grad + piece[:, here].astype(F32)
        for out, new in zip(into, adam_update(factor, moment, second, grad)):
            out[:, there] = new

    @pl.loop(0, cols_a // width)
    def _(i):
        some_columns(i * width, parts[::2], i * width)

    @pl.loop(0, cols_b // width)
    def _(i):
        some_columns(cols_a + i * width, parts[1::2], i * width)

    copies = [
        pltpu.make_async_copy(part, out.at[0], sems.at[1 + i])
        for i, (part, out) in enumerate(zip(parts, outs))
    ]
    for copy in copies:
        copy.start()
    for copy in copies:
        copy.wait()
    load.wait()


def join_kernel(cols_a, *refs):
    parts = refs[:-4]
    rows_a, flipped = refs[-3:-1]
    ranks = parts[0].shape[0]
    for i, part in enumerate(parts):
        rows_a[pl.ds(i * ranks, ranks), :] = part[:, :cols_a]
    rows_b = jnp.concatenate([part[:, cols_a:].astype(F32) for part in parts], axis=0)
    flipped[...] = (rows_b * ADAPTER_SCALE).T.astype(BF16)


def merge_kernel(k, rows, *refs):
    panel, rows_a, flipped = refs[:3]
    out, tile, sems = refs[-3:]
    cols = rows_a.shape[1]
    base = (lax.axis_index("tensor") ^ k) * cols
    columns = pl.ds(pl.multiple_of(base, cols), cols)
    width = 512
    copies = []
    for step in range(panel.shape[0] // rows):
        here = slice(step * rows, (step + 1) * rows)
        for low in range(0, cols, width):
            span = slice(low, low + width)
            at = pl.ds(pl.multiple_of(base + low, width), width)
            increment = jnp.dot(flipped[here, :], rows_a[:, span], preferred_element_type=F32)
            tile[here, span] = (panel[here, at].astype(F32) + increment).astype(BF16)
        part = pl.ds(step * rows, rows)
        copy = pltpu.make_async_copy(tile.at[part, :], out.at[0, part, columns], sems.at[step])
        copy.start()
        copies.append(copy)
    for copy in copies:
        copy.wait()


def per_device(
    n_dp,
    n_expert,
    n_tensor,
    weight,
    factor_a,
    factor_b,
    moment_a,
    second_a,
    first_moment_factor_b,
    second_b,
    grad_a,
    grad_b,
    slot_of,
):
    ranks, cols_a = factor_a.shape[1:]
    cols_b = factor_b.shape[2]
    cols = cols_a + cols_b

    pieces = pl.pallas_call(
        functools.partial(pack_kernel, n_dp, ranks, cols_a),
        in_specs=[HBM, HBM],
        out_specs=[VMEM] * (n_dp - 1),
        out_shape=[pltpu.VMEM((ranks, cols), BF16)] * (n_dp - 1),
        scratch_shapes=[
            pltpu.VMEM((n_dp - 1, ranks, cols), F32),
            pltpu.SemaphoreType.DMA((n_dp - 1, 2)),
        ],
        compiler_params=PARAMS,
        name="pack",
    )(left(grad_a), left(grad_b))
    got = [held(swap(pieces[k - 1], "dp", n_dp, k)) for k in range(n_dp - 1, 0, -1)]

    *state, order, stays = pl.pallas_call(
        functools.partial(load_kernel, ranks, cols_a),
        in_specs=[HBM] * 9,
        out_specs=[VMEM] * 4 + [SMEM] * 2,
        out_shape=[pltpu.VMEM((ranks, cols), F32)] * 4 + [pltpu.SMEM((1,), jnp.int32)] * 2,
        scratch_shapes=[pltpu.SMEM(slot_of.shape, jnp.int32), pltpu.SemaphoreType.DMA((9,))],
        compiler_params=PARAMS,
        cost_estimate=estimate(4 * ranks * cols * 4),
        name="load",
    )(
        *map(
            left,
            (
                slot_of,
                grad_a,
                grad_b,
                factor_a,
                factor_b,
                moment_a,
                first_moment_factor_b,
                second_a,
                second_b,
            ),
        ),
    )
    state = [held(x) for x in state]

    send = pl.pallas_call(
        send_kernel,
        in_specs=[VMEM] * (3 + n_dp),
        out_specs=VMEM,
        out_shape=pltpu.VMEM((ranks, cols), BF16),
        compiler_params=PARAMS,
        name="send",
    )(*state, *got)

    def move(slots):
        pairs = []
        for i, (expert, slot), j in itertools.product(
            range(n_dp), enumerate(slots), range(n_tensor)
        ):
            source = (i * n_expert + expert) * n_tensor + j
            partner = j if expert != slot else (j + 1) % n_tensor
            pairs.append((source, (i * n_expert + slot) * n_tensor + partner))
        moves = any(expert != slot for expert, slot in enumerate(slots))

        def branch(send):
            mine = lax.ppermute(send, ("dp", "expert", "tensor"), pairs) if moves else send
            return pl.pallas_call(
                keep_kernel,
                in_specs=[VMEM],
                out_specs=VMEM,
                out_shape=pltpu.VMEM((ranks, cols), BF16),
                compiler_params=PARAMS,
                name="keep",
            )(held(mine))

        return branch

    if n_expert <= MOST_SWITCHED:
        orders = itertools.permutations(range(n_expert))
        mine = lax.switch(order[0], [move(slots) for slots in orders], send)
        mine = jnp.where(stays[0] == 1, send, mine)
    else:
        mine = send
        here = lax.axis_index("expert")
        experts = jnp.arange(n_expert, dtype=jnp.int32)
        wanted = jnp.sum(jnp.where(slot_of == here, experts, 0)) ^ here
        for k in range(1, n_expert):
            mine = jnp.where(wanted == k, swap(send, "expert", n_expert, k), mine)

    parts = [mine] + [swap(mine, "dp", n_dp, k) for k in range(1, n_dp)]
    panel_shape = weight.shape[1:]
    shapes = [factor_a.shape, factor_b.shape] * 3
    *new, panel = pl.pallas_call(
        functools.partial(state_kernel, n_dp - 1, cols_a),
        in_specs=[HBM] + [VMEM] * (3 + n_dp),
        out_specs=[HBM] * 6 + [VMEM],
        out_shape=[jax.ShapeDtypeStruct(shape, F32) for shape in shapes]
        + [pltpu.VMEM(panel_shape, BF16)],
        scratch_shapes=[pltpu.VMEM(shape[1:], F32) for shape in shapes]
        + [pltpu.SemaphoreType.DMA((7,))],
        compiler_params=PARAMS,
        cost_estimate=estimate(weight.size * 4),
        name="state",
    )(left(weight), *state, *got)
    new_a, new_b, new_moment_a, new_moment_b, new_second_a, new_second_b = new
    rows_a, flipped, panel = pl.pallas_call(
        functools.partial(join_kernel, cols_a),
        in_specs=[VMEM] * (n_dp + 1),
        out_specs=[VMEM] * 3,
        out_shape=[
            pltpu.VMEM((ranks * n_dp, cols_a), BF16),
            pltpu.VMEM((cols_b, ranks * n_dp), BF16),
            pltpu.VMEM(panel_shape, BF16),
        ],
        input_output_aliases={n_dp: 2},
        compiler_params=PARAMS,
        name="join",
    )(*map(held, parts), held(panel))

    merged = None
    step_rows = 64
    for k in range(n_tensor):
        block = held(rows_a if k == 0 else swap(rows_a, "tensor", n_tensor, k))
        operands = [held(panel), block, held(flipped)] + ([] if merged is None else [merged])
        merged = pl.pallas_call(
            functools.partial(merge_kernel, k, step_rows),
            in_specs=[VMEM] * 3 + [HBM] * (len(operands) - 3),
            out_specs=HBM,
            out_shape=jax.ShapeDtypeStruct(weight.shape, BF16),
            scratch_shapes=[
                pltpu.VMEM((panel_shape[0], cols_a), BF16),
                pltpu.SemaphoreType.DMA((panel_shape[0] // step_rows,)),
            ],
            input_output_aliases={} if merged is None else {3: 0},
            compiler_params=PARAMS,
            cost_estimate=estimate(
                panel_shape[0] * cols_a * 2, 2 * panel_shape[0] * cols_a * ranks * n_dp
            ),
            name=f"merge{k}",
        )(*operands)
    return (merged, new_a, new_b, new_moment_a, new_second_a, new_moment_b, new_second_b)


def solution(mesh):
    sizes = dict(mesh.shape)

    def body(*args):
        return per_device(sizes["dp"], sizes["expert"], sizes["tensor"], *args)

    state = P("expert", "dp", "tensor")
    grad = P("dp", "expert", None, "tensor")
    weight = P("expert", "tensor", None)
    in_specs = (weight,) + (state,) * 6 + (grad,) * 2 + (P(),)
    out_specs = (weight,) + (state,) * 6
    return jax.shard_map(body, mesh=mesh, in_specs=in_specs, out_specs=out_specs, check_vma=False)
```

```python
import functools
import itertools

import jax
import jax.numpy as jnp
from jax import lax
from jax.experimental import pallas as pl
from jax.experimental.pallas import tpu as pltpu
from jax.sharding import PartitionSpec as P

ADAM_STEP = 20


ADAPTER_SCALE = 2.0
BETA_ONE = 0.9
BETA_TWO = 0.95
LEARN_RATE = 0.08
STABILITY_TERM = 1e-08

MOST_SWITCHED = 4

F32 = jnp.float32
BF16 = jnp.bfloat16
VMEM = pl.BlockSpec(memory_space=pltpu.VMEM)
SMEM = pl.BlockSpec(memory_space=pltpu.SMEM)
HBM = pl.BlockSpec(memory_space=pltpu.HBM)
PARAMS = pltpu.CompilerParams(vmem_limit_bytes=16 * 1024 * 1024)


def adam_update(param, moment, second, grad):
    corr_one = 1.0 - BETA_ONE**ADAM_STEP
    corr_two = 1.0 - BETA_TWO**ADAM_STEP
    moment_new = BETA_ONE * moment + (1.0 - BETA_ONE) * grad
    second_new = BETA_TWO * second + (1.0 - BETA_TWO) * grad * grad
    param_new = param - LEARN_RATE * (moment_new / corr_one) / (
        jnp.sqrt(second_new / corr_two) + STABILITY_TERM
    )
    return (param_new, moment_new, second_new)


def swap(x, axis, n, k):
    return lax.ppermute(x, axis, [(i, i ^ k) for i in range(n)])


def held(x):
    return pltpu.with_memory_space_constraint(x, pltpu.VMEM)


def left(x):
    return pltpu.with_memory_space_constraint(x, pltpu.HBM)


def estimate(nbytes, flops=0):
    return pl.CostEstimate(flops=flops, bytes_accessed=nbytes, transcendentals=0)


def pack_kernel(n_dp, ranks, cols_a, grad_a, grad_b, *refs):
    outs, rows, sems = refs[: n_dp - 1], refs[n_dp - 1], refs[n_dp]
    me = lax.axis_index("dp")
    copies = []
    for k in range(1, n_dp):
        start = pl.multiple_of((me ^ k) * ranks, ranks)
        pair = (
            pltpu.make_async_copy(
                grad_a.at[0, 0, pl.ds(start, ranks), :],
                rows.at[k - 1, :, pl.ds(0, cols_a)],
                sems.at[k - 1, 0],
            ),
            pltpu.make_async_copy(
                grad_b.at[0, 0, pl.ds(start, ranks), :],
                rows.at[k - 1, :, pl.ds(cols_a, rows.shape[2] - cols_a)],
                sems.at[k - 1, 1],
            ),
        )
        for copy in pair:
            copy.start()
        copies.append(pair)
    for k, pair in enumerate(copies):
        for copy in pair:
            copy.wait()
        outs[k][...] = rows[k].astype(BF16)


def load_kernel(ranks, cols_a, slots_in, *refs):
    grad_a, grad_b, fa, fb, ma, mb, sa, sb = refs[:8]
    grad, factor, moment, second, order, stays, slot_of, sems = refs[8:]
    me = lax.axis_index("dp")
    start = pl.multiple_of(me * ranks, ranks)
    first = pl.ds(0, cols_a)
    last = pl.ds(cols_a, grad.shape[1] - cols_a)
    pairs = [
        (grad_a.at[0, 0, pl.ds(start, ranks), :], grad.at[:, first]),
        (grad_b.at[0, 0, pl.ds(start, ranks), :], grad.at[:, last]),
        (fa.at[0], factor.at[:, first]),
        (fb.at[0], factor.at[:, last]),
        (ma.at[0], moment.at[:, first]),
        (mb.at[0], moment.at[:, last]),
        (sa.at[0], second.at[:, first]),
        (sb.at[0], second.at[:, last]),
        (slots_in, slot_of),
    ]
    copies = [pltpu.make_async_copy(a, b, sems.at[i]) for i, (a, b) in enumerate(pairs)]
    for copy in copies:
        copy.start()
    copies.pop().wait()
    n = slot_of.shape[0]
    number = jnp.int32(0)
    for i in range(n - 1):
        smaller = jnp.int32(0)
        for j in range(i + 1, n):
            smaller += (slot_of[j] < slot_of[i]).astype(jnp.int32)
        number = number * (n - i) + smaller
    order[0] = number
    here = lax.axis_index("expert")
    stays[0] = (slot_of[here] == here).astype(jnp.int32)
    for copy in copies:
        copy.wait()


def keep_kernel(piece, kept):
    kept[...] = piece[...]


def send_kernel(*refs):
    grad, factor, moment, second = refs[:4]
    total = grad[...]
    for piece in refs[4:-1]:
        total = total + piece[...].astype(F32)
    refs[-1][...] = adam_update(factor[...], moment[...], second[...], total)[0].astype(BF16)


def shard_copy(weight, panel, k, sem):
    cols = panel.shape[1]
    at = pl.multiple_of((lax.axis_index("tensor") ^ k) * cols, cols)
    return pltpu.make_async_copy(weight.at[0, :, pl.ds(at, cols)], panel, sem)


def state_kernel(n_got, cols_a, weight, *refs):
    ins = refs[: 4 + n_got]
    outs = refs[4 + n_got : 10 + n_got]
    panel = refs[10 + n_got]
    parts = refs[11 + n_got : 17 + n_got]
    sems = refs[-1]
    cols_b = ins[0].shape[1] - cols_a
    width = 256 if cols_a % 256 == 0 and cols_b % 256 == 0 else 128
    load = shard_copy(weight, panel, 0, sems.at[0])
    load.start()

    def some_columns(start, into, at):
        here = pl.ds(pl.multiple_of(start, width), width)
        there = pl.ds(pl.multiple_of(at, width), width)
        grad, factor, moment, second = (ref[:, here] for ref in ins[:4])
        for piece in ins[4:]:
            grad = grad + piece[:, here].astype(F32)
        for out, new in zip(into, adam_update(factor, moment, second, grad)):
            out[:, there] = new

    @pl.loop(0, cols_a // width)
    def _(i):
        some_columns(i * width, parts[::2], i * width)

    @pl.loop(0, cols_b // width)
    def _(i):
        some_columns(cols_a + i * width, parts[1::2], i * width)

    copies = [
        pltpu.make_async_copy(part, out.at[0], sems.at[1 + i])
        for i, (part, out) in enumerate(zip(parts, outs))
    ]
    for copy in copies:
        copy.start()
    for copy in copies:
        copy.wait()
    load.wait()


def join_kernel(cols_a, *refs):
    parts = refs[:-4]
    rows_a, flipped = refs[-3:-1]
    ranks = parts[0].shape[0]
    for i, part in enumerate(parts):
        rows_a[pl.ds(i * ranks, ranks), :] = part[:, :cols_a]
    rows_b = jnp.concatenate([part[:, cols_a:].astype(F32) for part in parts], axis=0)
    flipped[...] = (rows_b * ADAPTER_SCALE).T.astype(BF16)


def merge_kernel(k, rows, load_next, *refs):
    panel, rows_a, flipped = refs[:3]
    tile, sems, load_sem = refs[-3:]
    out = refs[-5] if load_next else refs[-4]
    cols = rows_a.shape[1]
    columns = pl.ds(pl.multiple_of((lax.axis_index("tensor") ^ k) * cols, cols), cols)
    load = None
    if load_next:
        load = shard_copy(refs[3], refs[-4], k + 1, load_sem.at[0])
        load.start()
    copies = []
    for step in range(panel.shape[0] // rows):
        here = slice(step * rows, (step + 1) * rows)
        increment = jnp.dot(flipped[here, :], rows_a[...], preferred_element_type=F32)
        tile[here, :] = (panel[here, :].astype(F32) + increment).astype(BF16)
        part = pl.ds(step * rows, rows)
        copy = pltpu.make_async_copy(tile.at[part, :], out.at[0, part, columns], sems.at[step])
        copy.start()
        copies.append(copy)
    for copy in copies:
        copy.wait()
    if load is not None:
        load.wait()


def per_device(
    n_dp,
    n_expert,
    n_tensor,
    weight,
    factor_a,
    factor_b,
    moment_a,
    second_a,
    first_moment_factor_b,
    second_b,
    grad_a,
    grad_b,
    slot_of,
):
    ranks, cols_a = factor_a.shape[1:]
    cols_b = factor_b.shape[2]
    cols = cols_a + cols_b

    pieces = pl.pallas_call(
        functools.partial(pack_kernel, n_dp, ranks, cols_a),
        in_specs=[HBM, HBM],
        out_specs=[VMEM] * (n_dp - 1),
        out_shape=[pltpu.VMEM((ranks, cols), BF16)] * (n_dp - 1),
        scratch_shapes=[
            pltpu.VMEM((n_dp - 1, ranks, cols), F32),
            pltpu.SemaphoreType.DMA((n_dp - 1, 2)),
        ],
        compiler_params=PARAMS,
        name="pack",
    )(left(grad_a), left(grad_b))
    got = [held(swap(pieces[k - 1], "dp", n_dp, k)) for k in range(n_dp - 1, 0, -1)]

    *state, order, stays = pl.pallas_call(
        functools.partial(load_kernel, ranks, cols_a),
        in_specs=[HBM] * 9,
        out_specs=[VMEM] * 4 + [SMEM] * 2,
        out_shape=[pltpu.VMEM((ranks, cols), F32)] * 4 + [pltpu.SMEM((1,), jnp.int32)] * 2,
        scratch_shapes=[pltpu.SMEM(slot_of.shape, jnp.int32), pltpu.SemaphoreType.DMA((9,))],
        compiler_params=PARAMS,
        cost_estimate=estimate(4 * ranks * cols * 4),
        name="load",
    )(
        *map(
            left,
            (
                slot_of,
                grad_a,
                grad_b,
                factor_a,
                factor_b,
                moment_a,
                first_moment_factor_b,
                second_a,
                second_b,
            ),
        ),
    )
    state = [held(x) for x in state]

    send = pl.pallas_call(
        send_kernel,
        in_specs=[VMEM] * (3 + n_dp),
        out_specs=VMEM,
        out_shape=pltpu.VMEM((ranks, cols), BF16),
        compiler_params=PARAMS,
        name="send",
    )(*state, *got)

    def move(slots):
        pairs = []
        for i, (expert, slot), j in itertools.product(
            range(n_dp), enumerate(slots), range(n_tensor)
        ):
            source = (i * n_expert + expert) * n_tensor + j
            partner = j if expert != slot else (j + 1) % n_tensor
            pairs.append((source, (i * n_expert + slot) * n_tensor + partner))
        moves = any(expert != slot for expert, slot in enumerate(slots))

        def branch(send):
            mine = lax.ppermute(send, ("dp", "expert", "tensor"), pairs) if moves else send
            return pl.pallas_call(
                keep_kernel,
                in_specs=[VMEM],
                out_specs=VMEM,
                out_shape=pltpu.VMEM((ranks, cols), BF16),
                compiler_params=PARAMS,
                name="keep",
            )(held(mine))

        return branch

    if n_expert <= MOST_SWITCHED:
        orders = itertools.permutations(range(n_expert))
        mine = lax.switch(order[0], [move(slots) for slots in orders], send)
        mine = jnp.where(stays[0] == 1, send, mine)
    else:
        mine = send
        here = lax.axis_index("expert")
        experts = jnp.arange(n_expert, dtype=jnp.int32)
        wanted = jnp.sum(jnp.where(slot_of == here, experts, 0)) ^ here
        for k in range(1, n_expert):
            mine = jnp.where(wanted == k, swap(send, "expert", n_expert, k), mine)

    parts = [mine] + [swap(mine, "dp", n_dp, k) for k in range(1, n_dp)]
    panel_shape = (weight.shape[1], cols_a)
    shapes = [factor_a.shape, factor_b.shape] * 3
    *new, panel = pl.pallas_call(
        functools.partial(state_kernel, n_dp - 1, cols_a),
        in_specs=[HBM] + [VMEM] * (3 + n_dp),
        out_specs=[HBM] * 6 + [VMEM],
        out_shape=[jax.ShapeDtypeStruct(shape, F32) for shape in shapes]
        + [pltpu.VMEM(panel_shape, BF16)],
        scratch_shapes=[pltpu.VMEM(shape[1:], F32) for shape in shapes]
        + [pltpu.SemaphoreType.DMA((7,))],
        compiler_params=PARAMS,
        cost_estimate=estimate(weight.size * 4),
        name="state",
    )(left(weight), *state, *got)
    new_a, new_b, new_moment_a, new_moment_b, new_second_a, new_second_b = new
    rows_a, flipped, panel = pl.pallas_call(
        functools.partial(join_kernel, cols_a),
        in_specs=[VMEM] * (n_dp + 1),
        out_specs=[VMEM] * 3,
        out_shape=[
            pltpu.VMEM((ranks * n_dp, cols_a), BF16),
            pltpu.VMEM((cols_b, ranks * n_dp), BF16),
            pltpu.VMEM(panel_shape, BF16),
        ],
        input_output_aliases={n_dp: 2},
        compiler_params=PARAMS,
        name="join",
    )(*map(held, parts), held(panel))

    merged = None
    step_rows = 128
    for k in range(n_tensor):
        block = held(rows_a if k == 0 else swap(rows_a, "tensor", n_tensor, k))
        load_next = k < n_tensor - 1
        operands = [held(panel), block, held(flipped)]
        operands += [left(weight)] if load_next else []
        operands += [] if merged is None else [merged]
        merged, *panels = pl.pallas_call(
            functools.partial(merge_kernel, k, step_rows, load_next),
            in_specs=[VMEM] * 3 + [HBM] * (len(operands) - 3),
            out_specs=[HBM] + [VMEM] * load_next,
            out_shape=[jax.ShapeDtypeStruct(weight.shape, BF16)]
            + [pltpu.VMEM(panel_shape, BF16)] * load_next,
            scratch_shapes=[
                pltpu.VMEM(panel_shape, BF16),
                pltpu.SemaphoreType.DMA((panel_shape[0] // step_rows,)),
                pltpu.SemaphoreType.DMA((1,)),
            ],
            input_output_aliases={} if merged is None else {len(operands) - 1: 0},
            compiler_params=PARAMS,
            cost_estimate=estimate(
                panel_shape[0] * cols_a * 2, 2 * panel_shape[0] * cols_a * ranks * n_dp
            ),
            name=f"merge{k}",
        )(*operands)
        panel = panels[0] if load_next else None
    return (merged, new_a, new_b, new_moment_a, new_second_a, new_moment_b, new_second_b)


def solution(mesh):
    sizes = dict(mesh.shape)

    def body(*args):
        return per_device(sizes["dp"], sizes["expert"], sizes["tensor"], *args)

    state = P("expert", "dp", "tensor")
    grad = P("dp", "expert", None, "tensor")
    weight = P("expert", "tensor", None)
    in_specs = (weight,) + (state,) * 6 + (grad,) * 2 + (P(),)
    out_specs = (weight,) + (state,) * 6
    return jax.shard_map(body, mesh=mesh, in_specs=in_specs, out_specs=out_specs, check_vma=False)
```

```python
import functools
import itertools

import jax
import jax.numpy as jnp
from jax import lax
from jax.experimental import pallas as pl
from jax.experimental.pallas import tpu as pltpu
from jax.sharding import PartitionSpec as P

ADAM_STEP = 20


ADAPTER_SCALE = 2.0
BETA_ONE = 0.9
BETA_TWO = 0.95
LEARN_RATE = 0.08
STABILITY_TERM = 1e-08

MOST_SWITCHED = 4

F32 = jnp.float32
BF16 = jnp.bfloat16
VMEM = pl.BlockSpec(memory_space=pltpu.VMEM)
SMEM = pl.BlockSpec(memory_space=pltpu.SMEM)
HBM = pl.BlockSpec(memory_space=pltpu.HBM)
PARAMS = pltpu.CompilerParams(vmem_limit_bytes=16 * 1024 * 1024)


def adam_update(param, moment, second, grad):
    corr_one = 1.0 - BETA_ONE**ADAM_STEP
    corr_two = 1.0 - BETA_TWO**ADAM_STEP
    moment_new = BETA_ONE * moment + (1.0 - BETA_ONE) * grad
    second_new = BETA_TWO * second + (1.0 - BETA_TWO) * grad * grad
    param_new = param - LEARN_RATE * (moment_new / corr_one) / (
        jnp.sqrt(second_new / corr_two) + STABILITY_TERM
    )
    return (param_new, moment_new, second_new)


def swap(x, axis, n, k):
    return lax.ppermute(x, axis, [(i, i ^ k) for i in range(n)])


def held(x):
    return pltpu.with_memory_space_constraint(x, pltpu.VMEM)


def left(x):
    return pltpu.with_memory_space_constraint(x, pltpu.HBM)


def estimate(nbytes, flops=0):
    return pl.CostEstimate(flops=flops, bytes_accessed=nbytes, transcendentals=0)


def pack_kernel(n_dp, ranks, cols_a, grad_a, grad_b, *refs):
    outs, rows, sems = refs[: n_dp - 1], refs[n_dp - 1], refs[n_dp]
    me = lax.axis_index("dp")
    copies = []
    for k in range(1, n_dp):
        start = pl.multiple_of((me ^ k) * ranks, ranks)
        pair = (
            pltpu.make_async_copy(
                grad_a.at[0, 0, pl.ds(start, ranks), :],
                rows.at[k - 1, :, pl.ds(0, cols_a)],
                sems.at[k - 1, 0],
            ),
            pltpu.make_async_copy(
                grad_b.at[0, 0, pl.ds(start, ranks), :],
                rows.at[k - 1, :, pl.ds(cols_a, rows.shape[2] - cols_a)],
                sems.at[k - 1, 1],
            ),
        )
        for copy in pair:
            copy.start()
        copies.append(pair)
    for k, pair in enumerate(copies):
        for copy in pair:
            copy.wait()
        outs[k][...] = rows[k].astype(BF16)


def load_kernel(ranks, cols_a, slots_in, *refs):
    grad_a, grad_b, fa, fb, ma, mb, sa, sb = refs[:8]
    grad, factor, moment, second, order, stays, slot_of, sems = refs[8:]
    me = lax.axis_index("dp")
    start = pl.multiple_of(me * ranks, ranks)
    first = pl.ds(0, cols_a)
    last = pl.ds(cols_a, grad.shape[1] - cols_a)
    pairs = [
        (grad_a.at[0, 0, pl.ds(start, ranks), :], grad.at[:, first]),
        (grad_b.at[0, 0, pl.ds(start, ranks), :], grad.at[:, last]),
        (fa.at[0], factor.at[:, first]),
        (fb.at[0], factor.at[:, last]),
        (ma.at[0], moment.at[:, first]),
        (mb.at[0], moment.at[:, last]),
        (sa.at[0], second.at[:, first]),
        (sb.at[0], second.at[:, last]),
        (slots_in, slot_of),
    ]
    copies = [pltpu.make_async_copy(a, b, sems.at[i]) for i, (a, b) in enumerate(pairs)]
    for copy in copies:
        copy.start()
    copies.pop().wait()
    n = slot_of.shape[0]
    number = jnp.int32(0)
    for i in range(n - 1):
        smaller = jnp.int32(0)
        for j in range(i + 1, n):
            smaller += (slot_of[j] < slot_of[i]).astype(jnp.int32)
        number = number * (n - i) + smaller
    order[0] = number
    here = lax.axis_index("expert")
    stays[0] = (slot_of[here] == here).astype(jnp.int32)
    for copy in copies:
        copy.wait()


def keep_kernel(piece, kept):
    kept[...] = piece[...]


def send_kernel(*refs):
    grad, factor, moment, second = refs[:4]
    total = grad[...]
    for piece in refs[4:-1]:
        total = total + piece[...].astype(F32)
    refs[-1][...] = adam_update(factor[...], moment[...], second[...], total)[0].astype(BF16)


def state_kernel(n_got, cols_a, weight, *refs):
    ins = refs[: 4 + n_got]
    outs = refs[4 + n_got : 10 + n_got]
    panel = refs[10 + n_got]
    parts = refs[11 + n_got : 17 + n_got]
    sems = refs[-1]
    cols_b = ins[0].shape[1] - cols_a
    width = 256 if cols_a % 256 == 0 and cols_b % 256 == 0 else 128
    load = pltpu.make_async_copy(weight.at[0], panel, sems.at[0])
    load.start()

    def some_columns(start, into, at):
        here = pl.ds(pl.multiple_of(start, width), width)
        there = pl.ds(pl.multiple_of(at, width), width)
        grad, factor, moment, second = (ref[:, here] for ref in ins[:4])
        for piece in ins[4:]:
            grad = grad + piece[:, here].astype(F32)
        for out, new in zip(into, adam_update(factor, moment, second, grad)):
            out[:, there] = new

    @pl.loop(0, cols_a // width)
    def _(i):
        some_columns(i * width, parts[::2], i * width)

    @pl.loop(0, cols_b // width)
    def _(i):
        some_columns(cols_a + i * width, parts[1::2], i * width)

    copies = [
        pltpu.make_async_copy(part, out.at[0], sems.at[1 + i])
        for i, (part, out) in enumerate(zip(parts, outs))
    ]
    for copy in copies:
        copy.start()
    for copy in copies:
        copy.wait()
    load.wait()


def join_kernel(cols_a, *refs):
    parts = refs[:-4]
    rows_a, flipped = refs[-3:-1]
    ranks = parts[0].shape[0]
    for i, part in enumerate(parts):
        rows_a[pl.ds(i * ranks, ranks), :] = part[:, :cols_a]
    rows_b = jnp.concatenate([part[:, cols_a:].astype(F32) for part in parts], axis=0)
    flipped[...] = (rows_b * ADAPTER_SCALE).T.astype(BF16)


def merge_kernel(k, rows, *refs):
    panel, rows_a, flipped = refs[:3]
    out, tile, sems = refs[-3:]
    cols = rows_a.shape[1]
    base = (lax.axis_index("tensor") ^ k) * cols
    columns = pl.ds(pl.multiple_of(base, cols), cols)
    width = 512
    copies = []
    for step in range(panel.shape[0] // rows):
        here = slice(step * rows, (step + 1) * rows)
        for low in range(0, cols, width):
            span = slice(low, low + width)
            at = pl.ds(pl.multiple_of(base + low, width), width)
            increment = jnp.dot(flipped[here, :], rows_a[:, span], preferred_element_type=F32)
            tile[here, span] = (panel[here, at].astype(F32) + increment).astype(BF16)
        part = pl.ds(step * rows, rows)
        copy = pltpu.make_async_copy(tile.at[part, :], out.at[0, part, columns], sems.at[step])
        copy.start(priority=step % 2)
        copies.append(copy)
    for copy in copies:
        copy.wait()


def per_device(
    n_dp,
    n_expert,
    n_tensor,
    weight,
    factor_a,
    factor_b,
    moment_a,
    second_a,
    first_moment_factor_b,
    second_b,
    grad_a,
    grad_b,
    slot_of,
):
    ranks, cols_a = factor_a.shape[1:]
    cols_b = factor_b.shape[2]
    cols = cols_a + cols_b

    pieces = pl.pallas_call(
        functools.partial(pack_kernel, n_dp, ranks, cols_a),
        in_specs=[HBM, HBM],
        out_specs=[VMEM] * (n_dp - 1),
        out_shape=[pltpu.VMEM((ranks, cols), BF16)] * (n_dp - 1),
        scratch_shapes=[
            pltpu.VMEM((n_dp - 1, ranks, cols), F32),
            pltpu.SemaphoreType.DMA((n_dp - 1, 2)),
        ],
        compiler_params=PARAMS,
        name="pack",
    )(left(grad_a), left(grad_b))
    got = [held(swap(pieces[k - 1], "dp", n_dp, k)) for k in range(n_dp - 1, 0, -1)]

    *state, order, stays = pl.pallas_call(
        functools.partial(load_kernel, ranks, cols_a),
        in_specs=[HBM] * 9,
        out_specs=[VMEM] * 4 + [SMEM] * 2,
        out_shape=[pltpu.VMEM((ranks, cols), F32)] * 4 + [pltpu.SMEM((1,), jnp.int32)] * 2,
        scratch_shapes=[pltpu.SMEM(slot_of.shape, jnp.int32), pltpu.SemaphoreType.DMA((9,))],
        compiler_params=PARAMS,
        cost_estimate=estimate(4 * ranks * cols * 4),
        name="load",
    )(
        *map(
            left,
            (
                slot_of,
                grad_a,
                grad_b,
                factor_a,
                factor_b,
                moment_a,
                first_moment_factor_b,
                second_a,
                second_b,
            ),
        ),
    )
    state = [held(x) for x in state]

    send = pl.pallas_call(
        send_kernel,
        in_specs=[VMEM] * (3 + n_dp),
        out_specs=VMEM,
        out_shape=pltpu.VMEM((ranks, cols), BF16),
        compiler_params=PARAMS,
        name="send",
    )(*state, *got)

    def move(slots):
        pairs = []
        for i, (expert, slot), j in itertools.product(
            range(n_dp), enumerate(slots), range(n_tensor)
        ):
            source = (i * n_expert + expert) * n_tensor + j
            partner = j if expert != slot else (j + 1) % n_tensor
            pairs.append((source, (i * n_expert + slot) * n_tensor + partner))
        moves = any(expert != slot for expert, slot in enumerate(slots))

        def branch(send):
            mine = lax.ppermute(send, ("dp", "expert", "tensor"), pairs) if moves else send
            return pl.pallas_call(
                keep_kernel,
                in_specs=[VMEM],
                out_specs=VMEM,
                out_shape=pltpu.VMEM((ranks, cols), BF16),
                compiler_params=PARAMS,
                name="keep",
            )(held(mine))

        return branch

    if n_expert <= MOST_SWITCHED:
        orders = itertools.permutations(range(n_expert))
        mine = lax.switch(order[0], [move(slots) for slots in orders], send)
        mine = jnp.where(stays[0] == 1, send, mine)
    else:
        mine = send
        here = lax.axis_index("expert")
        experts = jnp.arange(n_expert, dtype=jnp.int32)
        wanted = jnp.sum(jnp.where(slot_of == here, experts, 0)) ^ here
        for k in range(1, n_expert):
            mine = jnp.where(wanted == k, swap(send, "expert", n_expert, k), mine)

    parts = [mine] + [swap(mine, "dp", n_dp, k) for k in range(1, n_dp)]
    panel_shape = weight.shape[1:]
    shapes = [factor_a.shape, factor_b.shape] * 3
    *new, panel = pl.pallas_call(
        functools.partial(state_kernel, n_dp - 1, cols_a),
        in_specs=[HBM] + [VMEM] * (3 + n_dp),
        out_specs=[HBM] * 6 + [VMEM],
        out_shape=[jax.ShapeDtypeStruct(shape, F32) for shape in shapes]
        + [pltpu.VMEM(panel_shape, BF16)],
        scratch_shapes=[pltpu.VMEM(shape[1:], F32) for shape in shapes]
        + [pltpu.SemaphoreType.DMA((7,))],
        compiler_params=PARAMS,
        cost_estimate=estimate(weight.size * 4),
        name="state",
    )(left(weight), *state, *got)
    new_a, new_b, new_moment_a, new_moment_b, new_second_a, new_second_b = new
    rows_a, flipped, panel = pl.pallas_call(
        functools.partial(join_kernel, cols_a),
        in_specs=[VMEM] * (n_dp + 1),
        out_specs=[VMEM] * 3,
        out_shape=[
            pltpu.VMEM((ranks * n_dp, cols_a), BF16),
            pltpu.VMEM((cols_b, ranks * n_dp), BF16),
            pltpu.VMEM(panel_shape, BF16),
        ],
        input_output_aliases={n_dp: 2},
        compiler_params=PARAMS,
        name="join",
    )(*map(held, parts), held(panel))

    merged = None
    step_rows = 64
    for k in range(n_tensor):
        block = held(rows_a if k == 0 else swap(rows_a, "tensor", n_tensor, k))
        operands = [held(panel), block, held(flipped)] + ([] if merged is None else [merged])
        merged = pl.pallas_call(
            functools.partial(merge_kernel, k, step_rows),
            in_specs=[VMEM] * 3 + [HBM] * (len(operands) - 3),
            out_specs=HBM,
            out_shape=jax.ShapeDtypeStruct(weight.shape, BF16),
            scratch_shapes=[
                pltpu.VMEM((panel_shape[0], cols_a), BF16),
                pltpu.SemaphoreType.DMA((panel_shape[0] // step_rows,)),
            ],
            input_output_aliases={} if merged is None else {3: 0},
            compiler_params=PARAMS,
            cost_estimate=estimate(
                panel_shape[0] * cols_a * 2, 2 * panel_shape[0] * cols_a * ranks * n_dp
            ),
            name=f"merge{k}",
        )(*operands)
    return (merged, new_a, new_b, new_moment_a, new_second_a, new_moment_b, new_second_b)


def solution(mesh):
    sizes = dict(mesh.shape)

    def body(*args):
        return per_device(sizes["dp"], sizes["expert"], sizes["tensor"], *args)

    state = P("expert", "dp", "tensor")
    grad = P("dp", "expert", None, "tensor")
    weight = P("expert", "tensor", None)
    in_specs = (weight,) + (state,) * 6 + (grad,) * 2 + (P(),)
    out_specs = (weight,) + (state,) * 6
    return jax.shard_map(body, mesh=mesh, in_specs=in_specs, out_specs=out_specs, check_vma=False)
```

```python
import functools
import itertools

import jax
import jax.numpy as jnp
from jax import lax
from jax.experimental import pallas as pl
from jax.experimental.pallas import tpu as pltpu
from jax.sharding import PartitionSpec as P

ADAM_STEP = 20


ADAPTER_SCALE = 2.0
BETA_ONE = 0.9
BETA_TWO = 0.95
LEARN_RATE = 0.08
STABILITY_TERM = 1e-08

MOST_SWITCHED = 4

F32 = jnp.float32
BF16 = jnp.bfloat16
VMEM = pl.BlockSpec(memory_space=pltpu.VMEM)
SMEM = pl.BlockSpec(memory_space=pltpu.SMEM)
HBM = pl.BlockSpec(memory_space=pltpu.HBM)
PARAMS = pltpu.CompilerParams(vmem_limit_bytes=16 * 1024 * 1024)


def adam_update(param, moment, second, grad):
    corr_one = 1.0 - BETA_ONE**ADAM_STEP
    corr_two = 1.0 - BETA_TWO**ADAM_STEP
    moment_new = BETA_ONE * moment + (1.0 - BETA_ONE) * grad
    second_new = BETA_TWO * second + (1.0 - BETA_TWO) * grad * grad
    param_new = param - LEARN_RATE * (moment_new / corr_one) / (
        jnp.sqrt(second_new / corr_two) + STABILITY_TERM
    )
    return (param_new, moment_new, second_new)


def swap(x, axis, n, k):
    return lax.ppermute(x, axis, [(i, i ^ k) for i in range(n)])


def held(x):
    return pltpu.with_memory_space_constraint(x, pltpu.VMEM)


def left(x):
    return pltpu.with_memory_space_constraint(x, pltpu.HBM)


def estimate(nbytes, flops=0):
    return pl.CostEstimate(flops=flops, bytes_accessed=nbytes, transcendentals=0)


def pack_kernel(n_dp, ranks, cols_a, grad_a, grad_b, *refs):
    outs, rows, sems = refs[: n_dp - 1], refs[n_dp - 1], refs[n_dp]
    me = lax.axis_index("dp")
    copies = []
    for k in range(1, n_dp):
        start = pl.multiple_of((me ^ k) * ranks, ranks)
        pair = (
            pltpu.make_async_copy(
                grad_a.at[0, 0, pl.ds(start, ranks), :],
                rows.at[k - 1, :, pl.ds(0, cols_a)],
                sems.at[k - 1, 0],
            ),
            pltpu.make_async_copy(
                grad_b.at[0, 0, pl.ds(start, ranks), :],
                rows.at[k - 1, :, pl.ds(cols_a, rows.shape[2] - cols_a)],
                sems.at[k - 1, 1],
            ),
        )
        for copy in pair:
            copy.start()
        copies.append(pair)
    for k, pair in enumerate(copies):
        for copy in pair:
            copy.wait()
        outs[k][...] = rows[k].astype(BF16)


def load_kernel(ranks, cols_a, slots_in, *refs):
    grad_a, grad_b, fa, fb, ma, mb, sa, sb = refs[:8]
    grad, factor, moment, second, order, stays, slot_of, sems = refs[8:]
    me = lax.axis_index("dp")
    start = pl.multiple_of(me * ranks, ranks)
    first = pl.ds(0, cols_a)
    last = pl.ds(cols_a, grad.shape[1] - cols_a)
    pairs = [
        (grad_a.at[0, 0, pl.ds(start, ranks), :], grad.at[:, first]),
        (grad_b.at[0, 0, pl.ds(start, ranks), :], grad.at[:, last]),
        (fa.at[0], factor.at[:, first]),
        (fb.at[0], factor.at[:, last]),
        (ma.at[0], moment.at[:, first]),
        (mb.at[0], moment.at[:, last]),
        (sa.at[0], second.at[:, first]),
        (sb.at[0], second.at[:, last]),
        (slots_in, slot_of),
    ]
    copies = [pltpu.make_async_copy(a, b, sems.at[i]) for i, (a, b) in enumerate(pairs)]
    for copy in copies:
        copy.start()
    copies.pop().wait()
    n = slot_of.shape[0]
    number = jnp.int32(0)
    for i in range(n - 1):
        smaller = jnp.int32(0)
        for j in range(i + 1, n):
            smaller += (slot_of[j] < slot_of[i]).astype(jnp.int32)
        number = number * (n - i) + smaller
    order[0] = number
    here = lax.axis_index("expert")
    stays[0] = (slot_of[here] == here).astype(jnp.int32)
    for copy in copies:
        copy.wait()


def keep_kernel(piece, kept):
    kept[...] = piece[...]


def send_kernel(*refs):
    grad, factor, moment, second = refs[:4]
    total = grad[...]
    for piece in refs[4:-1]:
        total = total + piece[...].astype(F32)
    refs[-1][...] = adam_update(factor[...], moment[...], second[...], total)[0].astype(BF16)


def state_kernel(n_got, cols_a, weight, *refs):
    ins = refs[: 4 + n_got]
    outs = refs[4 + n_got : 10 + n_got]
    panel = refs[10 + n_got]
    parts = refs[11 + n_got : 17 + n_got]
    sems = refs[-1]
    cols_b = ins[0].shape[1] - cols_a
    width = 256 if cols_a % 256 == 0 and cols_b % 256 == 0 else 128
    load = pltpu.make_async_copy(weight.at[0], panel, sems.at[0])
    load.start()

    def some_columns(start, into, at):
        here = pl.ds(pl.multiple_of(start, width), width)
        there = pl.ds(pl.multiple_of(at, width), width)
        grad, factor, moment, second = (ref[:, here] for ref in ins[:4])
        for piece in ins[4:]:
            grad = grad + piece[:, here].astype(F32)
        for out, new in zip(into, adam_update(factor, moment, second, grad)):
            out[:, there] = new

    @pl.loop(0, cols_a // width)
    def _(i):
        some_columns(i * width, parts[::2], i * width)

    @pl.loop(0, cols_b // width)
    def _(i):
        some_columns(cols_a + i * width, parts[1::2], i * width)

    copies = [
        pltpu.make_async_copy(part, out.at[0], sems.at[1 + i])
        for i, (part, out) in enumerate(zip(parts, outs))
    ]
    for copy in copies:
        copy.start()
    for copy in copies:
        copy.wait()
    load.wait()


def join_kernel(cols_a, *refs):
    parts = refs[:-4]
    rows_a, flipped = refs[-3:-1]
    ranks = parts[0].shape[0]
    for i, part in enumerate(parts):
        rows_a[pl.ds(i * ranks, ranks), :] = part[:, :cols_a]
    rows_b = jnp.concatenate([part[:, cols_a:].astype(F32) for part in parts], axis=0)
    flipped[...] = (rows_b * ADAPTER_SCALE).T.astype(BF16)


def merge_kernel(k, rows, *refs):
    panel, rows_a, flipped = refs[:3]
    out, tile, sems = refs[-3:]
    cols = rows_a.shape[1]
    base = (lax.axis_index("tensor") ^ k) * cols
    columns = pl.ds(pl.multiple_of(base, cols), cols)
    width = 512
    copies = []
    for step in range(panel.shape[0] // rows):
        here = slice(step * rows, (step + 1) * rows)
        for low in range(0, cols, width):
            span = slice(low, low + width)
            at = pl.ds(pl.multiple_of(base + low, width), width)
            increment = jnp.dot(flipped[here, :], rows_a[:, span], preferred_element_type=F32)
            tile[here, span] = (panel[here, at].astype(F32) + increment).astype(BF16)
        part = pl.ds(step * rows, rows)
        copy = pltpu.make_async_copy(tile.at[part, :], out.at[0, part, columns], sems.at[step])
        copy.start()
        copies.append(copy)
    for copy in copies:
        copy.wait()


def per_device(
    n_dp,
    n_expert,
    n_tensor,
    weight,
    factor_a,
    factor_b,
    moment_a,
    second_a,
    first_moment_factor_b,
    second_b,
    grad_a,
    grad_b,
    slot_of,
):
    ranks, cols_a = factor_a.shape[1:]
    cols_b = factor_b.shape[2]
    cols = cols_a + cols_b

    pieces = pl.pallas_call(
        functools.partial(pack_kernel, n_dp, ranks, cols_a),
        in_specs=[HBM, HBM],
        out_specs=[VMEM] * (n_dp - 1),
        out_shape=[pltpu.VMEM((ranks, cols), BF16)] * (n_dp - 1),
        scratch_shapes=[
            pltpu.VMEM((n_dp - 1, ranks, cols), F32),
            pltpu.SemaphoreType.DMA((n_dp - 1, 2)),
        ],
        compiler_params=PARAMS,
        name="pack",
    )(left(grad_a), left(grad_b))
    ks = [*range(2, n_dp), 1]
    got = [held(swap(pieces[k - 1], "dp", n_dp, k)) for k in ks]

    *state, order, stays = pl.pallas_call(
        functools.partial(load_kernel, ranks, cols_a),
        in_specs=[HBM] * 9,
        out_specs=[VMEM] * 4 + [SMEM] * 2,
        out_shape=[pltpu.VMEM((ranks, cols), F32)] * 4 + [pltpu.SMEM((1,), jnp.int32)] * 2,
        scratch_shapes=[pltpu.SMEM(slot_of.shape, jnp.int32), pltpu.SemaphoreType.DMA((9,))],
        compiler_params=PARAMS,
        cost_estimate=estimate(4 * ranks * cols * 4),
        name="load",
    )(
        *map(
            left,
            (
                slot_of,
                grad_a,
                grad_b,
                factor_a,
                factor_b,
                moment_a,
                first_moment_factor_b,
                second_a,
                second_b,
            ),
        ),
    )
    state = [held(x) for x in state]

    send = pl.pallas_call(
        send_kernel,
        in_specs=[VMEM] * (3 + n_dp),
        out_specs=VMEM,
        out_shape=pltpu.VMEM((ranks, cols), BF16),
        compiler_params=PARAMS,
        name="send",
    )(*state, *got)

    def move(slots):
        pairs = []
        for i, (expert, slot), j in itertools.product(
            range(n_dp), enumerate(slots), range(n_tensor)
        ):
            source = (i * n_expert + expert) * n_tensor + j
            partner = j if expert != slot else (j + 1) % n_tensor
            pairs.append((source, (i * n_expert + slot) * n_tensor + partner))
        moves = any(expert != slot for expert, slot in enumerate(slots))

        def branch(send):
            mine = lax.ppermute(send, ("dp", "expert", "tensor"), pairs) if moves else send
            return pl.pallas_call(
                keep_kernel,
                in_specs=[VMEM],
                out_specs=VMEM,
                out_shape=pltpu.VMEM((ranks, cols), BF16),
                compiler_params=PARAMS,
                name="keep",
            )(held(mine))

        return branch

    if n_expert <= MOST_SWITCHED:
        orders = itertools.permutations(range(n_expert))
        mine = lax.switch(order[0], [move(slots) for slots in orders], send)
        mine = jnp.where(stays[0] == 1, send, mine)
    else:
        mine = send
        here = lax.axis_index("expert")
        experts = jnp.arange(n_expert, dtype=jnp.int32)
        wanted = jnp.sum(jnp.where(slot_of == here, experts, 0)) ^ here
        for k in range(1, n_expert):
            mine = jnp.where(wanted == k, swap(send, "expert", n_expert, k), mine)

    parts = [mine] + [swap(mine, "dp", n_dp, k) for k in ks[::-1]]
    panel_shape = weight.shape[1:]
    shapes = [factor_a.shape, factor_b.shape] * 3
    *new, panel = pl.pallas_call(
        functools.partial(state_kernel, n_dp - 1, cols_a),
        in_specs=[HBM] + [VMEM] * (3 + n_dp),
        out_specs=[HBM] * 6 + [VMEM],
        out_shape=[jax.ShapeDtypeStruct(shape, F32) for shape in shapes]
        + [pltpu.VMEM(panel_shape, BF16)],
        scratch_shapes=[pltpu.VMEM(shape[1:], F32) for shape in shapes]
        + [pltpu.SemaphoreType.DMA((7,))],
        compiler_params=PARAMS,
        cost_estimate=estimate(weight.size * 4),
        name="state",
    )(left(weight), *state, *got)
    new_a, new_b, new_moment_a, new_moment_b, new_second_a, new_second_b = new
    rows_a, flipped, panel = pl.pallas_call(
        functools.partial(join_kernel, cols_a),
        in_specs=[VMEM] * (n_dp + 1),
        out_specs=[VMEM] * 3,
        out_shape=[
            pltpu.VMEM((ranks * n_dp, cols_a), BF16),
            pltpu.VMEM((cols_b, ranks * n_dp), BF16),
            pltpu.VMEM(panel_shape, BF16),
        ],
        input_output_aliases={n_dp: 2},
        compiler_params=PARAMS,
        name="join",
    )(*map(held, parts), held(panel))

    merged = None
    step_rows = 64
    for k in range(n_tensor):
        block = held(rows_a if k == 0 else swap(rows_a, "tensor", n_tensor, k))
        operands = [held(panel), block, held(flipped)] + ([] if merged is None else [merged])
        merged = pl.pallas_call(
            functools.partial(merge_kernel, k, step_rows),
            in_specs=[VMEM] * 3 + [HBM] * (len(operands) - 3),
            out_specs=HBM,
            out_shape=jax.ShapeDtypeStruct(weight.shape, BF16),
            scratch_shapes=[
                pltpu.VMEM((panel_shape[0], cols_a), BF16),
                pltpu.SemaphoreType.DMA((panel_shape[0] // step_rows,)),
            ],
            input_output_aliases={} if merged is None else {3: 0},
            compiler_params=PARAMS,
            cost_estimate=estimate(
                panel_shape[0] * cols_a * 2, 2 * panel_shape[0] * cols_a * ranks * n_dp
            ),
            name=f"merge{k}",
        )(*operands)
    return (merged, new_a, new_b, new_moment_a, new_second_a, new_moment_b, new_second_b)


def solution(mesh):
    sizes = dict(mesh.shape)

    def body(*args):
        return per_device(sizes["dp"], sizes["expert"], sizes["tensor"], *args)

    state = P("expert", "dp", "tensor")
    grad = P("dp", "expert", None, "tensor")
    weight = P("expert", "tensor", None)
    in_specs = (weight,) + (state,) * 6 + (grad,) * 2 + (P(),)
    out_specs = (weight,) + (state,) * 6
    return jax.shard_map(body, mesh=mesh, in_specs=in_specs, out_specs=out_specs, check_vma=False)
```
